128 devices in a mesh: seq: 8 (over x, z_hi), head: 16 (over y, z_lo, core).
Axes of the slice: x: 4, y: 4, z: 4 (z_hi: 2, z_lo: 2; z = z_hi * 2 + z_lo), core: 2. Of those that a mesh axis runs over, the one named last changes fastest.
Arguments:
- queries: bfloat16 [8192, 8192], P('seq', 'head'), may hold values from -8 to 8
- keys: bfloat16 [8192, 1024], P('seq'), may hold values from -8 to 8
- values: bfloat16 [8192, 1024], P('seq'), may hold values from -24 to 24
- w_out: bfloat16 [8192, 6144], P('head'), may hold values from -0.0625 to 0.0625
Outputs:
- mixed: bfloat16 [8192, 6144], P(('seq', 'head'))
The draws below stay inside these ranges and needn't reach their ends.
All inputs are finite; a program needn't handle non-finite values.
Results may differ from the reference program's by a relative error of at most 0.023.
Values may be sent and summed in bfloat16 or wider, within the bound.
No kernel may reach another device: no remote copies, remote signals or barrier semaphores. Data moves between devices by JAX's collectives and lax.ppermute only.
A program may use at most 128 MiB of HBM per device.

```python
import jax
import jax.numpy as jnp
from jax import lax

D = 6144
HQ = 64
KV_HEADS = 8
DH = 128
SEQ_LEN = 8192
N_HEAD = 16


def draw_queries(key, part):
    key = jax.random.fold_in(key, 11)
    first = jax.random.fold_in(key, 0)
    out = jnp.clip(1.5 * jax.random.normal(first, (SEQ_LEN, HQ * DH), jnp.float32), -8.0, 8.0)
    return out.astype(jnp.bfloat16)


def draw_keys(key, part):
    key = jax.random.fold_in(key, 23)
    first = jax.random.fold_in(key, 0)
    out = jnp.clip(jax.random.normal(first, (SEQ_LEN, KV_HEADS * DH), jnp.float32), -8.0, 8.0)
    return out.astype(jnp.bfloat16)


def levels(rng, extent, cuts, smallest, high):
    def one(position, blocks):
        steps = jax.random.uniform(jax.random.fold_in(jax.random.fold_in(rng, 6), position), (blocks,), jnp.float32, smallest / len(cuts), high / len(cuts))
        return jnp.repeat(jnp.exp(steps), extent[position] // blocks).reshape((-1,) + (1,) * (len(extent) - position - 1))

    level = one(*cuts[0])
    for cut in cuts[1:]:
        level = level * one(*cut)
    return level


def scatter_about(stream_key, shape, deviation, limit, cuts=(), held_as=jnp.bfloat16):
    result = jax.random.normal(stream_key, shape, jnp.float32) * deviation
    if len(cuts) > 0:
        result = levels(stream_key, shape, cuts, -0.22, 0.18) * result
    return jnp.clip(result, min=-limit, max=limit).astype(held_as)


def setup_inputs(seed: int = 0) -> dict:
    splits = jax.random.split(jax.random.key(seed), 5)
    return {
        "queries": draw_queries(jax.random.fold_in(splits[4], 71), 0),
        "keys": draw_keys(jax.random.fold_in(splits[4], 71), 0),
        "values": scatter_about(splits[2], (SEQ_LEN, KV_HEADS * DH), 4.0, 24.0, ((0, 8),)),
        "w_out": scatter_about(splits[3], (HQ * DH, D), (HQ * DH) ** -0.5, 0.0625, ((0, 16),)),
    }


NEG = -1e30


def reference(queries, keys, values, w_out):
    heads_dev = HQ // N_HEAD
    group_size = HQ // KV_HEADS
    scale = DH ** -0.5
    pos = jnp.arange(SEQ_LEN, dtype=jnp.int32)
    allowed = pos[None, :] <= pos[:, None]

    def one_head(head):
        slot = head // group_size
        query = lax.dynamic_slice_in_dim(queries, (head * DH).astype(jnp.int32), DH, 1)
        key = lax.dynamic_slice_in_dim(keys, (slot * DH).astype(jnp.int32), DH, 1)
        value = lax.dynamic_slice_in_dim(values, (slot * DH).astype(jnp.int32), DH, 1)
        scores = jnp.dot(query, key.T, preferred_element_type=jnp.float32) * scale
        scores = jnp.where(allowed, scores, jnp.float32(NEG))
        top = jnp.max(scores, axis=-1, keepdims=True)
        weights = jnp.where(allowed, jnp.exp(scores - top), jnp.float32(0.0))
        totals = jnp.sum(weights, axis=-1, keepdims=True)
        summed = jnp.dot(weights.astype(jnp.bfloat16), value, preferred_element_type=jnp.float32)
        return (summed / totals).astype(jnp.bfloat16)

    heads_out = lax.map(one_head, jnp.arange(HQ, dtype=jnp.int32))
    attention = jnp.transpose(heads_out, (1, 0, 2)).reshape(SEQ_LEN, HQ * DH)
    group_width = heads_dev * DH

    def add_group(total, group):
        start = (group * group_width).astype(jnp.int32)
        columns = lax.dynamic_slice_in_dim(attention, start, group_width, 1)
        rows_w = lax.dynamic_slice_in_dim(w_out, start, group_width, 0)
        partial_value = jnp.dot(columns, rows_w, preferred_element_type=jnp.float32).astype(jnp.bfloat16)
        partial_value = lax.optimization_barrier(partial_value)
        return total + partial_value.astype(jnp.float32), None

    total, _ = lax.scan(add_group, jnp.zeros((SEQ_LEN, D), jnp.float32), jnp.arange(N_HEAD, dtype=jnp.int32))
    return total.astype(jnp.bfloat16)
```

```python
import functools

import jax
import jax.numpy as jnp
from jax import lax
from jax.experimental import pallas as pl
from jax.experimental.pallas import tpu as pltpu
from jax.sharding import PartitionSpec as P

KV_HEADS = 8
DH = 128
LOG2E = 1.4426950408889634
NEG = -1e30
LIMIT = 60.0
CHUNKS = 4
BF = jnp.bfloat16
F32 = jnp.float32
VMEM_LIMIT = 56 << 20


def prep_kernel(info, k_ref, v_ref, ko_ref, vo_ref, mine_ref):
    k = k_ref[...]
    ko_ref[...] = k
    rows = k.shape[0]
    for t in range(rows // DH):
        vo_ref[t * DH : (t + 1) * DH, :] = v_ref[t * DH : (t + 1) * DH, :].T
    mine_ref[...] = jnp.where(info[2] == 0, k, vo_ref[...])


def prep(info, keys, values):
    rows = keys.shape[0]
    col = pl.BlockSpec((rows, DH), lambda i, info: (0, info[1]))
    whole = pl.BlockSpec((rows, DH), lambda i, info: (0, 0))
    shape = jax.ShapeDtypeStruct((rows, DH), BF)
    return pl.pallas_call(
        prep_kernel,
        grid_spec=pltpu.PrefetchScalarGridSpec(
            num_scalar_prefetch=1, grid=(1,), in_specs=[col, col], out_specs=[whole] * 3
        ),
        out_shape=[shape] * 3,
        name="prep",
        compiler_params=pltpu.CompilerParams(vmem_limit_bytes=VMEM_LIMIT),
    )(info, keys, values)


def attend_kernel(
    chunk, blocks, info, q_ref, k_ref, v_ref, mine_ref, other_ref, o_ref,
    q_buf, k_buf, v_buf, qt_ref, acc_ref, m_ref, mx_ref, o_buf, sems,
):
    place, core = info[0], info[2]
    rows = k_ref.shape[0]
    groups, _, sub, width = q_ref.shape
    heads = width // DH
    qb = groups * sub
    cols = heads * qb
    half = cols // 2
    q_copy = pltpu.make_async_copy(q_ref.at[:, chunk], q_buf, sems.at[0, blocks])
    k_copy = pltpu.make_async_copy(k_ref, k_buf.at[0], sems.at[0, 0])
    v_copy = pltpu.make_async_copy(v_ref, v_buf.at[0], sems.at[1, 0])
    q_copy.start()
    k_copy.start()
    v_copy.start()

    def start(d):
        @pl.when(jnp.logical_and(d <= place, core == 0))
        def _():
            pltpu.make_async_copy(mine_ref.at[d - 1], k_buf.at[d], sems.at[0, d]).start()
            pltpu.make_async_copy(other_ref.at[d - 1], v_buf.at[d], sems.at[1, d]).start()

        @pl.when(jnp.logical_and(d <= place, core != 0))
        def _():
            pltpu.make_async_copy(other_ref.at[d - 1], k_buf.at[d], sems.at[0, d]).start()
            pltpu.make_async_copy(mine_ref.at[d - 1], v_buf.at[d], sems.at[1, d]).start()

    for d in range(1, blocks):
        start(d)
    q_copy.wait()
    for h in range(heads):
        qh = q_buf[:, :, h * DH : (h + 1) * DH].reshape(qb, DH).astype(F32) * (DH**-0.5 * LOG2E)
        high = qh.astype(BF)
        low = (qh - high.astype(F32)).astype(BF)
        qt_ref[0:DH, h * qb : (h + 1) * qb] = high.T
        qt_ref[DH : 2 * DH, h * qb : (h + 1) * qb] = low.T
    k_copy.wait()
    v_copy.wait()

    def keys_of(d):
        k = k_buf[d]
        return jnp.concatenate([k, k], axis=1)

    def values_of(d):
        tiles = [v_buf[d, t * DH : (t + 1) * DH, :] for t in range(rows // DH)]
        return jnp.concatenate([jnp.concatenate(tiles, axis=1), jnp.ones((16, rows), BF)], axis=0)

    def scores(kk, c0):
        return jnp.dot(kk, qt_ref[:, c0 : c0 + half], preferred_element_type=F32)

    kk, vt = keys_of(0), values_of(0)
    col = lax.broadcasted_iota(jnp.int32, (rows, half), 1) % qb
    pos = (col // sub) * (rows // groups) + chunk * sub + col % sub
    allowed = lax.broadcasted_iota(jnp.int32, (rows, half), 0) <= pos
    for c0 in (0, half):
        s = jnp.where(allowed, scores(kk, c0), NEG)
        m = jnp.max(s, axis=0, keepdims=True)
        m_ref[:, c0 : c0 + half] = jnp.broadcast_to(m, (8, half))
        acc_ref[0, :, c0 : c0 + half] = jnp.dot(vt, jnp.exp2(s - m).astype(BF), preferred_element_type=F32)

    def body(d, _):
        pltpu.make_async_copy(k_ref, k_buf.at[d], sems.at[0, d]).wait()
        pltpu.make_async_copy(v_ref, v_buf.at[d], sems.at[1, d]).wait()
        old, new = (d + 1) % 2, d % 2
        kk, vt = keys_of(d), values_of(d)
        for c0 in (0, half):
            s = scores(kk, c0)
            mx_ref[:, c0 : c0 + half] = jnp.max(s.reshape(rows // 8, 8, half), axis=0)
            p = jnp.exp2(s - m_ref[0:1, c0 : c0 + half]).astype(BF)
            acc_ref[new, :, c0 : c0 + half] = acc_ref[old, :, c0 : c0 + half] + jnp.dot(
                vt, p, preferred_element_type=F32
            )
        over = jnp.max(mx_ref[...] - m_ref[...])

        @pl.when(over > LIMIT)
        def _():
            for c0 in (0, half):
                m = m_ref[0:1, c0 : c0 + half]
                top = jnp.maximum(m, jnp.max(mx_ref[:, c0 : c0 + half], axis=0, keepdims=True))
                p = jnp.exp2(scores(kk, c0) - top).astype(BF)
                acc_ref[new, :, c0 : c0 + half] = acc_ref[old, :, c0 : c0 + half] * jnp.exp2(
                    m - top
                ) + jnp.dot(vt, p, preferred_element_type=F32)
                m_ref[:, c0 : c0 + half] = jnp.broadcast_to(top, (8, half))

        return 0

    lax.fori_loop(1, place + 1, body, 0)
    last = place % 2
    for h in range(heads):
        o = acc_ref[last, :, h * qb : (h + 1) * qb]
        o = (o[0:DH] / o[DH : DH + 1]).T.astype(BF)
        o_buf[:, h * DH : (h + 1) * DH] = o
    for a in range(groups // 4):
        for b in range(4):
            src = (a * 4 + b) * sub
            ra = (a + groups // 4 - info[3]) % (groups // 4)
            rb = b ^ info[4]
            dst = pl.multiple_of((ra * 4 + rb) * sub, sub)
            o_ref[pl.ds(dst, sub), :] = o_buf[src : src + sub, :]


def attend(info, q4, k, v, mine, other, chunk):
    rows = k.shape[0]
    blocks = mine.shape[0] + 1
    groups, _, sub, width = q4.shape
    qb = groups * sub
    cols = width // DH * qb
    any_space = pl.BlockSpec(memory_space=pl.ANY)
    return pl.pallas_call(
        functools.partial(attend_kernel, chunk, blocks),
        grid_spec=pltpu.PrefetchScalarGridSpec(
            num_scalar_prefetch=1,
            grid=(1,),
            in_specs=[any_space] * 5,
            out_specs=pl.BlockSpec((qb, width), lambda i, info: (0, 0)),
            scratch_shapes=[
                pltpu.VMEM((groups, sub, width), BF),
                pltpu.VMEM((blocks, rows, DH), BF),
                pltpu.VMEM((blocks, rows, DH), BF),
                pltpu.VMEM((2 * DH, cols), BF),
                pltpu.VMEM((2, DH + 16, cols), F32),
                pltpu.VMEM((8, cols), F32),
                pltpu.VMEM((8, cols), F32),
                pltpu.VMEM((qb, width), BF),
                pltpu.SemaphoreType.DMA((2, blocks + 1)),
            ],
        ),
        out_shape=jax.ShapeDtypeStruct((qb, width), BF),
        name="attend",
        cost_estimate=pl.CostEstimate(
            flops=4 * cols * rows * blocks * 2 * DH // 2, bytes_accessed=8 << 20, transcendentals=cols * rows * blocks // 2
        ),
        compiler_params=pltpu.CompilerParams(vmem_limit_bytes=VMEM_LIMIT),
    )(info, q4, k, v, mine, other)


def project_kernel(a_ref, b_ref, wa_ref, wb_ref, *outs):
    s = jnp.dot(a_ref[...], wa_ref[...], preferred_element_type=F32) + jnp.dot(
        b_ref[...], wb_ref[...], preferred_element_type=F32
    )
    n = s.shape[0] // len(outs)
    for i, o in enumerate(outs):
        o[...] = s[i * n : (i + 1) * n].astype(BF)


def project(info, mine, other, w, w_other, parts, tile=512):
    rows, width = mine.shape
    n = w_other.shape[1]

    def body(info, a, b, wa, wb, *outs):
        project_kernel(a, b, wa, wb, *outs)

    steps = n // tile
    whole = pl.BlockSpec((rows, width), lambda i, info: (0, 0))
    return pl.pallas_call(
        body,
        grid_spec=pltpu.PrefetchScalarGridSpec(
            num_scalar_prefetch=1,
            grid=(steps,),
            in_specs=[
                whole,
                whole,
                pl.BlockSpec((width, tile), lambda i, info: (0, info[2] * steps + i)),
                pl.BlockSpec((width, tile), lambda i, info: (0, i)),
            ],
            out_specs=[pl.BlockSpec((rows // parts, tile), lambda i, info: (0, i))] * parts,
        ),
        out_shape=[jax.ShapeDtypeStruct((rows // parts, n), BF)] * parts,
        name="project",
        cost_estimate=pl.CostEstimate(
            flops=4 * rows * width * n, bytes_accessed=4 * width * n + 4 * rows * n, transcendentals=0
        ),
        compiler_params=pltpu.CompilerParams(vmem_limit_bytes=VMEM_LIMIT),
    )(info, mine, other, w, w_other)


def local(queries, keys, values, w_out):
    n_seq, n_head = lax.axis_size("seq"), lax.axis_size("head")
    rows, width = queries.shape
    cols = w_out.shape[1]
    place = lax.axis_index("seq")
    head = lax.axis_index("head")
    core, y, z = head % 2, head // 4, head // 2 % 2
    n_y = n_head // 4
    info = jnp.stack([place, head * KV_HEADS // n_head, core, y, head % 4, z]).astype(jnp.int32)

    def to(f):
        return [(h, f(h // 4, h // 2 % 2, h % 2)) for h in range(n_head)]

    def at(y, z, c):
        return (y % n_y) * 4 + z * 2 + c

    swap_core = to(lambda y, z, c: at(y, z, 1 - c))
    swap_z = to(lambda y, z, c: at(y, 1 - z, c))
    by_y = {d: to(lambda y, z, c, d=d: at(y + d, z, c)) for d in range(1, n_y)}

    k, v, mine = prep(info, keys, values)
    sent = [
        lax.ppermute(mine, "seq", [(s, s + d) for s in range(n_seq - d)]) for d in range(1, n_seq)
    ]
    mine = jnp.stack(sent)
    other = lax.ppermute(mine, "head", swap_core)
    w_away = lax.dynamic_slice_in_dim(w_out, (1 - core) * (cols // 2), cols // 2, 1)
    w_other = lax.ppermute(w_away, "head", swap_core)

    sub = rows // n_head // CHUNKS
    q4 = queries.reshape(n_head, CHUNKS, sub, width)
    pieces = []
    for chunk in range(CHUNKS):
        out = attend(info, q4, k, v, mine, other, chunk)
        out_other = lax.ppermute(out, "head", swap_core)
        fixed = out_other.reshape(n_head // 2, 2, sub, width)[:, ::-1].reshape(out.shape)
        parts = project(info, out, fixed, w_out, w_other, n_y)
        got = [lax.ppermute(parts[d], "head", by_y[d]) for d in range(1, n_y)]
        total = parts[0].astype(F32)
        for g in got:
            total = total + g.astype(F32)
        total = total.reshape(2, 2 * sub, cols // 2)
        far = lax.ppermute(total[1].astype(BF), "head", swap_z)
        total = (total[0] + far.astype(F32)).astype(BF).reshape(2, sub, cols // 2)
        pieces.append(total)
    done = jnp.concatenate([p[0] for p in pieces], axis=0)
    away = jnp.concatenate([p[1] for p in pieces], axis=0)
    back = lax.ppermute(away, "head", swap_core)
    left = jnp.where(core == 0, done, back)
    right = jnp.where(core == 0, back, done)
    return jnp.concatenate([left, right], axis=1)


def solution(mesh):
    placed = (P("seq", "head"), P("seq", None), P("seq", None), P("head", None))
    return jax.shard_map(
        local, mesh=mesh, in_specs=placed, out_specs=P(("seq", "head"), None), check_vma=False
    )
```

```python
import functools

import jax
import jax.numpy as jnp
from jax import lax
from jax.experimental import pallas as pl
from jax.experimental.pallas import tpu as pltpu
from jax.sharding import PartitionSpec as P

KV_HEADS = 8
DH = 128
LOG2E = 1.4426950408889634
NEG = -1e30
LIMIT = 60.0
CHUNKS = 4
BF = jnp.bfloat16
F32 = jnp.float32
VMEM_LIMIT = 56 << 20
PARAMS = pltpu.CompilerParams(vmem_limit_bytes=VMEM_LIMIT)


def after(x, *deps):
    return lax.optimization_barrier((x, *deps))[0]


def prep_kernel(info, k_ref, v_ref, kv_ref):
    rows = k_ref.shape[0]
    kv_ref[0:rows, :] = k_ref[...]
    for t in range(rows // DH):
        kv_ref[rows + t * DH : rows + (t + 1) * DH, :] = v_ref[t * DH : (t + 1) * DH, :].T


def prep(info, keys, values):
    rows = keys.shape[0]
    col = pl.BlockSpec((rows, DH), lambda i, info: (0, info[1]))
    return pl.pallas_call(
        prep_kernel,
        grid_spec=pltpu.PrefetchScalarGridSpec(
            num_scalar_prefetch=1,
            grid=(1,),
            in_specs=[col, col],
            out_specs=pl.BlockSpec((2 * rows, DH), lambda i, info: (0, 0)),
        ),
        out_shape=jax.ShapeDtypeStruct((2 * rows, DH), BF),
        name="prep",
        compiler_params=PARAMS,
    )(info, keys, values)


def keys_of(kv):
    k = kv[0 : kv.shape[0] // 2, :]
    return jnp.concatenate([k, k], axis=1)


def values_of(kv):
    rows = kv.shape[0] // 2
    tiles = [kv[rows + t * DH : rows + (t + 1) * DH, :] for t in range(rows // DH)]
    return jnp.concatenate([jnp.concatenate(tiles, axis=1), jnp.ones((16, rows), BF)], axis=0)


def diagonal_kernel(groups, q_ref, kv_ref, qt_ref, acc_ref, m_ref):
    chunk = pl.program_id(0)
    _, _, sub, width = q_ref.shape
    rows = kv_ref.shape[0] // 2
    heads, qb = width // DH, groups * sub
    half = heads * qb // 2
    for h in range(heads):
        qh = q_ref[:, 0, :, h * DH : (h + 1) * DH].reshape(qb, DH).astype(F32) * (DH**-0.5 * LOG2E)
        high = qh.astype(BF)
        low = (qh - high.astype(F32)).astype(BF)
        qt_ref[0, 0:DH, h * qb : (h + 1) * qb] = high.T
        qt_ref[0, DH : 2 * DH, h * qb : (h + 1) * qb] = low.T
    kk, vt = keys_of(kv_ref[...]), values_of(kv_ref[...])
    col = lax.broadcasted_iota(jnp.int32, (rows, half), 1) % qb
    pos = (col // sub) * (rows // groups) + chunk * sub + col % sub
    allowed = lax.broadcasted_iota(jnp.int32, (rows, half), 0) <= pos
    for c0 in (0, half):
        s = jnp.dot(kk, qt_ref[0, :, c0 : c0 + half], preferred_element_type=F32)
        s = jnp.where(allowed, s, NEG)
        m = jnp.max(s, axis=0, keepdims=True)
        m_ref[0, :, c0 : c0 + half] = jnp.broadcast_to(m, (8, half))
        acc_ref[0, :, c0 : c0 + half] = jnp.dot(vt, jnp.exp2(s - m).astype(BF), preferred_element_type=F32)


def diagonal(q4, kv):
    groups, chunks, sub, width = q4.shape
    cols = groups * sub * width // DH
    one = lambda i: (i, 0, 0)
    return pl.pallas_call(
        functools.partial(diagonal_kernel, groups),
        grid=(chunks,),
        in_specs=[
            pl.BlockSpec((groups, 1, sub, width), lambda i: (0, i, 0, 0)),
            pl.BlockSpec(kv.shape, lambda i: (0, 0)),
        ],
        out_specs=[
            pl.BlockSpec((1, 2 * DH, cols), one),
            pl.BlockSpec((1, DH + 16, cols), one),
            pl.BlockSpec((1, 8, cols), one),
        ],
        out_shape=[
            jax.ShapeDtypeStruct((chunks, 2 * DH, cols), BF),
            jax.ShapeDtypeStruct((chunks, DH + 16, cols), F32),
            jax.ShapeDtypeStruct((chunks, 8, cols), F32),
        ],
        name="diagonal",
        cost_estimate=pl.CostEstimate(
            flops=chunks * cols * kv.shape[0] * 2 * DH, bytes_accessed=8 << 20, transcendentals=0
        ),
        compiler_params=PARAMS,
    )(q4, kv)


def attend_kernel(first, count, chunk, final, groups, n_y, info, *refs):
    ops = (count + 1) // 2
    qt_hbm, acc_hbm, m_hbm = refs[:3]
    mine, other = refs[3 : 3 + ops], refs[3 + ops : 3 + 2 * ops]
    refs = refs[3 + 2 * ops :]
    outs, (kv_buf, qt_ref, acc_ref, m_ref, mx_ref, sems) = refs[:-6], refs[-6:]
    place, core = info[0], info[2]
    rows = kv_buf.shape[1] // 2
    cols = qt_ref.shape[1]
    half = cols // 2
    todo = jnp.clip(place - first, 0, count)
    loads = [
        pltpu.make_async_copy(qt_hbm, qt_ref, sems.at[count]),
        pltpu.make_async_copy(acc_hbm, acc_ref.at[0], sems.at[count + 1]),
        pltpu.make_async_copy(m_hbm, m_ref, sems.at[count + 2]),
    ]
    for load in loads:
        load.start()
    for i in range(count):
        @pl.when(jnp.logical_and(i < todo, core == i % 2))
        def _():
            pltpu.make_async_copy(mine[i // 2], kv_buf.at[i], sems.at[i]).start()

        @pl.when(jnp.logical_and(i < todo, core != i % 2))
        def _():
            pltpu.make_async_copy(other[i // 2], kv_buf.at[i], sems.at[i]).start()

    for load in loads:
        load.wait()

    def scores(kk, c0):
        return jnp.dot(kk, qt_ref[:, c0 : c0 + half], preferred_element_type=F32)

    def body(i, _):
        pltpu.make_async_copy(mine[0], kv_buf.at[i], sems.at[i]).wait()
        old, new = i % 2, (i + 1) % 2
        kk, vt = keys_of(kv_buf.at[i]), values_of(kv_buf.at[i])
        for c0 in (0, half):
            s = scores(kk, c0)
            mx_ref[:, c0 : c0 + half] = jnp.max(s.reshape(rows // 8, 8, half), axis=0)
            p = jnp.exp2(s - m_ref[0:1, c0 : c0 + half]).astype(BF)
            acc_ref[new, :, c0 : c0 + half] = acc_ref[old, :, c0 : c0 + half] + jnp.dot(
                vt, p, preferred_element_type=F32
            )
        over = jnp.max(mx_ref[...] - m_ref[...])

        @pl.when(over > LIMIT)
        def _():
            for c0 in (0, half):
                m = m_ref[0:1, c0 : c0 + half]
                top = jnp.maximum(m, jnp.max(mx_ref[:, c0 : c0 + half], axis=0, keepdims=True))
                p = jnp.exp2(scores(kk, c0) - top).astype(BF)
                acc_ref[new, :, c0 : c0 + half] = acc_ref[old, :, c0 : c0 + half] * jnp.exp2(
                    m - top
                ) + jnp.dot(vt, p, preferred_element_type=F32)
                m_ref[:, c0 : c0 + half] = jnp.broadcast_to(top, (8, half))

        return 0

    lax.fori_loop(0, todo, body, 0)
    last = todo % 2
    if not final:
        outs[0][0] = acc_ref[last]
        outs[1][0] = m_ref[...]
        return
    (o_ref,) = outs
    qb = o_ref.shape[0]
    sub = qb // groups
    for h in range(o_ref.shape[1] // DH):
        o = acc_ref[last, :, h * qb : (h + 1) * qb]
        o = (o[0:DH] / o[DH : DH + 1]).T.astype(BF)
        for g in range(groups):
            ry = (g // 4 + n_y - info[3]) % n_y
            rz = (g // 2 % 2) ^ info[4]
            dst = (ry * 2 + rz) if chunk % 2 == 0 else (rz * n_y + ry)
            dst = pl.multiple_of((dst * 2 + g % 2) * sub, sub)
            o_ref[pl.ds(dst, sub), h * DH : (h + 1) * DH] = o[g * sub : (g + 1) * sub, :]


def attend(info, qt, acc, m, mine, other, first, count, chunk, slot, final, groups, n_y, width):
    cols = qt.shape[2]
    qb = cols // (width // DH)
    rows2 = mine[0].shape[0]
    any_space = pl.BlockSpec(memory_space=pl.ANY)
    if final:
        out_specs = pl.BlockSpec((qb, width), lambda i, info: (0, 0))
        out_shape = jax.ShapeDtypeStruct((qb, width), BF)
    else:
        out_specs = [
            pl.BlockSpec((1, DH + 16, cols), lambda i, info: (0, 0, 0)),
            pl.BlockSpec((1, 8, cols), lambda i, info: (0, 0, 0)),
        ]
        out_shape = [
            jax.ShapeDtypeStruct((1, DH + 16, cols), F32),
            jax.ShapeDtypeStruct((1, 8, cols), F32),
        ]

    def body(info, qt_ref, acc_ref, m_ref, *refs):
        attend_kernel(
            first, count, chunk, final, groups, n_y, info,
            qt_ref.at[chunk], acc_ref.at[slot], m_ref.at[slot], *refs,
        )

    return pl.pallas_call(
        body,
        grid_spec=pltpu.PrefetchScalarGridSpec(
            num_scalar_prefetch=1,
            grid=(1,),
            in_specs=[any_space] * (3 + 2 * len(mine)),
            out_specs=out_specs,
            scratch_shapes=[
                pltpu.VMEM((count, rows2, DH), BF),
                pltpu.VMEM((2 * DH, cols), BF),
                pltpu.VMEM((2, DH + 16, cols), F32),
                pltpu.VMEM((8, cols), F32),
                pltpu.VMEM((8, cols), F32),
                pltpu.SemaphoreType.DMA((count + 3,)),
            ],
        ),
        out_shape=out_shape,
        name="attend",
        cost_estimate=pl.CostEstimate(
            flops=4 * cols * rows2 * count * DH, bytes_accessed=4 << 20, transcendentals=0
        ),
        compiler_params=PARAMS,
    )(info, qt, acc, m, *mine, *other)


def project(info, mine, other, w, w_other, parts, tile):
    rows, width = mine.shape
    n = w.shape[1] // 2
    steps = n // tile

    def body(info, a, b, wa, wb, *outs):
        s = jnp.dot(a[...], wa[...], preferred_element_type=F32) + jnp.dot(
            b[...], wb[...], preferred_element_type=F32
        )
        part = s.shape[0] // len(outs)
        for i, o in enumerate(outs):
            o[...] = s[i * part : (i + 1) * part].astype(BF)

    whole = pl.BlockSpec((rows, width), lambda i, info: (0, 0))
    weights = pl.BlockSpec((width, tile), lambda i, info: (0, info[2] * steps + i))
    return pl.pallas_call(
        body,
        grid_spec=pltpu.PrefetchScalarGridSpec(
            num_scalar_prefetch=1,
            grid=(steps,),
            in_specs=[whole, whole, weights, weights],
            out_specs=[pl.BlockSpec((rows // parts, tile), lambda i, info: (0, i))] * parts,
        ),
        out_shape=[jax.ShapeDtypeStruct((rows // parts, n), BF)] * parts,
        name="project",
        cost_estimate=pl.CostEstimate(
            flops=4 * rows * width * n, bytes_accessed=4 * width * n + 4 * rows * n, transcendentals=0
        ),
        compiler_params=PARAMS,
    )(info, mine, other, w, w_other)


def add(*terms):
    total = terms[0].astype(F32)
    for t in terms[1:]:
        total = total + t.astype(F32)
    return total.astype(BF)


def local(queries, keys, values, w_out):
    n_seq, n_head = lax.axis_size("seq"), lax.axis_size("head")
    rows, width = queries.shape
    cols = w_out.shape[1]
    place = lax.axis_index("seq")
    head = lax.axis_index("head")
    core, y, z = head % 2, head // 4, head // 2 % 2
    n_y = n_head // 4
    info = jnp.stack([place, head * KV_HEADS // n_head, core, y, z]).astype(jnp.int32)

    def to(f):
        return [(h, f(h // 4, h // 2 % 2, h % 2)) for h in range(n_head)]

    def at(y, z, c):
        return (y % n_y) * 4 + z * 2 + c

    swap_core = to(lambda y, z, c: at(y, z, 1 - c))
    swap_z = to(lambda y, z, c: at(y, 1 - z, c))
    by_y = {d: to(lambda y, z, c, d=d: at(y + d, z, c)) for d in range(1, n_y)}

    def over_head(x, pairs):
        return lax.ppermute(x, "head", pairs)

    kv = prep(info, keys, values)
    mine = []
    for op in range(n_seq // 2):
        pairs = []
        for s in range(n_seq):
            for h in range(n_head):
                d = 2 * op + 1 + h % 2
                if s + d < n_seq:
                    pairs.append((s * n_head + h, (s + d) * n_head + h))
        mine.append(lax.ppermute(kv, ("seq", "head"), pairs))
    sub = rows // n_head // CHUNKS
    q4 = queries.reshape(n_head, CHUNKS, sub, width)
    qt, acc, m = diagonal(q4, kv)
    near = n_seq // 4
    other = [over_head(x, swap_core) for x in mine[:near]]
    w_other = over_head(after(w_out, m), swap_core)

    def run(acc, m, slot, ops, chunk, final, *deps):
        first = 2 * ops[0]
        count = min(2 * len(ops), n_seq - 1 - first)
        return attend(
            after(info, *deps), qt, acc, m, [mine[i] for i in ops], [other[i] for i in ops],
            first, count, chunk, slot, final, n_head, n_y, width,
        )

    ops = list(range(n_seq // 2))
    acc0, m0 = run(acc, m, 0, ops[:near], 0, False)
    other += [over_head(after(x, m0), swap_core) for x in mine[near:]]
    acc1, m1 = run(acc, m, 1, ops[:near], 1, False, acc0)
    out = [None] * CHUNKS
    out[0] = run(acc0, m0, 0, ops[near:], 0, True, acc1)
    far = [None] * CHUNKS
    far[0] = over_head(out[0], swap_core)
    out[1] = run(acc1, m1, 0, ops[near:], 1, True, out[0])
    far[1] = over_head(out[1], swap_core)

    def projected(i, *deps):
        return project(after(info, *deps), out[i], far[i], w_out, w_other, n_y if i % 2 == 0 else 2, cols // 4)

    def first_stage(i, parts):
        if i % 2 == 0:
            return [over_head(parts[d], by_y[d]) for d in range(1, n_y)]
        return [over_head(parts[1], swap_z)]

    def second_stage(i, total):
        if i % 2 == 0:
            return total[: 2 * sub], [over_head(total[2 * sub :], swap_z)]
        got = [over_head(total[d * 2 * sub : (d + 1) * 2 * sub], by_y[d]) for d in range(1, n_y)]
        return total[: 2 * sub], got

    parts0 = projected(0, out[1])
    got0 = first_stage(0, parts0)
    out[2] = run(acc, m, 2, ops, 2, True, parts0[0])
    far[2] = over_head(out[2], swap_core)
    parts1 = projected(1, out[2])
    got1 = first_stage(1, parts1)
    sum0 = add(parts0[0], *got0)
    keep0, back0 = second_stage(0, sum0)
    out[3] = run(acc, m, 3, ops, 3, True, parts1[0], sum0)
    far[3] = over_head(out[3], swap_core)
    parts2 = projected(2, out[3])
    got2 = first_stage(2, parts2)
    sum1 = add(after(parts1[0], parts2[0]), *got1)
    keep1, back1 = second_stage(1, sum1)
    parts3 = projected(3, parts2[0], sum1)
    got3 = first_stage(3, parts3)
    sum2 = add(after(parts2[0], parts3[0]), *got2)
    keep2, back2 = second_stage(2, sum2)
    sum3 = add(parts3[0], *got3)
    keep3, back3 = second_stage(3, sum3)
    pieces = [
        add(k, *b).reshape(2, sub, cols // 2)
        for k, b in ((keep0, back0), (keep1, back1), (keep2, back2), (keep3, back3))
    ]
    done = jnp.concatenate([jnp.where(core == 0, p[0], p[1]) for p in pieces], axis=0)
    away = jnp.concatenate([jnp.where(core == 0, p[1], p[0]) for p in pieces], axis=0)
    back = over_head(away, swap_core)
    left = jnp.where(core == 0, done, back)
    right = jnp.where(core == 0, back, done)
    return jnp.concatenate([left, right], axis=1)


def solution(mesh):
    placed = (P("seq", "head"), P("seq", None), P("seq", None), P("head", None))
    return jax.shard_map(
        local, mesh=mesh, in_specs=placed, out_specs=P(("seq", "head"), None), check_vma=False
    )
```

```python
import functools

import jax
import jax.numpy as jnp
from jax import lax
from jax.experimental import pallas as pl
from jax.experimental.pallas import tpu as pltpu
from jax.sharding import PartitionSpec as P

KV_HEADS = 8
DH = 128
LOG2E = 1.4426950408889634
NEG = -1e30
LIMIT = 60.0
BF = jnp.bfloat16
F32 = jnp.float32
PARAMS = pltpu.CompilerParams(vmem_limit_bytes=56 << 20)
FETCH = ((7, 3), (6, 2), (5, 1), (4, None))
SLOTS = [d for pair in FETCH for d in pair if d is not None]
TABLE = 6


def after(x, *deps):
    return lax.optimization_barrier((x, *deps))[0]


def prep_kernel(info, k_ref, v_ref, kv_ref):
    rows = k_ref.shape[0]
    kv_ref[0:rows, :] = k_ref[...]
    for t in range(rows // DH):
        kv_ref[rows + t * DH : rows + (t + 1) * DH, :] = v_ref[t * DH : (t + 1) * DH, :].T


def prep(info, keys, values):
    rows = keys.shape[0]
    col = pl.BlockSpec((rows, DH), lambda i, info: (0, info[1]))
    return pl.pallas_call(
        prep_kernel,
        grid_spec=pltpu.PrefetchScalarGridSpec(
            num_scalar_prefetch=1,
            grid=(1,),
            in_specs=[col, col],
            out_specs=pl.BlockSpec((2 * rows, DH), lambda i, info: (0, 0)),
        ),
        out_shape=jax.ShapeDtypeStruct((2 * rows, DH), BF),
        name="prep",
        compiler_params=PARAMS,
    )(info, keys, values)


def keys_of(kv):
    k = kv[0 : kv.shape[0] // 2, :]
    return jnp.concatenate([k, k], axis=1)


def values_of(kv):
    rows = kv.shape[0] // 2
    tiles = [kv[rows + t * DH : rows + (t + 1) * DH, :] for t in range(rows // DH)]
    return jnp.concatenate([jnp.concatenate(tiles, axis=1), jnp.ones((16, rows), BF)], axis=0)


def load_queries(q, h, qt_ref):
    qb = q.shape[0]
    scaled = q.astype(F32) * (DH**-0.5 * LOG2E)
    high = scaled.astype(BF)
    low = (scaled - high.astype(F32)).astype(BF)
    qt_ref[0:DH, h * qb : (h + 1) * qb] = high.T
    qt_ref[DH : 2 * DH, h * qb : (h + 1) * qb] = low.T


def exact_block(kv, behind, second, groups, qt_ref, acc, m_ref):
    rows = kv.shape[0] // 2
    heads = KV_HEADS // 2
    qb = qt_ref.shape[1] // heads
    sub = qb // groups
    kk, vt = keys_of(kv), values_of(kv)
    j = lax.broadcasted_iota(jnp.int32, (rows, qb), 1)
    pos = behind * rows + j // sub * (rows // groups) + second * sub + j % sub
    allowed = lax.broadcasted_iota(jnp.int32, (rows, qb), 0) <= pos
    for h in range(heads):
        c = slice(h * qb, (h + 1) * qb)
        s = jnp.where(allowed, jnp.dot(kk, qt_ref[:, c], preferred_element_type=F32), NEG)
        m = m_ref[0:1, c]
        top = jnp.maximum(m, jnp.max(s, axis=0, keepdims=True))
        acc[:, c] = acc[:, c] * jnp.exp2(m - top) + jnp.dot(
            vt, jnp.exp2(s - top).astype(BF), preferred_element_type=F32
        )
        m_ref[:, c] = jnp.broadcast_to(top, (8, qb))


def own_kernel(groups, q_ref, kv_ref, qt_ref, acc_ref, m_ref):
    _, _, sub, width = q_ref.shape
    for h in range(width // DH):
        load_queries(q_ref[:, 0, :, h * DH : (h + 1) * DH].reshape(groups * sub, DH), h, qt_ref)
    acc_ref[...] = jnp.zeros_like(acc_ref)
    m_ref[...] = jnp.full_like(m_ref, NEG)
    exact_block(kv_ref, 0, 0, groups, qt_ref, acc_ref, m_ref)


def own(q4, kv):
    groups, _, sub, width = q4.shape
    cols = groups * sub * width // DH
    return pl.pallas_call(
        functools.partial(own_kernel, groups),
        grid=(1,),
        in_specs=[
            pl.BlockSpec((groups, 1, sub, width), lambda i: (0, 0, 0, 0)),
            pl.BlockSpec(kv.shape, lambda i: (0, 0)),
        ],
        out_specs=[
            pl.BlockSpec((2 * DH, cols), lambda i: (0, 0)),
            pl.BlockSpec((DH + 16, cols), lambda i: (0, 0)),
            pl.BlockSpec((8, cols), lambda i: (0, 0)),
        ],
        out_shape=[
            jax.ShapeDtypeStruct((2 * DH, cols), BF),
            jax.ShapeDtypeStruct((DH + 16, cols), F32),
            jax.ShapeDtypeStruct((8, cols), F32),
        ],
        name="own",
        cost_estimate=pl.CostEstimate(
            flops=2 * cols * kv.shape[0] * 2 * DH, bytes_accessed=8 << 20, transcendentals=0
        ),
        compiler_params=PARAMS,
    )(q4, kv)


def attend_kernel(late, groups, n_y, n_seq, info, q_ref, own_ref, qt_hbm, acc_hbm, m_hbm, *refs):
    ops = n_seq // 2
    mine, other = refs[:ops], refs[ops : 2 * ops]
    o_ref, peer_ref, q_buf, kv_buf, qt_ref, acc_ref, m_ref, mx_ref, count, sems = refs[2 * ops :]
    place, core, partner = info[0], info[2], info[5]
    rows = own_ref.shape[0] // 2
    cols = qt_ref.shape[1]
    heads = KV_HEADS // 2
    qb = cols // heads
    sub = qb // groups
    half = cols // 4
    light = place < partner
    limit = jnp.maximum(place, partner) if late else jnp.minimum(place, partner)
    fresh = limit != place
    n = len(SLOTS)

    def behind(i):
        return limit - place if i is None else limit - lax.bitwise_xor(place, info[TABLE + i])

    def start(src, slot, sem):
        pltpu.make_async_copy(src, kv_buf.at[slot], sems.at[sem]).start()

    def wait(slot):
        pltpu.make_async_copy(own_ref, kv_buf.at[slot], sems.at[slot]).wait()

    need_own = jnp.logical_and(fresh, place < limit)

    @pl.when(fresh)
    def _():
        pltpu.make_async_copy(q_ref, q_buf, sems.at[n + 1]).start()

    @pl.when(jnp.logical_not(fresh))
    def _():
        pltpu.make_async_copy(qt_hbm, qt_ref, sems.at[n + 1]).start()
        pltpu.make_async_copy(acc_hbm, acc_ref.at[0], sems.at[n + 2]).start()
        pltpu.make_async_copy(m_hbm, m_ref, sems.at[n + 3]).start()

    @pl.when(need_own)
    def _():
        start(own_ref, 0, 0)

    for i in range(n):

        @pl.when(jnp.logical_and(behind(i) >= 0, core == i % 2))
        def _():
            start(mine[i // 2], i + 1, i + 1)

        @pl.when(jnp.logical_and(behind(i) >= 0, core != i % 2))
        def _():
            start(other[i // 2], i + 1, i + 1)

    @pl.when(fresh)
    def _():
        pltpu.make_async_copy(q_ref, q_buf, sems.at[n + 1]).wait()
        for h in range(heads):
            load_queries(q_buf[:, :, h * DH : (h + 1) * DH].reshape(qb, DH), h, qt_ref)
        acc_ref[0] = jnp.zeros(acc_ref.shape[1:], F32)
        m_ref[...] = jnp.full_like(m_ref, NEG)

    @pl.when(jnp.logical_not(fresh))
    def _():
        pltpu.make_async_copy(qt_hbm, qt_ref, sems.at[n + 1]).wait()
        pltpu.make_async_copy(acc_hbm, acc_ref.at[0], sems.at[n + 2]).wait()
        pltpu.make_async_copy(m_hbm, m_ref, sems.at[n + 3]).wait()

    count[0] = 0

    def exact(slot, _):
        back = limit - jnp.where(slot == 0, place, partner)

        @pl.when(jnp.logical_and(fresh, back >= 0))
        def _():
            wait(slot)
            exact_block(kv_buf.at[slot], back, 1, groups, qt_ref, acc_ref.at[0], m_ref)

        return 0

    lax.fori_loop(0, 2, exact, 0)

    def scores(kk, c0):
        return jnp.dot(kk, qt_ref[:, c0 : c0 + half], preferred_element_type=F32)

    def add_block(i, _):
        taken = jnp.logical_and(fresh, i == 0)

        @pl.when(jnp.logical_and(behind(i) > 0, jnp.logical_not(taken)))
        def _():
            slot = i + 1
            wait(slot)
            old = count[0] % 2
            new = 1 - old
            count[0] = count[0] + 1
            kk, vt = keys_of(kv_buf.at[slot]), values_of(kv_buf.at[slot])
            for c0 in range(0, cols, half):
                s = scores(kk, c0)
                mx_ref[:, c0 : c0 + half] = jnp.max(s.reshape(rows // 8, 8, half), axis=0)
                p = jnp.exp2(s - m_ref[0:1, c0 : c0 + half]).astype(BF)
                acc_ref[new, :, c0 : c0 + half] = acc_ref[old, :, c0 : c0 + half] + jnp.dot(
                    vt, p, preferred_element_type=F32
                )
            over = jnp.max(mx_ref[...] - m_ref[...])

            @pl.when(over > LIMIT)
            def _():
                for c0 in range(0, cols, half):
                    m = m_ref[0:1, c0 : c0 + half]
                    top = jnp.maximum(m, jnp.max(mx_ref[:, c0 : c0 + half], axis=0, keepdims=True))
                    p = jnp.exp2(scores(kk, c0) - top).astype(BF)
                    acc_ref[new, :, c0 : c0 + half] = acc_ref[old, :, c0 : c0 + half] * jnp.exp2(
                        m - top
                    ) + jnp.dot(vt, p, preferred_element_type=F32)
                    m_ref[:, c0 : c0 + half] = jnp.broadcast_to(top, (8, half))

        return 0

    lax.fori_loop(0, n, add_block, 0)
    last = count[0] % 2
    for h in range(heads):
        o = acc_ref[last, :, h * qb : (h + 1) * qb]
        o = (o[0:DH] / o[DH : DH + 1]).T.astype(BF)
        for g in range(groups):
            ry = (g // 4 + n_y - info[3]) % n_y
            rz = (g // 2 % 2) ^ info[4]
            by_y = ((ry * 2 + rz) * 2 + g % 2) * sub
            by_z = (((ry // 2 * 2 + rz) * 2 + ry % 2) * 2 + g % 2) * sub
            piece = o[g * sub : (g + 1) * sub, :]
            here = pl.multiple_of(jnp.where(core == 0, by_y, by_z), sub)
            there = pl.multiple_of(jnp.where(core == 0, by_z, by_y), sub)
            o_ref[pl.ds(here, sub), h * DH : (h + 1) * DH] = piece
            peer_ref[pl.ds(there, sub), h * DH : (h + 1) * DH] = piece


def attend(info, late, q, kv, state, mine, other, n_y, n_seq):
    groups, sub, width = q.shape
    qb = groups * sub
    cols = qb * width // DH
    any_space = pl.BlockSpec(memory_space=pl.ANY)
    out = pl.BlockSpec((qb, width), lambda i, info: (0, 0))
    return pl.pallas_call(
        functools.partial(attend_kernel, late, groups, n_y, n_seq),
        grid_spec=pltpu.PrefetchScalarGridSpec(
            num_scalar_prefetch=1,
            grid=(1,),
            in_specs=[any_space] * (5 + 2 * len(mine)),
            out_specs=[out, out],
            scratch_shapes=[
                pltpu.VMEM(q.shape, BF),
                pltpu.VMEM((len(SLOTS) + 1, *kv.shape), BF),
                pltpu.VMEM((2 * DH, cols), BF),
                pltpu.VMEM((2, DH + 16, cols), F32),
                pltpu.VMEM((8, cols), F32),
                pltpu.VMEM((8, cols), F32),
                pltpu.SMEM((1,), jnp.int32),
                pltpu.SemaphoreType.DMA((len(SLOTS) + 4,)),
            ],
        ),
        out_shape=[jax.ShapeDtypeStruct((qb, width), BF)] * 2,
        name="attend_late" if late else "attend_early",
        cost_estimate=pl.CostEstimate(
            flops=2 * cols * kv.shape[0] * (7 if late else 2) * DH, bytes_accessed=4 << 20, transcendentals=0
        ),
        compiler_params=PARAMS,
    )(info, q, kv, *state, *mine, *other)


def project(info, mine, other, w, w_other, parts, tile):
    rows, width = mine.shape
    n = w.shape[1] // 2
    steps = n // tile

    def body(info, a, b, wa, wb, *outs):
        s = jnp.dot(a[...], wa[...], preferred_element_type=F32) + jnp.dot(
            b[...], wb[...], preferred_element_type=F32
        )
        part = s.shape[0] // len(outs)
        for i, o in enumerate(outs):
            o[...] = s[i * part : (i + 1) * part].astype(BF)

    whole = pl.BlockSpec((rows, width), lambda i, info: (0, 0))
    weights = pl.BlockSpec((width, tile), lambda i, info: (0, info[2] * steps + i))
    return pl.pallas_call(
        body,
        grid_spec=pltpu.PrefetchScalarGridSpec(
            num_scalar_prefetch=1,
            grid=(steps,),
            in_specs=[whole, whole, weights, weights],
            out_specs=[pl.BlockSpec((rows // parts, tile), lambda i, info: (0, i))] * parts,
        ),
        out_shape=[jax.ShapeDtypeStruct((rows // parts, n), BF)] * parts,
        name="project",
        cost_estimate=pl.CostEstimate(
            flops=4 * rows * width * n, bytes_accessed=4 * width * n + 4 * rows * n, transcendentals=0
        ),
        compiler_params=PARAMS,
    )(info, mine, other, w, w_other)


def add(*terms):
    total = terms[0].astype(F32)
    for t in terms[1:]:
        total = total + t.astype(F32)
    return total.astype(BF)


def local(queries, keys, values, w_out):
    n_seq, n_head = lax.axis_size("seq"), lax.axis_size("head")
    rows, width = queries.shape
    cols = w_out.shape[1]
    place = lax.axis_index("seq")
    head = lax.axis_index("head")
    core, y, z = head % 2, head // 4, head // 2 % 2
    n_y = n_head // 4
    partner = n_seq - 1 - place
    info = jnp.stack([place, head * KV_HEADS // n_head, core, y, z, partner, *SLOTS]).astype(jnp.int32)

    def over_all(x, f):
        pairs = []
        for s in range(n_seq):
            for h in range(n_head):
                to = f(s, h // 4, h // 2 % 2, h % 2)
                if to is not None:
                    s2, y2, z2, c2 = to
                    pairs.append((s * n_head + h, s2 * n_head + (y2 % n_y) * 4 + z2 * 2 + c2))
        return lax.ppermute(x, ("seq", "head"), pairs)

    def swap_core(x):
        return over_all(x, lambda s, y, z, c: (s, y, z, 1 - c))

    def fetch(x, pair):
        def to(s, y, z, c):
            if pair[c] is None:
                return None
            t = s ^ pair[c]
            return (t, y, z, c) if s <= max(t, n_seq - 1 - t) else None

        return over_all(x, to)

    sub = rows // n_head // 2
    q4 = queries.reshape(n_head, 2, sub, width)
    kv = prep(info, keys, values)
    q_far = over_all(q4[:, 1], lambda s, y, z, c: (n_seq - 1 - s, y, z, c))
    mine = [fetch(kv, pair) for pair in FETCH]
    state = own(q4, kv)
    other = [swap_core(after(x, state[2])) for x in mine]
    w_other = swap_core(after(w_out, state[2], q_far, *mine))

    def stage_one(parts):
        return [
            over_all(parts[1], lambda s, y, z, c: (s, y, 1 - z, c) if c else (s, y + 1, z, c)),
            over_all(parts[3], lambda s, y, z, c: (s, y, 1 - z, c) if c else (s, y - 1, z, c)),
            over_all(parts[2], lambda s, y, z, c: None if c else (s, y + 2, z, c)),
        ]

    def sum_one(parts, got):
        first = parts[0].astype(F32) + got[0].astype(F32)
        extra = got[1].astype(F32) + got[2].astype(F32)
        a = (first + jnp.where(core == 0, extra, 0.0)).astype(BF)
        b = add(parts[2], got[1])
        n = a.shape[0] // 2
        return a[:n], a[n:], b[:n], b[n:]

    def stage_two(total):
        return [
            over_all(total[1], lambda s, y, z, c: (s, y + 1, z, c) if c else (s, y, 1 - z, c)),
            over_all(total[3], lambda s, y, z, c: (s, y - 1, z, c) if c else None),
            over_all(total[2], lambda s, y, z, c: (s, y + 2, z, c) if c else None),
        ]

    early, early_peer = attend(info, False, q_far, kv, state, mine, other, n_y, n_seq)
    early_far = swap_core(early_peer)
    parts_e = project(info, early, early_far, w_out, w_other, n_y, cols // 4)
    got_e = stage_one(parts_e)
    late, late_peer = attend(after(info, parts_e[0]), True, q_far, kv, state, mine, other, n_y, n_seq)
    late_far = swap_core(late_peer)
    total_e = sum_one(parts_e, got_e)
    got2_e = stage_two(total_e)
    parts_l = project(after(info, *total_e), late, late_far, w_out, w_other, n_y, cols // 4)
    got_l = stage_one(parts_l)
    done_e = add(after(total_e[0], parts_l[0]), *got2_e).reshape(2, sub, cols // 2)
    total_l = sum_one(parts_l, got_l)
    got2_l = stage_two(total_l)
    done_l = add(total_l[0], *got2_l).reshape(2, sub, cols // 2)

    light = place < partner
    own_rows = jnp.where(light, done_e, done_l)
    far_rows = jnp.where(light, done_l, done_e)

    def by_core(x, same):
        return jnp.where((core == 0) == same, x[0], x[1])

    home = over_all(by_core(far_rows, True), lambda s, y, z, c: (n_seq - 1 - s, y, z, c))
    home_other = over_all(by_core(far_rows, False), lambda s, y, z, c: (n_seq - 1 - s, y, z, 1 - c))
    own_other = swap_core(by_core(own_rows, False))
    here = jnp.concatenate([by_core(own_rows, True), home], axis=0)
    there = jnp.concatenate([own_other, home_other], axis=0)
    left = jnp.where(core == 0, here, there)
    right = jnp.where(core == 0, there, here)
    return jnp.concatenate([left, right], axis=1)


def solution(mesh):
    placed = (P("seq", "head"), P("seq", None), P("seq", None), P("head", None))
    return jax.shard_map(
        local, mesh=mesh, in_specs=placed, out_specs=P(("seq", "head"), None), check_vma=False
    )
```

```python
import functools

import jax
import jax.numpy as jnp
from jax import lax
from jax.experimental import pallas as pl
from jax.experimental.pallas import tpu as pltpu
from jax.sharding import PartitionSpec as P

KV_HEADS = 8
DH = 128
LOG2E = 1.4426950408889634
NEG = -1e30
LIMIT = 60.0
BF = jnp.bfloat16
F32 = jnp.float32
PARAMS = pltpu.CompilerParams(vmem_limit_bytes=56 << 20)
FETCH = ((7, 3), (6, 2), (5, 1), (4, None))
SLOTS = [d for pair in FETCH for d in pair if d is not None]
TABLE = 6


def after(x, *deps):
    return lax.optimization_barrier((x, *deps))[0]


def prep_kernel(info, k_ref, v_ref, kv_ref):
    rows = k_ref.shape[0]
    kv_ref[0:rows, :] = k_ref[...]
    for t in range(rows // DH):
        kv_ref[rows + t * DH : rows + (t + 1) * DH, :] = v_ref[t * DH : (t + 1) * DH, :].T


def prep(info, keys, values):
    rows = keys.shape[0]
    col = pl.BlockSpec((rows, DH), lambda i, info: (0, info[1]))
    return pl.pallas_call(
        prep_kernel,
        grid_spec=pltpu.PrefetchScalarGridSpec(
            num_scalar_prefetch=1,
            grid=(1,),
            in_specs=[col, col],
            out_specs=pl.BlockSpec((2 * rows, DH), lambda i, info: (0, 0)),
        ),
        out_shape=jax.ShapeDtypeStruct((2 * rows, DH), BF),
        name="prep",
        compiler_params=PARAMS,
    )(info, keys, values)


def keys_of(kv):
    k = kv[0 : kv.shape[0] // 2, :]
    return jnp.concatenate([k, k], axis=1)


def values_of(kv):
    rows = kv.shape[0] // 2
    tiles = [kv[rows + t * DH : rows + (t + 1) * DH, :] for t in range(rows // DH)]
    return jnp.concatenate([jnp.concatenate(tiles, axis=1), jnp.ones((16, rows), BF)], axis=0)


def load_queries(q, h, qt_ref):
    qb = q.shape[0]
    scaled = q.astype(F32) * (DH**-0.5 * LOG2E)
    high = scaled.astype(BF)
    low = (scaled - high.astype(F32)).astype(BF)
    qt_ref[0:DH, h * qb : (h + 1) * qb] = high.T
    qt_ref[DH : 2 * DH, h * qb : (h + 1) * qb] = low.T


def exact_block(kv, behind, second, groups, qt_ref, acc, m_ref):
    rows = kv.shape[0] // 2
    heads = KV_HEADS // 2
    qb = qt_ref.shape[1] // heads
    sub = qb // groups
    kk, vt = keys_of(kv), values_of(kv)
    j = lax.broadcasted_iota(jnp.int32, (rows, qb), 1)
    pos = behind * rows + j // sub * (rows // groups) + second * sub + j % sub
    allowed = lax.broadcasted_iota(jnp.int32, (rows, qb), 0) <= pos
    for h in range(heads):
        c = slice(h * qb, (h + 1) * qb)
        s = jnp.where(allowed, jnp.dot(kk, qt_ref[:, c], preferred_element_type=F32), NEG)
        m = m_ref[0:1, c]
        top = jnp.maximum(m, jnp.max(s, axis=0, keepdims=True))
        acc[:, c] = acc[:, c] * jnp.exp2(m - top) + jnp.dot(
            vt, jnp.exp2(s - top).astype(BF), preferred_element_type=F32
        )
        m_ref[:, c] = jnp.broadcast_to(top, (8, qb))


def own_kernel(groups, q_ref, kv_ref, qt_ref, acc_ref, m_ref):
    _, _, sub, width = q_ref.shape
    for h in range(width // DH):
        load_queries(q_ref[:, 0, :, h * DH : (h + 1) * DH].reshape(groups * sub, DH), h, qt_ref)
    acc_ref[...] = jnp.zeros_like(acc_ref)
    m_ref[...] = jnp.full_like(m_ref, NEG)
    exact_block(kv_ref, 0, 0, groups, qt_ref, acc_ref, m_ref)


def own(q4, kv):
    groups, _, sub, width = q4.shape
    cols = groups * sub * width // DH
    return pl.pallas_call(
        functools.partial(own_kernel, groups),
        grid=(1,),
        in_specs=[
            pl.BlockSpec((groups, 1, sub, width), lambda i: (0, 0, 0, 0)),
            pl.BlockSpec(kv.shape, lambda i: (0, 0)),
        ],
        out_specs=[
            pl.BlockSpec((2 * DH, cols), lambda i: (0, 0)),
            pl.BlockSpec((DH + 16, cols), lambda i: (0, 0)),
            pl.BlockSpec((8, cols), lambda i: (0, 0)),
        ],
        out_shape=[
            jax.ShapeDtypeStruct((2 * DH, cols), BF),
            jax.ShapeDtypeStruct((DH + 16, cols), F32),
            jax.ShapeDtypeStruct((8, cols), F32),
        ],
        name="own",
        cost_estimate=pl.CostEstimate(
            flops=2 * cols * kv.shape[0] * 2 * DH, bytes_accessed=8 << 20, transcendentals=0
        ),
        compiler_params=PARAMS,
    )(q4, kv)


def attend_kernel(foreign, groups, n_y, n_seq, info, own_ref, *refs):
    ops = n_seq // 2
    inputs = 1 if foreign else 3
    mine, other = refs[inputs : inputs + ops], refs[inputs + ops : inputs + 2 * ops]
    o_ref, peer_ref, q_buf, kv_buf, qt_ref, acc_ref, m_ref, mx_ref, count, sems = refs[inputs + 2 * ops :]
    place, core, partner = info[0], info[2], info[5]
    rows = own_ref.shape[0] // 2
    cols = qt_ref.shape[1]
    heads = KV_HEADS // 2
    qb = cols // heads
    sub = qb // groups
    half = cols // 4
    limit = partner if foreign else place
    n = len(SLOTS)
    if foreign:
        state = [pltpu.make_async_copy(refs[0], q_buf, sems.at[n + 1])]
    else:
        state = [
            pltpu.make_async_copy(refs[0], qt_ref, sems.at[n + 1]),
            pltpu.make_async_copy(refs[1], acc_ref.at[0], sems.at[n + 2]),
            pltpu.make_async_copy(refs[2], m_ref, sems.at[n + 3]),
        ]

    def behind(i):
        return limit - lax.bitwise_xor(place, info[TABLE + i])

    def start(src, slot):
        pltpu.make_async_copy(src, kv_buf.at[slot], sems.at[slot]).start()

    def wait(slot):
        pltpu.make_async_copy(own_ref, kv_buf.at[slot], sems.at[slot]).wait()

    for load in state:
        load.start()
    if foreign:

        @pl.when(place < limit)
        def _():
            start(own_ref, 0)

    for i in range(n):

        @pl.when(jnp.logical_and(behind(i) >= 0, core == i % 2))
        def _():
            start(mine[i // 2], i + 1)

        @pl.when(jnp.logical_and(behind(i) >= 0, core != i % 2))
        def _():
            start(other[i // 2], i + 1)

    for load in state:
        load.wait()
    count[0] = 0
    if foreign:
        for h in range(heads):
            load_queries(q_buf[:, :, h * DH : (h + 1) * DH].reshape(qb, DH), h, qt_ref)
        acc_ref[0] = jnp.zeros(acc_ref.shape[1:], F32)
        m_ref[...] = jnp.full_like(m_ref, NEG)

        def exact(slot, _):
            back = limit - jnp.where(slot == 0, place, partner)

            @pl.when(back >= 0)
            def _():
                wait(slot)
                exact_block(kv_buf.at[slot], back, 1, groups, qt_ref, acc_ref.at[0], m_ref)

            return 0

        lax.fori_loop(0, 2, exact, 0)

    def scores(kk, c0):
        return jnp.dot(kk, qt_ref[:, c0 : c0 + half], preferred_element_type=F32)

    def add_block(i, _):
        @pl.when(behind(i) > 0)
        def _():
            slot = i + 1
            wait(slot)
            old = count[0] % 2
            new = 1 - old
            count[0] = count[0] + 1
            kk, vt = keys_of(kv_buf.at[slot]), values_of(kv_buf.at[slot])
            for c0 in range(0, cols, half):
                s = scores(kk, c0)
                mx_ref[:, c0 : c0 + half] = jnp.max(s.reshape(rows // 8, 8, half), axis=0)
                p = jnp.exp2(s - m_ref[0:1, c0 : c0 + half]).astype(BF)
                acc_ref[new, :, c0 : c0 + half] = acc_ref[old, :, c0 : c0 + half] + jnp.dot(
                    vt, p, preferred_element_type=F32
                )
            over = jnp.max(mx_ref[...] - m_ref[...])

            @pl.when(over > LIMIT)
            def _():
                for c0 in range(0, cols, half):
                    m = m_ref[0:1, c0 : c0 + half]
                    top = jnp.maximum(m, jnp.max(mx_ref[:, c0 : c0 + half], axis=0, keepdims=True))
                    p = jnp.exp2(scores(kk, c0) - top).astype(BF)
                    acc_ref[new, :, c0 : c0 + half] = acc_ref[old, :, c0 : c0 + half] * jnp.exp2(
                        m - top
                    ) + jnp.dot(vt, p, preferred_element_type=F32)
                    m_ref[:, c0 : c0 + half] = jnp.broadcast_to(top, (8, half))

        return 0

    lax.fori_loop(0, n, add_block, 0)
    last = count[0] % 2
    for h in range(heads):
        o = acc_ref[last, :, h * qb : (h + 1) * qb]
        o = (o[0:DH] * (1.0 / o[DH : DH + 1])).astype(BF).T
        for g in range(groups):
            ry = (g // 4 + n_y - info[3]) % n_y
            rz = (g // 2 % 2) ^ info[4]
            by_y = ((ry * 2 + rz) * 2 + g % 2) * sub
            by_z = (((ry // 2 * 2 + rz) * 2 + ry % 2) * 2 + g % 2) * sub
            piece = o[g * sub : (g + 1) * sub, :]
            here = pl.multiple_of(jnp.where(core == 0, by_y, by_z), sub)
            there = pl.multiple_of(jnp.where(core == 0, by_z, by_y), sub)
            o_ref[pl.ds(here, sub), h * DH : (h + 1) * DH] = piece
            peer_ref[pl.ds(there, sub), h * DH : (h + 1) * DH] = piece


def attend(info, kv, state, q_shape, mine, other, n_y, n_seq):
    foreign = len(state) == 1
    groups, sub, width = q_shape
    qb = groups * sub
    cols = qb * width // DH
    any_space = pl.BlockSpec(memory_space=pl.ANY)
    out = pl.BlockSpec((qb, width), lambda i, info: (0, 0))
    return pl.pallas_call(
        functools.partial(attend_kernel, foreign, groups, n_y, n_seq),
        grid_spec=pltpu.PrefetchScalarGridSpec(
            num_scalar_prefetch=1,
            grid=(1,),
            in_specs=[any_space] * (1 + len(state) + 2 * len(mine)),
            out_specs=[out, out],
            scratch_shapes=[
                pltpu.VMEM(q_shape, BF),
                pltpu.VMEM((len(SLOTS) + 1, *kv.shape), BF),
                pltpu.VMEM((2 * DH, cols), BF),
                pltpu.VMEM((2, DH + 16, cols), F32),
                pltpu.VMEM((8, cols), F32),
                pltpu.VMEM((8, cols), F32),
                pltpu.SMEM((1,), jnp.int32),
                pltpu.SemaphoreType.DMA((len(SLOTS) + 4,)),
            ],
        ),
        out_shape=[jax.ShapeDtypeStruct((qb, width), BF)] * 2,
        name="attend_foreign" if foreign else "attend_own",
        cost_estimate=pl.CostEstimate(
            flops=2 * cols * kv.shape[0] * 4 * DH, bytes_accessed=4 << 20, transcendentals=0
        ),
        compiler_params=PARAMS,
    )(info, kv, *state, *mine, *other)


def project(info, mine, other, w, w_other, parts, tile):
    rows, width = mine.shape
    n = w.shape[1] // 2
    steps = n // tile

    def body(info, a, b, wa, wb, *outs):
        s = jnp.dot(a[...], wa[...], preferred_element_type=F32) + jnp.dot(
            b[...], wb[...], preferred_element_type=F32
        )
        part = s.shape[0] // len(outs)
        for i, o in enumerate(outs):
            o[...] = s[i * part : (i + 1) * part].astype(BF)

    whole = pl.BlockSpec((rows, width), lambda i, info: (0, 0))
    weights = pl.BlockSpec((width, tile), lambda i, info: (0, info[2] * steps + i))
    return pl.pallas_call(
        body,
        grid_spec=pltpu.PrefetchScalarGridSpec(
            num_scalar_prefetch=1,
            grid=(steps,),
            in_specs=[whole, whole, weights, weights],
            out_specs=[pl.BlockSpec((rows // parts, tile), lambda i, info: (0, i))] * parts,
        ),
        out_shape=[jax.ShapeDtypeStruct((rows // parts, n), BF)] * parts,
        name="project",
        cost_estimate=pl.CostEstimate(
            flops=4 * rows * width * n, bytes_accessed=4 * width * n + 4 * rows * n, transcendentals=0
        ),
        compiler_params=PARAMS,
    )(info, mine, other, w, w_other)


def sum_one(info, parts, got, tile):
    def body(info, p0, p2, g0, g1, g2, a0, a1, b0, b1):
        first = p0[...].astype(F32) + g0[...].astype(F32)
        middle = g1[...].astype(F32)
        first = first + jnp.where(info[2] == 0, middle + g2[...].astype(F32), 0.0)
        second = p2[...].astype(F32) + middle
        n = a0.shape[0]
        a0[...] = first[:n].astype(BF)
        a1[...] = first[n:].astype(BF)
        b0[...] = second[:n].astype(BF)
        b1[...] = second[n:].astype(BF)

    rows, cols = parts[0].shape
    whole = pl.BlockSpec((rows, tile), lambda i, info: (0, i))
    half = pl.BlockSpec((rows // 2, tile), lambda i, info: (0, i))
    return pl.pallas_call(
        body,
        grid_spec=pltpu.PrefetchScalarGridSpec(
            num_scalar_prefetch=1, grid=(cols // tile,), in_specs=[whole] * 5, out_specs=[half] * 4
        ),
        out_shape=[jax.ShapeDtypeStruct((rows // 2, cols), BF)] * 4,
        name="sum_one",
        compiler_params=PARAMS,
    )(info, parts[0], parts[2], *got)


def add(*terms):
    total = terms[0].astype(F32)
    for t in terms[1:]:
        total = total + t.astype(F32)
    return total.astype(BF)


def local(queries, keys, values, w_out):
    n_seq, n_head = lax.axis_size("seq"), lax.axis_size("head")
    rows, width = queries.shape
    cols = w_out.shape[1]
    place = lax.axis_index("seq")
    head = lax.axis_index("head")
    core, y, z = head % 2, head // 4, head // 2 % 2
    n_y = n_head // 4
    partner = n_seq - 1 - place
    info = jnp.stack([place, head * KV_HEADS // n_head, core, y, z, partner, *SLOTS]).astype(jnp.int32)

    def over_all(x, f):
        pairs = []
        for s in range(n_seq):
            for h in range(n_head):
                to = f(s, h // 4, h // 2 % 2, h % 2)
                if to is not None:
                    s2, y2, z2, c2 = to
                    pairs.append((s * n_head + h, s2 * n_head + (y2 % n_y) * 4 + z2 * 2 + c2))
        return lax.ppermute(x, ("seq", "head"), pairs)

    def swap_core(x):
        return over_all(x, lambda s, y, z, c: (s, y, z, 1 - c))

    def fetch(x, pair):
        def to(s, y, z, c):
            if pair[c] is None:
                return None
            t = s ^ pair[c]
            return (t, y, z, c) if s <= max(t, n_seq - 1 - t) else None

        return over_all(x, to)

    sub = rows // n_head // 2
    q4 = queries.reshape(n_head, 2, sub, width)
    w_other = swap_core(w_out)
    kv = prep(info, keys, values)
    mine = [fetch(kv, pair) for pair in FETCH]
    state = own(q4, kv)
    other = [swap_core(after(x, state[2])) for x in mine]
    q_far = over_all(after(q4[:, 1], state[2], *mine), lambda s, y, z, c: (n_seq - 1 - s, y, z, c))

    def stage_one(parts):
        return [
            over_all(parts[1], lambda s, y, z, c: (s, y, 1 - z, c) if c else (s, y + 1, z, c)),
            over_all(parts[3], lambda s, y, z, c: (s, y, 1 - z, c) if c else (s, y - 1, z, c)),
            over_all(parts[2], lambda s, y, z, c: None if c else (s, y + 2, z, c)),
        ]

    def stage_two(total):
        return [
            over_all(total[1], lambda s, y, z, c: (s, y + 1, z, c) if c else (s, y, 1 - z, c)),
            over_all(total[3], lambda s, y, z, c: (s, y - 1, z, c) if c else None),
            over_all(total[2], lambda s, y, z, c: (s, y + 2, z, c) if c else None),
        ]

    half = (n_head, sub, width)
    near, near_peer = attend(info, kv, state, half, mine, other, n_y, n_seq)
    near_far = swap_core(near_peer)
    parts_n = project(info, near, near_far, w_out, w_other, n_y, cols // 4)
    got_n = stage_one(parts_n)
    far, far_peer = attend(after(info, parts_n[0]), kv, [q_far], half, mine, other, n_y, n_seq)
    far_far = swap_core(far_peer)
    total_n = sum_one(info, parts_n, got_n, cols // 4)
    got2_n = stage_two(total_n)
    parts_f = project(after(info, *total_n), far, far_far, w_out, w_other, n_y, cols // 4)
    done_n = add(total_n[0], *got2_n).reshape(2, sub, cols // 2)
    parts_f = [after(p, done_n) for p in parts_f]
    got_f = stage_one(parts_f)

    def by_core(x, same):
        return jnp.where((core == 0) == same, x[0], x[1])

    own_other = swap_core(by_core(done_n, False))
    total_f = sum_one(info, parts_f, got_f, cols // 4)
    got2_f = stage_two(total_f)
    done_f = add(total_f[0], *got2_f).reshape(2, sub, cols // 2)
    home = over_all(by_core(done_f, True), lambda s, y, z, c: (n_seq - 1 - s, y, z, c))
    home_other = over_all(by_core(done_f, False), lambda s, y, z, c: (n_seq - 1 - s, y, z, 1 - c))
    here = jnp.concatenate([by_core(done_n, True), home], axis=0)
    there = jnp.concatenate([own_other, home_other], axis=0)
    left = jnp.where(core == 0, here, there)
    right = jnp.where(core == 0, there, here)
    return jnp.concatenate([left, right], axis=1)


def solution(mesh):
    placed = (P("seq", "head"), P("seq", None), P("seq", None), P("head", None))
    return jax.shard_map(
        local, mesh=mesh, in_specs=placed, out_specs=P(("seq", "head"), None), check_vma=False
    )
```

```python
import functools

import jax
import jax.numpy as jnp
from jax import lax
from jax.experimental import pallas as pl
from jax.experimental.pallas import tpu as pltpu
from jax.sharding import PartitionSpec as P

KV_HEADS = 8
DH = 128
LOG2E = 1.4426950408889634
NEG = -1e30
LIMIT = 60.0
BF = jnp.bfloat16
F32 = jnp.float32
PARAMS = pltpu.CompilerParams(vmem_limit_bytes=62 << 20)
FETCH = ((7, 3), (6, 2), (5, 1), (4, None))
SLOTS = [d for pair in FETCH for d in pair if d is not None]
TABLE = 6


def after(x, *deps):
    return lax.optimization_barrier((x, *deps))[0]


def prep_kernel(info, k_ref, v_ref, kv_ref):
    rows = k_ref.shape[0]
    kv_ref[0:rows, :] = k_ref[...]
    for t in range(rows // DH):
        kv_ref[rows + t * DH : rows + (t + 1) * DH, :] = v_ref[t * DH : (t + 1) * DH, :].T


def prep(info, keys, values):
    rows = keys.shape[0]
    col = pl.BlockSpec((rows, DH), lambda i, info: (0, info[1]))
    return pl.pallas_call(
        prep_kernel,
        grid_spec=pltpu.PrefetchScalarGridSpec(
            num_scalar_prefetch=1,
            grid=(1,),
            in_specs=[col, col],
            out_specs=pl.BlockSpec((2 * rows, DH), lambda i, info: (0, 0)),
        ),
        out_shape=jax.ShapeDtypeStruct((2 * rows, DH), BF),
        name="prep",
        compiler_params=PARAMS,
    )(info, keys, values)


def keys_of(kv):
    k = kv[0 : kv.shape[0] // 2, :]
    return jnp.concatenate([k, k], axis=1)


def values_of(kv):
    rows = kv.shape[0] // 2
    tiles = [kv[rows + t * DH : rows + (t + 1) * DH, :] for t in range(rows // DH)]
    return jnp.concatenate([jnp.concatenate(tiles, axis=1), jnp.ones((16, rows), BF)], axis=0)


def load_queries(q, h, qt_ref):
    qb = q.shape[0]
    scaled = q.astype(F32) * (DH**-0.5 * LOG2E)
    high = scaled.astype(BF)
    low = (scaled - high.astype(F32)).astype(BF)
    qt_ref[0:DH, h * qb : (h + 1) * qb] = high.T
    qt_ref[DH : 2 * DH, h * qb : (h + 1) * qb] = low.T


def exact_block(kv, behind, second, groups, qt_ref, acc, m_ref):
    rows = kv.shape[0] // 2
    heads = KV_HEADS // 2
    qb = qt_ref.shape[1] // heads
    sub = qb // groups
    kk, vt = keys_of(kv), values_of(kv)
    j = lax.broadcasted_iota(jnp.int32, (rows, qb), 1)
    pos = behind * rows + j // sub * (rows // groups) + second * sub + j % sub
    allowed = lax.broadcasted_iota(jnp.int32, (rows, qb), 0) <= pos
    for h in range(heads):
        c = slice(h * qb, (h + 1) * qb)
        s = jnp.where(allowed, jnp.dot(kk, qt_ref[:, c], preferred_element_type=F32), NEG)
        m = m_ref[0:1, c]
        top = jnp.maximum(m, jnp.max(s, axis=0, keepdims=True))
        acc[:, c] = acc[:, c] * jnp.exp2(m - top) + jnp.dot(
            vt, jnp.exp2(s - top).astype(BF), preferred_element_type=F32
        )
        m_ref[:, c] = jnp.broadcast_to(top, (8, qb))


def own_kernel(groups, q_ref, kv_ref, qt_ref, acc_ref, m_ref):
    _, _, sub, width = q_ref.shape
    for h in range(width // DH):
        load_queries(q_ref[:, 0, :, h * DH : (h + 1) * DH].reshape(groups * sub, DH), h, qt_ref)
    acc_ref[...] = jnp.zeros_like(acc_ref)
    m_ref[...] = jnp.full_like(m_ref, NEG)
    exact_block(kv_ref, 0, 0, groups, qt_ref, acc_ref, m_ref)


def own(q4, kv):
    groups, _, sub, width = q4.shape
    cols = groups * sub * width // DH
    return pl.pallas_call(
        functools.partial(own_kernel, groups),
        grid=(1,),
        in_specs=[
            pl.BlockSpec((groups, 1, sub, width), lambda i: (0, 0, 0, 0)),
            pl.BlockSpec(kv.shape, lambda i: (0, 0)),
        ],
        out_specs=[
            pl.BlockSpec((2 * DH, cols), lambda i: (0, 0)),
            pl.BlockSpec((DH + 16, cols), lambda i: (0, 0)),
            pl.BlockSpec((8, cols), lambda i: (0, 0)),
        ],
        out_shape=[
            jax.ShapeDtypeStruct((2 * DH, cols), BF),
            jax.ShapeDtypeStruct((DH + 16, cols), F32),
            jax.ShapeDtypeStruct((8, cols), F32),
        ],
        name="own",
        cost_estimate=pl.CostEstimate(
            flops=2 * cols * kv.shape[0] * 2 * DH, bytes_accessed=8 << 20, transcendentals=0
        ),
        compiler_params=PARAMS,
    )(q4, kv)


def attend_kernel(foreign, groups, n_y, n_seq, info, own_ref, *refs):
    ops = n_seq // 2
    inputs = 1 if foreign else 3
    mine, other = refs[inputs : inputs + ops], refs[inputs + ops : inputs + 2 * ops]
    o_ref, peer_ref, q_buf, kv_buf, qt_ref, acc_ref, m_ref, mx_ref, count, sems = refs[inputs + 2 * ops :]
    place, core, partner = info[0], info[2], info[5]
    rows = own_ref.shape[0] // 2
    cols = qt_ref.shape[1]
    heads = KV_HEADS // 2
    qb = cols // heads
    sub = qb // groups
    half = cols // 4
    limit = partner if foreign else place
    n = len(SLOTS)
    if foreign:
        state = [pltpu.make_async_copy(refs[0], q_buf, sems.at[n + 1])]
    else:
        state = [
            pltpu.make_async_copy(refs[0], qt_ref, sems.at[n + 1]),
            pltpu.make_async_copy(refs[1], acc_ref.at[0], sems.at[n + 2]),
            pltpu.make_async_copy(refs[2], m_ref, sems.at[n + 3]),
        ]

    def behind(i):
        return limit - lax.bitwise_xor(place, info[TABLE + i])

    def start(src, slot):
        pltpu.make_async_copy(src, kv_buf.at[slot], sems.at[slot]).start()

    def wait(slot):
        pltpu.make_async_copy(own_ref, kv_buf.at[slot], sems.at[slot]).wait()

    for load in state:
        load.start()
    if foreign:

        @pl.when(place < limit)
        def _():
            start(own_ref, 0)

    for i in range(n):

        @pl.when(jnp.logical_and(behind(i) >= 0, core == i % 2))
        def _():
            start(mine[i // 2], i + 1)

        @pl.when(jnp.logical_and(behind(i) >= 0, core != i % 2))
        def _():
            start(other[i // 2], i + 1)

    for load in state:
        load.wait()
    count[0] = 0
    if foreign:
        for h in range(heads):
            load_queries(q_buf[:, :, h * DH : (h + 1) * DH].reshape(qb, DH), h, qt_ref)
        acc_ref[0] = jnp.zeros(acc_ref.shape[1:], F32)
        m_ref[...] = jnp.full_like(m_ref, NEG)

        def exact(slot, _):
            back = limit - jnp.where(slot == 0, place, partner)

            @pl.when(back >= 0)
            def _():
                wait(slot)
                exact_block(kv_buf.at[slot], back, 1, groups, qt_ref, acc_ref.at[0], m_ref)

            return 0

        lax.fori_loop(0, 2, exact, 0)

    def scores(kk, c0):
        return jnp.dot(kk, qt_ref[:, c0 : c0 + half], preferred_element_type=F32)

    def add_block(i, _):
        @pl.when(behind(i) > 0)
        def _():
            slot = i + 1
            wait(slot)
            old = count[0] % 2
            new = 1 - old
            count[0] = count[0] + 1
            kk, vt = keys_of(kv_buf.at[slot]), values_of(kv_buf.at[slot])
            for c0 in range(0, cols, half):
                s = scores(kk, c0)
                mx_ref[:, c0 : c0 + half] = jnp.max(s.reshape(rows // 8, 8, half), axis=0)
                p = jnp.exp2(s - m_ref[0:1, c0 : c0 + half]).astype(BF)
                acc_ref[new, :, c0 : c0 + half] = acc_ref[old, :, c0 : c0 + half] + jnp.dot(
                    vt, p, preferred_element_type=F32
                )
            over = jnp.max(mx_ref[...] - m_ref[...])

            @pl.when(over > LIMIT)
            def _():
                for c0 in range(0, cols, half):
                    m = m_ref[0:1, c0 : c0 + half]
                    top = jnp.maximum(m, jnp.max(mx_ref[:, c0 : c0 + half], axis=0, keepdims=True))
                    p = jnp.exp2(scores(kk, c0) - top).astype(BF)
                    acc_ref[new, :, c0 : c0 + half] = acc_ref[old, :, c0 : c0 + half] * jnp.exp2(
                        m - top
                    ) + jnp.dot(vt, p, preferred_element_type=F32)
                    m_ref[:, c0 : c0 + half] = jnp.broadcast_to(top, (8, half))

        return 0

    lax.fori_loop(0, n, add_block, 0)
    last = count[0] % 2
    for h in range(heads):
        o = acc_ref[last, :, h * qb : (h + 1) * qb]
        o = (o[0:DH] * (1.0 / o[DH : DH + 1])).astype(BF).T
        for g in range(groups):
            ry = (g // 4 + n_y - info[3]) % n_y
            rz = (g // 2 % 2) ^ info[4]
            by_y = ((ry * 2 + rz) * 2 + g % 2) * sub
            by_z = (((ry // 2 * 2 + rz) * 2 + ry % 2) * 2 + g % 2) * sub
            piece = o[g * sub : (g + 1) * sub, :]
            here = pl.multiple_of(jnp.where(core == 0, by_y, by_z), sub)
            there = pl.multiple_of(jnp.where(core == 0, by_z, by_y), sub)
            o_ref[pl.ds(here, sub), h * DH : (h + 1) * DH] = piece
            peer_ref[pl.ds(there, sub), h * DH : (h + 1) * DH] = piece


def attend(info, kv, state, q_shape, mine, other, n_y, n_seq):
    foreign = len(state) == 1
    groups, sub, width = q_shape
    qb = groups * sub
    cols = qb * width // DH
    any_space = pl.BlockSpec(memory_space=pl.ANY)
    out = pl.BlockSpec((qb, width), lambda i, info: (0, 0))
    return pl.pallas_call(
        functools.partial(attend_kernel, foreign, groups, n_y, n_seq),
        grid_spec=pltpu.PrefetchScalarGridSpec(
            num_scalar_prefetch=1,
            grid=(1,),
            in_specs=[any_space] * (1 + len(state) + 2 * len(mine)),
            out_specs=[out, out],
            scratch_shapes=[
                pltpu.VMEM(q_shape, BF),
                pltpu.VMEM((len(SLOTS) + 1, *kv.shape), BF),
                pltpu.VMEM((2 * DH, cols), BF),
                pltpu.VMEM((2, DH + 16, cols), F32),
                pltpu.VMEM((8, cols), F32),
                pltpu.VMEM((8, cols), F32),
                pltpu.SMEM((1,), jnp.int32),
                pltpu.SemaphoreType.DMA((len(SLOTS) + 4,)),
            ],
        ),
        out_shape=[jax.ShapeDtypeStruct((qb, width), BF)] * 2,
        name="attend_foreign" if foreign else "attend_own",
        cost_estimate=pl.CostEstimate(
            flops=2 * cols * kv.shape[0] * 4 * DH, bytes_accessed=4 << 20, transcendentals=0
        ),
        compiler_params=PARAMS,
    )(info, kv, *state, *mine, *other)


def project(info, mine, other, w, w_other, parts, tile):
    rows, width = mine.shape
    n = w.shape[1] // 2
    steps = n // tile

    def body(info, a, b, wa, wb, *outs):
        s = jnp.dot(a[...], wa[...], preferred_element_type=F32) + jnp.dot(
            b[...], wb[...], preferred_element_type=F32
        )
        part = s.shape[0] // len(outs)
        for i, o in enumerate(outs):
            o[...] = s[i * part : (i + 1) * part].astype(BF)

    whole = pl.BlockSpec((rows, width), lambda i, info: (0, 0))
    weights = pl.BlockSpec((width, tile), lambda i, info: (0, info[2] * steps + i))
    return pl.pallas_call(
        body,
        grid_spec=pltpu.PrefetchScalarGridSpec(
            num_scalar_prefetch=1,
            grid=(steps,),
            in_specs=[whole, whole, weights, weights],
            out_specs=[pl.BlockSpec((rows // parts, tile), lambda i, info: (0, i))] * parts,
        ),
        out_shape=[jax.ShapeDtypeStruct((rows // parts, n), BF)] * parts,
        name="project",
        cost_estimate=pl.CostEstimate(
            flops=4 * rows * width * n, bytes_accessed=4 * width * n + 4 * rows * n, transcendentals=0
        ),
        compiler_params=PARAMS,
    )(info, mine, other, w, w_other)


def add(*terms):
    total = terms[0].astype(F32)
    for t in terms[1:]:
        total = total + t.astype(F32)
    return total.astype(BF)


def local(queries, keys, values, w_out):
    n_seq, n_head = lax.axis_size("seq"), lax.axis_size("head")
    rows, width = queries.shape
    cols = w_out.shape[1]
    place = lax.axis_index("seq")
    head = lax.axis_index("head")
    core, y, z = head % 2, head // 4, head // 2 % 2
    n_y = n_head // 4
    partner = n_seq - 1 - place
    info = jnp.stack([place, head * KV_HEADS // n_head, core, y, z, partner, *SLOTS]).astype(jnp.int32)

    def over_all(x, f):
        pairs = []
        for s in range(n_seq):
            for h in range(n_head):
                to = f(s, h // 4, h // 2 % 2, h % 2)
                if to is not None:
                    s2, y2, z2, c2 = to
                    pairs.append((s * n_head + h, s2 * n_head + (y2 % n_y) * 4 + z2 * 2 + c2))
        return lax.ppermute(x, ("seq", "head"), pairs)

    def swap_core(x):
        return over_all(x, lambda s, y, z, c: (s, y, z, 1 - c))

    def fetch(x, pair):
        def to(s, y, z, c):
            if pair[c] is None:
                return None
            t = s ^ pair[c]
            return (t, y, z, c) if s <= max(t, n_seq - 1 - t) else None

        return over_all(x, to)

    sub = rows // n_head // 2
    q4 = queries.reshape(n_head, 2, sub, width)
    w_other = swap_core(w_out)
    kv = prep(info, keys, values)
    mine = [fetch(kv, pair) for pair in FETCH]
    q_far = over_all(q4[:, 1], lambda s, y, z, c: (n_seq - 1 - s, y, z, c))
    state = own(q4, kv)
    other = [swap_core(after(x, state[2], q_far)) for x in mine]

    def stage_one(parts):
        return [
            over_all(parts[1], lambda s, y, z, c: (s, y, 1 - z, c) if c else (s, y + 1, z, c)),
            over_all(parts[3], lambda s, y, z, c: (s, y, 1 - z, c) if c else (s, y - 1, z, c)),
            over_all(parts[2], lambda s, y, z, c: None if c else (s, y + 2, z, c)),
        ]

    def sum_one(parts, got):
        first = parts[0].astype(F32) + got[0].astype(F32)
        extra = got[1].astype(F32) + got[2].astype(F32)
        a = (first + jnp.where(core == 0, extra, 0.0)).astype(BF)
        b = add(parts[2], got[1])
        n = a.shape[0] // 2
        return a[:n], a[n:], b[:n], b[n:]

    def stage_two(total):
        return [
            over_all(total[1], lambda s, y, z, c: (s, y + 1, z, c) if c else (s, y, 1 - z, c)),
            over_all(total[3], lambda s, y, z, c: (s, y - 1, z, c) if c else None),
            over_all(total[2], lambda s, y, z, c: (s, y + 2, z, c) if c else None),
        ]

    half = (n_head, sub, width)
    near, near_peer = attend(info, kv, state, half, mine, other, n_y, n_seq)
    near_far = swap_core(near_peer)
    parts_n = project(info, near, near_far, w_out, w_other, n_y, cols // 4)
    got_n = stage_one(parts_n)
    far, far_peer = attend(after(info, parts_n[0]), kv, [q_far], half, mine, other, n_y, n_seq)
    far_far = swap_core(far_peer)
    total_n = sum_one([after(p, far) for p in parts_n], got_n)
    got2_n = stage_two(total_n)
    parts_f = project(after(info, *total_n), far, far_far, w_out, w_other, n_y, cols // 4)
    done_n = add(total_n[0], *got2_n).reshape(2, sub, cols // 2)

    def by_core(x, same):
        return jnp.where((core == 0) == same, x[0], x[1])

    own_other = swap_core(by_core(done_n, False))
    parts_f = [after(p, own_other) for p in parts_f]
    got_f = stage_one(parts_f)
    total_f = sum_one(parts_f, got_f)
    got2_f = stage_two(total_f)
    done_f = add(total_f[0], *got2_f).reshape(2, sub, cols // 2)
    home = over_all(by_core(done_f, True), lambda s, y, z, c: (n_seq - 1 - s, y, z, c))
    home_other = over_all(by_core(done_f, False), lambda s, y, z, c: (n_seq - 1 - s, y, z, 1 - c))
    here = jnp.concatenate([by_core(done_n, True), home], axis=0)
    there = jnp.concatenate([own_other, home_other], axis=0)
    left = jnp.where(core == 0, here, there)
    right = jnp.where(core == 0, there, here)
    return jnp.concatenate([left, right], axis=1)


def solution(mesh):
    placed = (P("seq", "head"), P("seq", None), P("seq", None), P("head", None))
    return jax.shard_map(
        local, mesh=mesh, in_specs=placed, out_specs=P(("seq", "head"), None), check_vma=False
    )
```

```python
import functools

import jax
import jax.numpy as jnp
from jax import lax
from jax.experimental import pallas as pl
from jax.experimental.pallas import tpu as pltpu
from jax.sharding import PartitionSpec as P

KV_HEADS = 8
DH = 128
LOG2E = 1.4426950408889634
NEG = -1e30
LIMIT = 60.0
BF = jnp.bfloat16
F32 = jnp.float32
PARAMS = pltpu.CompilerParams(vmem_limit_bytes=62 << 20)
FETCH = ((7, 3), (6, 2), (5, 1), (4, None))
SLOTS = [d for pair in FETCH for d in pair if d is not None]
TABLE = 6


def after(x, *deps):
    return lax.optimization_barrier((x, *deps))[0]


def prep_kernel(info, k_ref, v_ref, kv_ref):
    rows = k_ref.shape[0]
    kv_ref[0:rows, :] = k_ref[...]
    for t in range(rows // DH):
        kv_ref[rows + t * DH : rows + (t + 1) * DH, :] = v_ref[t * DH : (t + 1) * DH, :].T


def prep(info, keys, values):
    rows = keys.shape[0]
    col = pl.BlockSpec((rows, DH), lambda i, info: (0, info[1]))
    return pl.pallas_call(
        prep_kernel,
        grid_spec=pltpu.PrefetchScalarGridSpec(
            num_scalar_prefetch=1,
            grid=(1,),
            in_specs=[col, col],
            out_specs=pl.BlockSpec((2 * rows, DH), lambda i, info: (0, 0)),
        ),
        out_shape=jax.ShapeDtypeStruct((2 * rows, DH), BF),
        name="prep",
        compiler_params=PARAMS,
    )(info, keys, values)


def keys_of(kv):
    k = kv[0 : kv.shape[0] // 2, :]
    return jnp.concatenate([k, k], axis=1)


def values_of(kv):
    rows = kv.shape[0] // 2
    tiles = [kv[rows + t * DH : rows + (t + 1) * DH, :] for t in range(rows // DH)]
    return jnp.concatenate([jnp.concatenate(tiles, axis=1), jnp.ones((16, rows), BF)], axis=0)


def load_queries(q, h, qt_ref):
    qb = q.shape[0]
    scaled = q.astype(F32) * (DH**-0.5 * LOG2E)
    high = scaled.astype(BF)
    low = (scaled - high.astype(F32)).astype(BF)
    qt_ref[0:DH, h * qb : (h + 1) * qb] = high.T
    qt_ref[DH : 2 * DH, h * qb : (h + 1) * qb] = low.T


def exact_block(kv, behind, second, groups, qt_ref, acc, m_ref):
    rows = kv.shape[0] // 2
    heads = KV_HEADS // 2
    qb = qt_ref.shape[1] // heads
    sub = qb // groups
    kk, vt = keys_of(kv), values_of(kv)
    j = lax.broadcasted_iota(jnp.int32, (rows, qb), 1)
    pos = behind * rows + j // sub * (rows // groups) + second * sub + j % sub
    allowed = lax.broadcasted_iota(jnp.int32, (rows, qb), 0) <= pos
    for h in range(heads):
        c = slice(h * qb, (h + 1) * qb)
        s = jnp.where(allowed, jnp.dot(kk, qt_ref[:, c], preferred_element_type=F32), NEG)
        m = m_ref[0:1, c]
        top = jnp.maximum(m, jnp.max(s, axis=0, keepdims=True))
        acc[:, c] = acc[:, c] * jnp.exp2(m - top) + jnp.dot(
            vt, jnp.exp2(s - top).astype(BF), preferred_element_type=F32
        )
        m_ref[:, c] = jnp.broadcast_to(top, (8, qb))


def own_kernel(groups, q_ref, kv_ref, qt_ref, acc_ref, m_ref):
    _, _, sub, width = q_ref.shape
    for h in range(width // DH):
        load_queries(q_ref[:, 0, :, h * DH : (h + 1) * DH].reshape(groups * sub, DH), h, qt_ref)
    acc_ref[...] = jnp.zeros_like(acc_ref)
    m_ref[...] = jnp.full_like(m_ref, NEG)
    exact_block(kv_ref, 0, 0, groups, qt_ref, acc_ref, m_ref)


def own(q4, kv):
    groups, _, sub, width = q4.shape
    cols = groups * sub * width // DH
    return pl.pallas_call(
        functools.partial(own_kernel, groups),
        grid=(1,),
        in_specs=[
            pl.BlockSpec((groups, 1, sub, width), lambda i: (0, 0, 0, 0)),
            pl.BlockSpec(kv.shape, lambda i: (0, 0)),
        ],
        out_specs=[
            pl.BlockSpec((2 * DH, cols), lambda i: (0, 0)),
            pl.BlockSpec((DH + 16, cols), lambda i: (0, 0)),
            pl.BlockSpec((8, cols), lambda i: (0, 0)),
        ],
        out_shape=[
            jax.ShapeDtypeStruct((2 * DH, cols), BF),
            jax.ShapeDtypeStruct((DH + 16, cols), F32),
            jax.ShapeDtypeStruct((8, cols), F32),
        ],
        name="own",
        cost_estimate=pl.CostEstimate(
            flops=2 * cols * kv.shape[0] * 2 * DH, bytes_accessed=8 << 20, transcendentals=0
        ),
        compiler_params=PARAMS,
    )(q4, kv)


def attend_kernel(foreign, groups, n_y, n_seq, info, own_ref, *refs):
    ops = n_seq // 2
    inputs = 1 if foreign else 3
    mine, other = refs[inputs : inputs + ops], refs[inputs + ops : inputs + 2 * ops]
    o_ref, peer_ref, q_buf, kv_buf, qt_ref, acc_ref, m_ref, mx_ref, count, sems = refs[inputs + 2 * ops :]
    place, core, partner = info[0], info[2], info[5]
    rows = own_ref.shape[0] // 2
    cols = qt_ref.shape[1]
    heads = KV_HEADS // 2
    qb = cols // heads
    sub = qb // groups
    half = cols // 4
    limit = partner if foreign else place
    n = len(SLOTS)
    if foreign:
        state = [pltpu.make_async_copy(refs[0], q_buf, sems.at[n + 1])]
    else:
        state = [
            pltpu.make_async_copy(refs[0], qt_ref, sems.at[n + 1]),
            pltpu.make_async_copy(refs[1], acc_ref.at[0], sems.at[n + 2]),
            pltpu.make_async_copy(refs[2], m_ref, sems.at[n + 3]),
        ]

    def behind(i):
        return limit - lax.bitwise_xor(place, info[TABLE + i])

    def start(src, slot):
        pltpu.make_async_copy(src, kv_buf.at[slot], sems.at[slot]).start()

    def wait(slot):
        pltpu.make_async_copy(own_ref, kv_buf.at[slot], sems.at[slot]).wait()

    for load in state:
        load.start()
    if foreign:

        @pl.when(place < limit)
        def _():
            start(own_ref, 0)

    for i in range(n):

        @pl.when(jnp.logical_and(behind(i) >= 0, core == i % 2))
        def _():
            start(mine[i // 2], i + 1)

        @pl.when(jnp.logical_and(behind(i) >= 0, core != i % 2))
        def _():
            start(other[i // 2], i + 1)

    for load in state:
        load.wait()
    count[0] = 0
    if foreign:
        for h in range(heads):
            load_queries(q_buf[:, :, h * DH : (h + 1) * DH].reshape(qb, DH), h, qt_ref)
        acc_ref[0] = jnp.zeros(acc_ref.shape[1:], F32)
        m_ref[...] = jnp.full_like(m_ref, NEG)

        def exact(slot, _):
            back = limit - jnp.where(slot == 0, place, partner)

            @pl.when(back >= 0)
            def _():
                wait(slot)
                exact_block(kv_buf.at[slot], back, 1, groups, qt_ref, acc_ref.at[0], m_ref)

            return 0

        lax.fori_loop(0, 2, exact, 0)

    def scores(kk, c0):
        return jnp.dot(kk, qt_ref[:, c0 : c0 + half], preferred_element_type=F32)

    def add_block(i, _):
        @pl.when(behind(i) > 0)
        def _():
            slot = i + 1
            wait(slot)
            old = count[0] % 2
            new = 1 - old
            count[0] = count[0] + 1
            kk, vt = keys_of(kv_buf.at[slot]), values_of(kv_buf.at[slot])
            for c0 in range(0, cols, half):
                s = scores(kk, c0)
                mx_ref[:, c0 : c0 + half] = jnp.max(s.reshape(rows // 8, 8, half), axis=0)
                p = jnp.exp2(s - m_ref[0:1, c0 : c0 + half]).astype(BF)
                acc_ref[new, :, c0 : c0 + half] = acc_ref[old, :, c0 : c0 + half] + jnp.dot(
                    vt, p, preferred_element_type=F32
                )
            over = jnp.max(mx_ref[...] - m_ref[...])

            @pl.when(over > LIMIT)
            def _():
                for c0 in range(0, cols, half):
                    m = m_ref[0:1, c0 : c0 + half]
                    top = jnp.maximum(m, jnp.max(mx_ref[:, c0 : c0 + half], axis=0, keepdims=True))
                    p = jnp.exp2(scores(kk, c0) - top).astype(BF)
                    acc_ref[new, :, c0 : c0 + half] = acc_ref[old, :, c0 : c0 + half] * jnp.exp2(
                        m - top
                    ) + jnp.dot(vt, p, preferred_element_type=F32)
                    m_ref[:, c0 : c0 + half] = jnp.broadcast_to(top, (8, half))

        return 0

    lax.fori_loop(0, n, add_block, 0)
    last = count[0] % 2
    for h in range(heads):
        o = acc_ref[last, :, h * qb : (h + 1) * qb]
        o = (o[0:DH] * (1.0 / o[DH : DH + 1])).astype(BF).T
        for g in range(groups):
            ry = (g // 4 + n_y - info[3]) % n_y
            rz = (g // 2 % 2) ^ info[4]
            by_y = ((ry * 2 + rz) * 2 + g % 2) * sub
            by_z = (((ry // 2 * 2 + rz) * 2 + ry % 2) * 2 + g % 2) * sub
            piece = o[g * sub : (g + 1) * sub, :]
            here = pl.multiple_of(jnp.where(core == 0, by_y, by_z), sub)
            there = pl.multiple_of(jnp.where(core == 0, by_z, by_y), sub)
            o_ref[pl.ds(here, sub), h * DH : (h + 1) * DH] = piece
            peer_ref[pl.ds(there, sub), h * DH : (h + 1) * DH] = piece


def attend(info, kv, state, q_shape, mine, other, n_y, n_seq):
    foreign = len(state) == 1
    groups, sub, width = q_shape
    qb = groups * sub
    cols = qb * width // DH
    any_space = pl.BlockSpec(memory_space=pltpu.HBM)
    out = pl.BlockSpec((qb, width), lambda i, info: (0, 0))
    return pl.pallas_call(
        functools.partial(attend_kernel, foreign, groups, n_y, n_seq),
        grid_spec=pltpu.PrefetchScalarGridSpec(
            num_scalar_prefetch=1,
            grid=(1,),
            in_specs=[any_space] * (1 + len(state) + 2 * len(mine)),
            out_specs=[out, out],
            scratch_shapes=[
                pltpu.VMEM(q_shape, BF),
                pltpu.VMEM((len(SLOTS) + 1, *kv.shape), BF),
                pltpu.VMEM((2 * DH, cols), BF),
                pltpu.VMEM((2, DH + 16, cols), F32),
                pltpu.VMEM((8, cols), F32),
                pltpu.VMEM((8, cols), F32),
                pltpu.SMEM((1,), jnp.int32),
                pltpu.SemaphoreType.DMA((len(SLOTS) + 4,)),
            ],
        ),
        out_shape=[jax.ShapeDtypeStruct((qb, width), BF)] * 2,
        name="attend_foreign" if foreign else "attend_own",
        cost_estimate=pl.CostEstimate(
            flops=2 * cols * kv.shape[0] * 4 * DH, bytes_accessed=4 << 20, transcendentals=0
        ),
        compiler_params=PARAMS,
    )(info, kv, *state, *mine, *other)


def project(info, mine, other, w, w_other, parts, tile):
    rows, width = mine.shape
    n = w.shape[1] // 2
    steps = n // tile

    def body(info, a, b, wa, wb, *outs):
        s = jnp.dot(a[...], wa[...], preferred_element_type=F32) + jnp.dot(
            b[...], wb[...], preferred_element_type=F32
        )
        part = s.shape[0] // len(outs)
        for i, o in enumerate(outs):
            o[...] = s[i * part : (i + 1) * part].astype(BF)

    whole = pl.BlockSpec((rows, width), lambda i, info: (0, 0))
    weights = pl.BlockSpec((width, tile), lambda i, info: (0, info[2] * steps + i))
    return pl.pallas_call(
        body,
        grid_spec=pltpu.PrefetchScalarGridSpec(
            num_scalar_prefetch=1,
            grid=(steps,),
            in_specs=[whole, whole, weights, weights],
            out_specs=[pl.BlockSpec((rows // parts, tile), lambda i, info: (0, i))] * parts,
        ),
        out_shape=[jax.ShapeDtypeStruct((rows // parts, n), BF)] * parts,
        name="project",
        cost_estimate=pl.CostEstimate(
            flops=4 * rows * width * n, bytes_accessed=4 * width * n + 4 * rows * n, transcendentals=0
        ),
        compiler_params=PARAMS,
    )(info, mine, other, w, w_other)


def add(*terms):
    total = terms[0].astype(F32)
    for t in terms[1:]:
        total = total + t.astype(F32)
    return total.astype(BF)


def local(queries, keys, values, w_out):
    n_seq, n_head = lax.axis_size("seq"), lax.axis_size("head")
    rows, width = queries.shape
    cols = w_out.shape[1]
    place = lax.axis_index("seq")
    head = lax.axis_index("head")
    core, y, z = head % 2, head // 4, head // 2 % 2
    n_y = n_head // 4
    partner = n_seq - 1 - place
    info = jnp.stack([place, head * KV_HEADS // n_head, core, y, z, partner, *SLOTS]).astype(jnp.int32)

    def over_all(x, f):
        pairs = []
        for s in range(n_seq):
            for h in range(n_head):
                to = f(s, h // 4, h // 2 % 2, h % 2)
                if to is not None:
                    s2, y2, z2, c2 = to
                    pairs.append((s * n_head + h, s2 * n_head + (y2 % n_y) * 4 + z2 * 2 + c2))
        return lax.ppermute(x, ("seq", "head"), pairs)

    def swap_core(x):
        return over_all(x, lambda s, y, z, c: (s, y, z, 1 - c))

    def fetch(x, pair):
        def to(s, y, z, c):
            if pair[c] is None:
                return None
            t = s ^ pair[c]
            return (t, y, z, c) if s <= max(t, n_seq - 1 - t) else None

        return over_all(x, to)

    sub = rows // n_head // 2
    q4 = queries.reshape(n_head, 2, sub, width)
    w_other = swap_core(w_out)
    kv = prep(info, keys, values)
    mine = [fetch(kv, pair) for pair in FETCH]
    state = own(q4, kv)
    other = [swap_core(after(x, state[2])) for x in mine]
    q_far = over_all(after(q4[:, 1], state[2], *mine), lambda s, y, z, c: (n_seq - 1 - s, y, z, c))

    def stage_one(parts):
        return [
            over_all(parts[1], lambda s, y, z, c: (s, y, 1 - z, c) if c else (s, y + 1, z, c)),
            over_all(parts[3], lambda s, y, z, c: (s, y, 1 - z, c) if c else (s, y - 1, z, c)),
            over_all(parts[2], lambda s, y, z, c: None if c else (s, y + 2, z, c)),
        ]

    def sum_one(parts, got):
        first = parts[0].astype(F32) + got[0].astype(F32)
        extra = got[1].astype(F32) + got[2].astype(F32)
        a = (first + jnp.where(core == 0, extra, 0.0)).astype(BF)
        b = add(parts[2], got[1])
        n = a.shape[0] // 2
        return a[:n], a[n:], b[:n], b[n:]

    def stage_two(total):
        return [
            over_all(total[1], lambda s, y, z, c: (s, y + 1, z, c) if c else (s, y, 1 - z, c)),
            over_all(total[3], lambda s, y, z, c: (s, y - 1, z, c) if c else None),
            over_all(total[2], lambda s, y, z, c: (s, y + 2, z, c) if c else None),
        ]

    half = (n_head, sub, width)
    near, near_peer = attend(info, kv, state, half, mine, other, n_y, n_seq)
    near_far = swap_core(after(near_peer, q_far))
    parts_n = project(info, near, near_far, w_out, w_other, n_y, cols // 4)
    got_n = stage_one(parts_n)
    far, far_peer = attend(after(info, parts_n[0]), kv, [q_far], half, mine, other, n_y, n_seq)
    far_far = swap_core(far_peer)
    total_n = sum_one([after(p, far) for p in parts_n], got_n)
    got2_n = stage_two(total_n)
    parts_f = project(after(info, *total_n), far, far_far, w_out, w_other, n_y, cols // 4)
    done_n = add(total_n[0], *got2_n).reshape(2, sub, cols // 2)

    def by_core(x, same):
        return jnp.where((core == 0) == same, x[0], x[1])

    own_other = swap_core(by_core(done_n, False))
    parts_f = [after(p, own_other) for p in parts_f]
    got_f = stage_one(parts_f)
    total_f = sum_one(parts_f, got_f)
    got2_f = stage_two(total_f)
    done_f = add(total_f[0], *got2_f).reshape(2, sub, cols // 2)
    home = over_all(by_core(done_f, True), lambda s, y, z, c: (n_seq - 1 - s, y, z, c))
    home_other = over_all(by_core(done_f, False), lambda s, y, z, c: (n_seq - 1 - s, y, z, 1 - c))
    here = jnp.concatenate([by_core(done_n, True), home], axis=0)
    there = jnp.concatenate([own_other, home_other], axis=0)
    left = jnp.where(core == 0, here, there)
    right = jnp.where(core == 0, there, here)
    return jnp.concatenate([left, right], axis=1)


def solution(mesh):
    placed = (P("seq", "head"), P("seq", None), P("seq", None), P("head", None))
    return jax.shard_map(
        local, mesh=mesh, in_specs=placed, out_specs=P(("seq", "head"), None), check_vma=False
    )
```

```python
import functools

import jax
import jax.numpy as jnp
from jax import lax
from jax.experimental import pallas as pl
from jax.experimental.pallas import tpu as pltpu
from jax.sharding import PartitionSpec as P

KV_HEADS = 8
DH = 128
LOG2E = 1.4426950408889634
NEG = -1e30
LIMIT = 60.0
BF = jnp.bfloat16
F32 = jnp.float32
PARAMS = pltpu.CompilerParams(vmem_limit_bytes=64 << 20)
FETCH = ((7, 3), (6, 2), (5, 1), (4, None))
SLOTS = [d for pair in FETCH for d in pair if d is not None]
TABLE = 6


def after(x, *deps):
    return lax.optimization_barrier((x, *deps))[0]


def prep_kernel(info, k_ref, v_ref, kv_ref):
    rows = k_ref.shape[0]
    kv_ref[0:rows, :] = k_ref[...]
    for t in range(rows // DH):
        kv_ref[rows + t * DH : rows + (t + 1) * DH, :] = v_ref[t * DH : (t + 1) * DH, :].T


def prep(info, keys, values):
    rows = keys.shape[0]
    col = pl.BlockSpec((rows, DH), lambda i, info: (0, info[1]))
    return pl.pallas_call(
        prep_kernel,
        grid_spec=pltpu.PrefetchScalarGridSpec(
            num_scalar_prefetch=1,
            grid=(1,),
            in_specs=[col, col],
            out_specs=pl.BlockSpec((2 * rows, DH), lambda i, info: (0, 0)),
        ),
        out_shape=jax.ShapeDtypeStruct((2 * rows, DH), BF),
        name="prep",
        compiler_params=PARAMS,
    )(info, keys, values)


def keys_of(kv):
    k = kv[0 : kv.shape[0] // 2, :]
    return jnp.concatenate([k, k], axis=1)


def values_of(kv):
    rows = kv.shape[0] // 2
    tiles = [kv[rows + t * DH : rows + (t + 1) * DH, :] for t in range(rows // DH)]
    return jnp.concatenate([jnp.concatenate(tiles, axis=1), jnp.ones((16, rows), BF)], axis=0)


def load_queries(q, h, qt_ref):
    qb = q.shape[0]
    scaled = q.astype(F32) * (DH**-0.5 * LOG2E)
    high = scaled.astype(BF)
    low = (scaled - high.astype(F32)).astype(BF)
    qt_ref[0:DH, h * qb : (h + 1) * qb] = high.T
    qt_ref[DH : 2 * DH, h * qb : (h + 1) * qb] = low.T


def exact_block(kv, behind, second, groups, qt_ref, acc, m_ref):
    rows = kv.shape[0] // 2
    heads = KV_HEADS // 2
    qb = qt_ref.shape[1] // heads
    sub = qb // groups
    kk, vt = keys_of(kv), values_of(kv)
    j = lax.broadcasted_iota(jnp.int32, (rows, qb), 1)
    pos = behind * rows + j // sub * (rows // groups) + second * sub + j % sub
    allowed = lax.broadcasted_iota(jnp.int32, (rows, qb), 0) <= pos
    for h in range(heads):
        c = slice(h * qb, (h + 1) * qb)
        s = jnp.where(allowed, jnp.dot(kk, qt_ref[:, c], preferred_element_type=F32), NEG)
        m = m_ref[0:1, c]
        top = jnp.maximum(m, jnp.max(s, axis=0, keepdims=True))
        acc[:, c] = acc[:, c] * jnp.exp2(m - top) + jnp.dot(
            vt, jnp.exp2(s - top).astype(BF), preferred_element_type=F32
        )
        m_ref[:, c] = jnp.broadcast_to(top, (8, qb))


def own_kernel(groups, q_ref, kv_ref, qt_ref, acc_ref, m_ref):
    _, _, sub, width = q_ref.shape
    for h in range(width // DH):
        load_queries(q_ref[:, 0, :, h * DH : (h + 1) * DH].reshape(groups * sub, DH), h, qt_ref)
    acc_ref[...] = jnp.zeros_like(acc_ref)
    m_ref[...] = jnp.full_like(m_ref, NEG)
    exact_block(kv_ref, 0, 0, groups, qt_ref, acc_ref, m_ref)


def own(q4, kv):
    groups, _, sub, width = q4.shape
    cols = groups * sub * width // DH
    return pl.pallas_call(
        functools.partial(own_kernel, groups),
        grid=(1,),
        in_specs=[
            pl.BlockSpec((groups, 1, sub, width), lambda i: (0, 0, 0, 0)),
            pl.BlockSpec(kv.shape, lambda i: (0, 0)),
        ],
        out_specs=[
            pl.BlockSpec((2 * DH, cols), lambda i: (0, 0)),
            pl.BlockSpec((DH + 16, cols), lambda i: (0, 0)),
            pl.BlockSpec((8, cols), lambda i: (0, 0)),
        ],
        out_shape=[
            jax.ShapeDtypeStruct((2 * DH, cols), BF),
            jax.ShapeDtypeStruct((DH + 16, cols), F32),
            jax.ShapeDtypeStruct((8, cols), F32),
        ],
        name="own",
        cost_estimate=pl.CostEstimate(
            flops=2 * cols * kv.shape[0] * 2 * DH, bytes_accessed=8 << 20, transcendentals=0
        ),
        compiler_params=PARAMS,
    )(q4, kv)


def attend_kernel(foreign, groups, n_y, n_seq, info, own_ref, *refs):
    ops = n_seq // 2
    inputs = 1 if foreign else 3
    mine, other = refs[inputs : inputs + ops], refs[inputs + ops : inputs + 2 * ops]
    o_ref, peer_ref, q_buf, kv_buf, qt_ref, acc_ref, m_ref, mx_ref, count, sems = refs[inputs + 2 * ops :]
    place, core, partner = info[0], info[2], info[5]
    rows = own_ref.shape[0] // 2
    cols = qt_ref.shape[1]
    heads = KV_HEADS // 2
    qb = cols // heads
    sub = qb // groups
    half = cols // 4
    limit = partner if foreign else place
    n = len(SLOTS)
    if foreign:
        state = [pltpu.make_async_copy(refs[0], q_buf, sems.at[n + 1])]
    else:
        state = [
            pltpu.make_async_copy(refs[0], qt_ref, sems.at[n + 1]),
            pltpu.make_async_copy(refs[1], acc_ref.at[0], sems.at[n + 2]),
            pltpu.make_async_copy(refs[2], m_ref, sems.at[n + 3]),
        ]

    def behind(i):
        return limit - lax.bitwise_xor(place, info[TABLE + i])

    def start(src, slot):
        pltpu.make_async_copy(src, kv_buf.at[slot], sems.at[slot]).start()

    def wait(slot):
        pltpu.make_async_copy(own_ref, kv_buf.at[slot], sems.at[slot]).wait()

    for load in state:
        load.start()
    if foreign:

        @pl.when(place < limit)
        def _():
            start(own_ref, 0)

    for i in range(n):

        @pl.when(jnp.logical_and(behind(i) >= 0, core == i % 2))
        def _():
            start(mine[i // 2], i + 1)

        @pl.when(jnp.logical_and(behind(i) >= 0, core != i % 2))
        def _():
            start(other[i // 2], i + 1)

    for load in state:
        load.wait()
    count[0] = 0
    if foreign:
        for h in range(heads):
            load_queries(q_buf[:, :, h * DH : (h + 1) * DH].reshape(qb, DH), h, qt_ref)
        acc_ref[0] = jnp.zeros(acc_ref.shape[1:], F32)
        m_ref[...] = jnp.full_like(m_ref, NEG)

        wait(1)
        exact_block(kv_buf.at[1], 0, 1, groups, qt_ref, acc_ref.at[0], m_ref)

    def scores(kk, c0):
        return jnp.dot(kk, qt_ref[:, c0 : c0 + half], preferred_element_type=F32)

    def add_block(slot, _):
        i = jnp.maximum(slot - 1, 0)

        @pl.when(jnp.where(slot == 0, limit - place, behind(i)) > 0)
        def _():
            wait(slot)
            old = count[0] % 2
            new = 1 - old
            count[0] = count[0] + 1
            kk, vt = keys_of(kv_buf.at[slot]), values_of(kv_buf.at[slot])
            for c0 in range(0, cols, half):
                s = scores(kk, c0)
                mx_ref[:, c0 : c0 + half] = jnp.max(s.reshape(rows // 8, 8, half), axis=0)
                p = jnp.exp2(s - m_ref[0:1, c0 : c0 + half]).astype(BF)
                acc_ref[new, :, c0 : c0 + half] = acc_ref[old, :, c0 : c0 + half] + jnp.dot(
                    vt, p, preferred_element_type=F32
                )
            over = jnp.max(mx_ref[...] - m_ref[...])

            @pl.when(over > LIMIT)
            def _():
                for c0 in range(0, cols, half):
                    m = m_ref[0:1, c0 : c0 + half]
                    top = jnp.maximum(m, jnp.max(mx_ref[:, c0 : c0 + half], axis=0, keepdims=True))
                    p = jnp.exp2(scores(kk, c0) - top).astype(BF)
                    acc_ref[new, :, c0 : c0 + half] = acc_ref[old, :, c0 : c0 + half] * jnp.exp2(
                        m - top
                    ) + jnp.dot(vt, p, preferred_element_type=F32)
                    m_ref[:, c0 : c0 + half] = jnp.broadcast_to(top, (8, half))

        return 0

    lax.fori_loop(0, n + 1, add_block, 0)
    last = count[0] % 2
    for h in range(heads):
        o = acc_ref[last, :, h * qb : (h + 1) * qb]
        o = (o[0:DH] * (1.0 / o[DH : DH + 1])).astype(BF).T
        for g in range(groups):
            ry = (g // 4 + n_y - info[3]) % n_y
            rz = (g // 2 % 2) ^ info[4]
            by_y = ((ry * 2 + rz) * 2 + g % 2) * sub
            by_z = (((ry // 2 * 2 + rz) * 2 + ry % 2) * 2 + g % 2) * sub
            piece = o[g * sub : (g + 1) * sub, :]
            here = pl.multiple_of(jnp.where(core == 0, by_y, by_z), sub)
            there = pl.multiple_of(jnp.where(core == 0, by_z, by_y), sub)
            o_ref[pl.ds(here, sub), h * DH : (h + 1) * DH] = piece
            peer_ref[pl.ds(there, sub), h * DH : (h + 1) * DH] = piece


def attend(info, kv, state, q_shape, mine, other, n_y, n_seq):
    foreign = len(state) == 1
    groups, sub, width = q_shape
    qb = groups * sub
    cols = qb * width // DH
    any_space = pl.BlockSpec(memory_space=pltpu.HBM)
    out = pl.BlockSpec((qb, width), lambda i, info: (0, 0))
    return pl.pallas_call(
        functools.partial(attend_kernel, foreign, groups, n_y, n_seq),
        grid_spec=pltpu.PrefetchScalarGridSpec(
            num_scalar_prefetch=1,
            grid=(1,),
            in_specs=[any_space] * (1 + len(state) + 2 * len(mine)),
            out_specs=[out, out],
            scratch_shapes=[
                pltpu.VMEM(q_shape, BF),
                pltpu.VMEM((len(SLOTS) + 1, *kv.shape), BF),
                pltpu.VMEM((2 * DH, cols), BF),
                pltpu.VMEM((2, DH + 16, cols), F32),
                pltpu.VMEM((8, cols), F32),
                pltpu.VMEM((8, cols), F32),
                pltpu.SMEM((1,), jnp.int32),
                pltpu.SemaphoreType.DMA((len(SLOTS) + 4,)),
            ],
        ),
        out_shape=[jax.ShapeDtypeStruct((qb, width), BF)] * 2,
        name="attend_foreign" if foreign else "attend_own",
        cost_estimate=pl.CostEstimate(
            flops=2 * cols * kv.shape[0] * 4 * DH, bytes_accessed=4 << 20, transcendentals=0
        ),
        compiler_params=PARAMS,
    )(info, kv, *state, *mine, *other)


def project(info, mine, other, w, w_other, parts, tile):
    rows, width = mine.shape
    n = w.shape[1] // 2
    steps = n // tile

    def body(info, a, b, wa, wb, *outs):
        s = jnp.dot(a[...], wa[...], preferred_element_type=F32) + jnp.dot(
            b[...], wb[...], preferred_element_type=F32
        )
        part = s.shape[0] // len(outs)
        for i, o in enumerate(outs):
            o[...] = s[i * part : (i + 1) * part].astype(BF)

    whole = pl.BlockSpec((rows, width), lambda i, info: (0, 0))
    weights = pl.BlockSpec((width, tile), lambda i, info: (0, info[2] * steps + i))
    return pl.pallas_call(
        body,
        grid_spec=pltpu.PrefetchScalarGridSpec(
            num_scalar_prefetch=1,
            grid=(steps,),
            in_specs=[whole, whole, weights, weights],
            out_specs=[pl.BlockSpec((rows // parts, tile), lambda i, info: (0, i))] * parts,
        ),
        out_shape=[jax.ShapeDtypeStruct((rows // parts, n), BF)] * parts,
        name="project",
        cost_estimate=pl.CostEstimate(
            flops=4 * rows * width * n, bytes_accessed=4 * width * n + 4 * rows * n, transcendentals=0
        ),
        compiler_params=PARAMS,
    )(info, mine, other, w, w_other)


def add(*terms):
    total = terms[0].astype(F32)
    for t in terms[1:]:
        total = total + t.astype(F32)
    return total.astype(BF)


def local(queries, keys, values, w_out):
    n_seq, n_head = lax.axis_size("seq"), lax.axis_size("head")
    rows, width = queries.shape
    cols = w_out.shape[1]
    place = lax.axis_index("seq")
    head = lax.axis_index("head")
    core, y, z = head % 2, head // 4, head // 2 % 2
    n_y = n_head // 4
    partner = n_seq - 1 - place
    info = jnp.stack([place, head * KV_HEADS // n_head, core, y, z, partner, *SLOTS]).astype(jnp.int32)

    def over_all(x, f):
        pairs = []
        for s in range(n_seq):
            for h in range(n_head):
                to = f(s, h // 4, h // 2 % 2, h % 2)
                if to is not None:
                    s2, y2, z2, c2 = to
                    pairs.append((s * n_head + h, s2 * n_head + (y2 % n_y) * 4 + z2 * 2 + c2))
        return lax.ppermute(x, ("seq", "head"), pairs)

    def swap_core(x):
        return over_all(x, lambda s, y, z, c: (s, y, z, 1 - c))

    def fetch(x, pair):
        def to(s, y, z, c):
            if pair[c] is None:
                return None
            t = s ^ pair[c]
            return (t, y, z, c) if s <= max(t, n_seq - 1 - t) else None

        return over_all(x, to)

    sub = rows // n_head // 2
    q4 = queries.reshape(n_head, 2, sub, width)
    w_other = swap_core(w_out)
    kv = prep(info, keys, values)
    mine = [fetch(kv, pair) for pair in FETCH]
    state = own(q4, kv)
    other = [swap_core(after(x, state[2])) for x in mine]
    q_far = over_all(after(q4[:, 1], state[2], *mine), lambda s, y, z, c: (n_seq - 1 - s, y, z, c))

    def stage_one(parts):
        return [
            over_all(parts[1], lambda s, y, z, c: (s, y, 1 - z, c) if c else (s, y + 1, z, c)),
            over_all(parts[3], lambda s, y, z, c: (s, y, 1 - z, c) if c else (s, y - 1, z, c)),
            over_all(parts[2], lambda s, y, z, c: None if c else (s, y + 2, z, c)),
        ]

    def sum_one(parts, got):
        first = parts[0].astype(F32) + got[0].astype(F32)
        extra = got[1].astype(F32) + got[2].astype(F32)
        a = (first + jnp.where(core == 0, extra, 0.0)).astype(BF)
        b = add(parts[2], got[1])
        n = a.shape[0] // 2
        return a[:n], a[n:], b[:n], b[n:]

    def stage_two(total):
        return [
            over_all(total[1], lambda s, y, z, c: (s, y + 1, z, c) if c else (s, y, 1 - z, c)),
            over_all(total[3], lambda s, y, z, c: (s, y - 1, z, c) if c else None),
            over_all(total[2], lambda s, y, z, c: (s, y + 2, z, c) if c else None),
        ]

    half = (n_head, sub, width)
    near, near_peer = attend(info, kv, state, half, mine, other, n_y, n_seq)
    near_far = swap_core(near_peer)
    parts_n = project(after(info, q_far), near, near_far, w_out, w_other, n_y, cols // 4)
    got_n = stage_one(parts_n)
    far, far_peer = attend(after(info, parts_n[0]), kv, [q_far], half, mine, other, n_y, n_seq)
    far_far = swap_core(far_peer)
    total_n = sum_one([after(p, far) for p in parts_n], got_n)
    got2_n = stage_two(total_n)
    parts_f = project(after(info, *total_n), far, far_far, w_out, w_other, n_y, cols // 4)
    done_n = add(total_n[0], *got2_n).reshape(2, sub, cols // 2)

    def by_core(x, same):
        return jnp.where((core == 0) == same, x[0], x[1])

    parts_f = [after(p, done_n) for p in parts_f]
    got_f = stage_one(parts_f)
    own_other = swap_core(by_core(done_n, False))
    total_f = sum_one([after(p, own_other) for p in parts_f], got_f)
    got2_f = stage_two(total_f)
    done_f = add(total_f[0], *got2_f).reshape(2, sub, cols // 2)
    home = over_all(by_core(done_f, True), lambda s, y, z, c: (n_seq - 1 - s, y, z, c))
    home_other = over_all(by_core(done_f, False), lambda s, y, z, c: (n_seq - 1 - s, y, z, 1 - c))
    here = jnp.concatenate([by_core(done_n, True), home], axis=0)
    there = jnp.concatenate([own_other, home_other], axis=0)
    left = jnp.where(core == 0, here, there)
    right = jnp.where(core == 0, there, here)
    return jnp.concatenate([left, right], axis=1)


def solution(mesh):
    placed = (P("seq", "head"), P("seq", None), P("seq", None), P("head", None))
    return jax.shard_map(
        local, mesh=mesh, in_specs=placed, out_specs=P(("seq", "head"), None), check_vma=False
    )
```

```python
import functools

import jax
import jax.numpy as jnp
from jax import lax
from jax.experimental import pallas as pl
from jax.experimental.pallas import tpu as pltpu
from jax.sharding import PartitionSpec as P

KV_HEADS = 8
DH = 128
LOG2E = 1.4426950408889634
NEG = -1e30
LIMIT = 60.0
BF = jnp.bfloat16
F32 = jnp.float32
PARAMS = pltpu.CompilerParams(vmem_limit_bytes=64 << 20)
FETCH = ((7, 3), (6, 2), (5, 1), (4, None))
SLOTS = [d for pair in FETCH for d in pair if d is not None]
TABLE = 6


def after(x, *deps):
    return lax.optimization_barrier((x, *deps))[0]


def prep_kernel(info, k_ref, v_ref, kv_ref):
    rows = k_ref.shape[0]
    kv_ref[0:rows, :] = k_ref[...]
    for t in range(rows // DH):
        kv_ref[rows + t * DH : rows + (t + 1) * DH, :] = v_ref[t * DH : (t + 1) * DH, :].T


def prep(info, keys, values):
    rows = keys.shape[0]
    col = pl.BlockSpec((rows, DH), lambda i, info: (0, info[1]))
    return pl.pallas_call(
        prep_kernel,
        grid_spec=pltpu.PrefetchScalarGridSpec(
            num_scalar_prefetch=1,
            grid=(1,),
            in_specs=[col, col],
            out_specs=pl.BlockSpec((2 * rows, DH), lambda i, info: (0, 0)),
        ),
        out_shape=jax.ShapeDtypeStruct((2 * rows, DH), BF),
        name="prep",
        compiler_params=PARAMS,
    )(info, keys, values)


def keys_of(kv):
    k = kv[0 : kv.shape[0] // 2, :]
    return jnp.concatenate([k, k], axis=1)


def values_of(kv):
    rows = kv.shape[0] // 2
    tiles = [kv[rows + t * DH : rows + (t + 1) * DH, :] for t in range(rows // DH)]
    return jnp.concatenate([jnp.concatenate(tiles, axis=1), jnp.ones((16, rows), BF)], axis=0)


def load_queries(q, h, qt_ref):
    qb = q.shape[0]
    scaled = q.astype(F32) * (DH**-0.5 * LOG2E)
    high = scaled.astype(BF)
    low = (scaled - high.astype(F32)).astype(BF)
    qt_ref[0:DH, h * qb : (h + 1) * qb] = high.T
    qt_ref[DH : 2 * DH, h * qb : (h + 1) * qb] = low.T


def exact_block(kv, behind, second, groups, qt_ref, acc, m_ref):
    rows = kv.shape[0] // 2
    heads = KV_HEADS // 2
    qb = qt_ref.shape[1] // heads
    sub = qb // groups
    kk, vt = keys_of(kv), values_of(kv)
    j = lax.broadcasted_iota(jnp.int32, (rows, qb), 1)
    pos = behind * rows + j // sub * (rows // groups) + second * sub + j % sub
    allowed = lax.broadcasted_iota(jnp.int32, (rows, qb), 0) <= pos
    for h in range(heads):
        c = slice(h * qb, (h + 1) * qb)
        s = jnp.where(allowed, jnp.dot(kk, qt_ref[:, c], preferred_element_type=F32), NEG)
        m = m_ref[0:1, c]
        top = jnp.maximum(m, jnp.max(s, axis=0, keepdims=True))
        acc[:, c] = acc[:, c] * jnp.exp2(m - top) + jnp.dot(
            vt, jnp.exp2(s - top).astype(BF), preferred_element_type=F32
        )
        m_ref[:, c] = jnp.broadcast_to(top, (8, qb))


def own_kernel(groups, q_ref, kv_ref, qt_ref, acc_ref, m_ref):
    _, _, sub, width = q_ref.shape
    for h in range(width // DH):
        load_queries(q_ref[:, 0, :, h * DH : (h + 1) * DH].reshape(groups * sub, DH), h, qt_ref)
    acc_ref[...] = jnp.zeros_like(acc_ref)
    m_ref[...] = jnp.full_like(m_ref, NEG)
    exact_block(kv_ref, 0, 0, groups, qt_ref, acc_ref, m_ref)


def own(q4, kv):
    groups, _, sub, width = q4.shape
    cols = groups * sub * width // DH
    return pl.pallas_call(
        functools.partial(own_kernel, groups),
        grid=(1,),
        in_specs=[
            pl.BlockSpec((groups, 1, sub, width), lambda i: (0, 0, 0, 0)),
            pl.BlockSpec(kv.shape, lambda i: (0, 0)),
        ],
        out_specs=[
            pl.BlockSpec((2 * DH, cols), lambda i: (0, 0)),
            pl.BlockSpec((DH + 16, cols), lambda i: (0, 0)),
            pl.BlockSpec((8, cols), lambda i: (0, 0)),
        ],
        out_shape=[
            jax.ShapeDtypeStruct((2 * DH, cols), BF),
            jax.ShapeDtypeStruct((DH + 16, cols), F32),
            jax.ShapeDtypeStruct((8, cols), F32),
        ],
        name="own",
        cost_estimate=pl.CostEstimate(
            flops=2 * cols * kv.shape[0] * 2 * DH, bytes_accessed=8 << 20, transcendentals=0
        ),
        compiler_params=PARAMS,
    )(q4, kv)


def attend_kernel(foreign, groups, n_y, n_seq, info, own_ref, *refs):
    ops = n_seq // 2
    inputs = 1 if foreign else 3
    mine, other = refs[inputs : inputs + ops], refs[inputs + ops : inputs + 2 * ops]
    o_ref, q_buf, kv_buf, qt_ref, acc_ref, m_ref, mx_ref, count, sems = refs[inputs + 2 * ops :]
    place, core, partner = info[0], info[2], info[5]
    rows = own_ref.shape[0] // 2
    cols = qt_ref.shape[1]
    heads = KV_HEADS // 2
    qb = cols // heads
    sub = qb // groups
    half = cols // 4
    limit = partner if foreign else place
    n = len(SLOTS)
    if foreign:
        state = [pltpu.make_async_copy(refs[0], q_buf, sems.at[n + 1])]
    else:
        state = [
            pltpu.make_async_copy(refs[0], qt_ref, sems.at[n + 1]),
            pltpu.make_async_copy(refs[1], acc_ref.at[0], sems.at[n + 2]),
            pltpu.make_async_copy(refs[2], m_ref, sems.at[n + 3]),
        ]

    def behind(i):
        return limit - lax.bitwise_xor(place, info[TABLE + i])

    def start(src, slot):
        pltpu.make_async_copy(src, kv_buf.at[slot], sems.at[slot]).start()

    def wait(slot):
        pltpu.make_async_copy(own_ref, kv_buf.at[slot], sems.at[slot]).wait()

    for load in state:
        load.start()
    if foreign:

        @pl.when(place < limit)
        def _():
            start(own_ref, 0)

    for i in range(n):

        @pl.when(jnp.logical_and(behind(i) >= 0, core == i % 2))
        def _():
            start(mine[i // 2], i + 1)

        @pl.when(jnp.logical_and(behind(i) >= 0, core != i % 2))
        def _():
            start(other[i // 2], i + 1)

    for load in state:
        load.wait()
    count[0] = 0
    if foreign:
        for h in range(heads):
            load_queries(q_buf[:, :, h * DH : (h + 1) * DH].reshape(qb, DH), h, qt_ref)
        acc_ref[0] = jnp.zeros(acc_ref.shape[1:], F32)
        m_ref[...] = jnp.full_like(m_ref, NEG)

        wait(1)
        exact_block(kv_buf.at[1], 0, 1, groups, qt_ref, acc_ref.at[0], m_ref)

    def scores(kk, c0):
        return jnp.dot(kk, qt_ref[:, c0 : c0 + half], preferred_element_type=F32)

    def add_block(slot, _):
        i = jnp.maximum(slot - 1, 0)

        @pl.when(jnp.where(slot == 0, limit - place, behind(i)) > 0)
        def _():
            wait(slot)
            old = count[0] % 2
            new = 1 - old
            count[0] = count[0] + 1
            kk, vt = keys_of(kv_buf.at[slot]), values_of(kv_buf.at[slot])
            for c0 in range(0, cols, half):
                s = scores(kk, c0)
                mx_ref[:, c0 : c0 + half] = jnp.max(s.reshape(rows // 8, 8, half), axis=0)
                p = jnp.exp2(s - m_ref[0:1, c0 : c0 + half]).astype(BF)
                acc_ref[new, :, c0 : c0 + half] = acc_ref[old, :, c0 : c0 + half] + jnp.dot(
                    vt, p, preferred_element_type=F32
                )
            over = jnp.max(mx_ref[...] - m_ref[...])

            @pl.when(over > LIMIT)
            def _():
                for c0 in range(0, cols, half):
                    m = m_ref[0:1, c0 : c0 + half]
                    top = jnp.maximum(m, jnp.max(mx_ref[:, c0 : c0 + half], axis=0, keepdims=True))
                    p = jnp.exp2(scores(kk, c0) - top).astype(BF)
                    acc_ref[new, :, c0 : c0 + half] = acc_ref[old, :, c0 : c0 + half] * jnp.exp2(
                        m - top
                    ) + jnp.dot(vt, p, preferred_element_type=F32)
                    m_ref[:, c0 : c0 + half] = jnp.broadcast_to(top, (8, half))

        return 0

    lax.fori_loop(0, n + 1, add_block, 0)
    last = count[0] % 2
    for h in range(heads):
        o = acc_ref[last, :, h * qb : (h + 1) * qb]
        o = (o[0:DH] * (1.0 / o[DH : DH + 1])).astype(BF).T
        for g in range(groups):
            ry = (g // 4 + n_y - info[3]) % n_y
            rz = (g // 2 % 2) ^ info[4]
            dst = pl.multiple_of(((ry * 2 + rz) * 2 + g % 2) * sub, sub)
            o_ref[pl.ds(dst, sub), h * DH : (h + 1) * DH] = o[g * sub : (g + 1) * sub, :]


def attend(info, kv, state, q_shape, mine, other, n_y, n_seq):
    foreign = len(state) == 1
    groups, sub, width = q_shape
    qb = groups * sub
    cols = qb * width // DH
    any_space = pl.BlockSpec(memory_space=pltpu.HBM)
    out = pl.BlockSpec((qb, width), lambda i, info: (0, 0))
    return pl.pallas_call(
        functools.partial(attend_kernel, foreign, groups, n_y, n_seq),
        grid_spec=pltpu.PrefetchScalarGridSpec(
            num_scalar_prefetch=1,
            grid=(1,),
            in_specs=[any_space] * (1 + len(state) + 2 * len(mine)),
            out_specs=out,
            scratch_shapes=[
                pltpu.VMEM(q_shape, BF),
                pltpu.VMEM((len(SLOTS) + 1, *kv.shape), BF),
                pltpu.VMEM((2 * DH, cols), BF),
                pltpu.VMEM((2, DH + 16, cols), F32),
                pltpu.VMEM((8, cols), F32),
                pltpu.VMEM((8, cols), F32),
                pltpu.SMEM((1,), jnp.int32),
                pltpu.SemaphoreType.DMA((len(SLOTS) + 4,)),
            ],
        ),
        out_shape=jax.ShapeDtypeStruct((qb, width), BF),
        name="attend_foreign" if foreign else "attend_own",
        cost_estimate=pl.CostEstimate(
            flops=2 * cols * kv.shape[0] * 4 * DH, bytes_accessed=4 << 20, transcendentals=0
        ),
        compiler_params=PARAMS,
    )(info, kv, *state, *mine, *other)


def project(info, mine, other, w, w_other, parts, tile):
    rows, width = mine.shape
    n = w.shape[1] // 2
    steps = n // tile

    def body(info, a, b, wa, wb, *outs):
        s = jnp.dot(a[...], wa[...], preferred_element_type=F32) + jnp.dot(
            b[...], wb[...], preferred_element_type=F32
        )
        part = s.shape[0] // len(outs)
        for i, o in enumerate(outs):
            o[...] = s[i * part : (i + 1) * part].astype(BF)

    whole = pl.BlockSpec((rows, width), lambda i, info: (0, 0))
    weights = pl.BlockSpec((width, tile), lambda i, info: (0, info[2] * steps + i))
    return pl.pallas_call(
        body,
        grid_spec=pltpu.PrefetchScalarGridSpec(
            num_scalar_prefetch=1,
            grid=(steps,),
            in_specs=[whole, whole, weights, weights],
            out_specs=[pl.BlockSpec((rows // parts, tile), lambda i, info: (0, i))] * parts,
        ),
        out_shape=[jax.ShapeDtypeStruct((rows // parts, n), BF)] * parts,
        name="project",
        cost_estimate=pl.CostEstimate(
            flops=4 * rows * width * n, bytes_accessed=4 * width * n + 4 * rows * n, transcendentals=0
        ),
        compiler_params=PARAMS,
    )(info, mine, other, w, w_other)


def add(*terms):
    total = terms[0].astype(F32)
    for t in terms[1:]:
        total = total + t.astype(F32)
    return total.astype(BF)


def local(queries, keys, values, w_out):
    n_seq, n_head = lax.axis_size("seq"), lax.axis_size("head")
    rows, width = queries.shape
    cols = w_out.shape[1]
    place = lax.axis_index("seq")
    head = lax.axis_index("head")
    core, y, z = head % 2, head // 4, head // 2 % 2
    n_y = n_head // 4
    partner = n_seq - 1 - place
    info = jnp.stack([place, head * KV_HEADS // n_head, core, y, z, partner, *SLOTS]).astype(jnp.int32)

    def over_all(x, f):
        pairs = []
        for s in range(n_seq):
            for h in range(n_head):
                to = f(s, h // 4, h // 2 % 2, h % 2)
                if to is not None:
                    s2, y2, z2, c2 = to
                    pairs.append((s * n_head + h, s2 * n_head + (y2 % n_y) * 4 + z2 * 2 + c2))
        return lax.ppermute(x, ("seq", "head"), pairs)

    def swap_core(x):
        return over_all(x, lambda s, y, z, c: (s, y, z, 1 - c))

    def fetch(x, pair):
        def to(s, y, z, c):
            if pair[c] is None:
                return None
            t = s ^ pair[c]
            return (t, y, z, c) if s <= max(t, n_seq - 1 - t) else None

        return over_all(x, to)

    sub = rows // n_head // 2
    q4 = queries.reshape(n_head, 2, sub, width)
    w_other = swap_core(w_out)
    kv = prep(info, keys, values)
    mine = [fetch(kv, pair) for pair in FETCH]
    state = own(q4, kv)
    other = [swap_core(after(x, state[2])) for x in mine]
    q_far = over_all(after(q4[:, 1], state[2], *mine), lambda s, y, z, c: (n_seq - 1 - s, y, z, c))

    ways = [(2, 1), (1, 0), (3, 0), (0, 1), (2, 0), (1, 1), (3, 1)]

    def scatter(parts):
        return [over_all(parts[a * 2 + b], lambda s, y, z, c, a=a, b=b: (s, y + a, z ^ b, c)) for a, b in ways]

    def by_core(x, same):
        return jnp.where((core == 0) == same, x[0], x[1])

    half = (n_head, sub, width)
    near = attend(info, kv, state, half, mine, other, n_y, n_seq)
    near_far = swap_core(near)
    parts_n = project(after(info, q_far), near, near_far, w_out, w_other, 2 * n_y, cols // 4)
    got_n = scatter(parts_n)
    far = attend(after(info, parts_n[0]), kv, [q_far], half, mine, other, n_y, n_seq)
    far_far = swap_core(after(far, *got_n[:4]))
    parts_f = project(info, far, far_far, w_out, w_other, 2 * n_y, cols // 4)
    got_f = scatter(parts_f)
    done_n = add(after(parts_n[0], parts_f[0]), *got_n).reshape(2, sub, cols // 2)
    own_other = swap_core(by_core(done_n, False))
    done_f = add(after(parts_f[0], own_other), *got_f).reshape(2, sub, cols // 2)
    home = over_all(by_core(done_f, True), lambda s, y, z, c: (n_seq - 1 - s, y, z, c))
    home_other = over_all(by_core(done_f, False), lambda s, y, z, c: (n_seq - 1 - s, y, z, 1 - c))
    here = jnp.concatenate([by_core(done_n, True), home], axis=0)
    there = jnp.concatenate([own_other, home_other], axis=0)
    left = jnp.where(core == 0, here, there)
    right = jnp.where(core == 0, there, here)
    return jnp.concatenate([left, right], axis=1)


def solution(mesh):
    placed = (P("seq", "head"), P("seq", None), P("seq", None), P("head", None))
    return jax.shard_map(
        local, mesh=mesh, in_specs=placed, out_specs=P(("seq", "head"), None), check_vma=False
    )
```

```python
import functools

import jax
import jax.numpy as jnp
from jax import lax
from jax.experimental import pallas as pl
from jax.experimental.pallas import tpu as pltpu
from jax.sharding import PartitionSpec as P

KV_HEADS = 8
DH = 128
LOG2E = 1.4426950408889634
NEG = -1e30
LIMIT = 60.0
BF = jnp.bfloat16
F32 = jnp.float32
PARAMS = pltpu.CompilerParams(vmem_limit_bytes=64 << 20)
FETCH = ((7, 3), (6, 2), (5, 1), (4, None))
SLOTS = [d for pair in FETCH for d in pair if d is not None]
TABLE = 6


def after(x, *deps):
    return lax.optimization_barrier((x, *deps))[0]


def prep_kernel(info, k_ref, v_ref, kv_ref):
    rows = k_ref.shape[0]
    kv_ref[0:rows, :] = k_ref[...]
    for t in range(rows // DH):
        kv_ref[rows + t * DH : rows + (t + 1) * DH, :] = v_ref[t * DH : (t + 1) * DH, :].T


def prep(info, keys, values):
    rows = keys.shape[0]
    col = pl.BlockSpec((rows, DH), lambda i, info: (0, info[1]))
    return pl.pallas_call(
        prep_kernel,
        grid_spec=pltpu.PrefetchScalarGridSpec(
            num_scalar_prefetch=1,
            grid=(1,),
            in_specs=[col, col],
            out_specs=pl.BlockSpec((2 * rows, DH), lambda i, info: (0, 0)),
        ),
        out_shape=jax.ShapeDtypeStruct((2 * rows, DH), BF),
        name="prep",
        compiler_params=PARAMS,
    )(info, keys, values)


def keys_of(kv):
    k = kv[0 : kv.shape[0] // 2, :]
    return jnp.concatenate([k, k], axis=1)


def values_of(kv):
    rows = kv.shape[0] // 2
    tiles = [kv[rows + t * DH : rows + (t + 1) * DH, :] for t in range(rows // DH)]
    return jnp.concatenate([jnp.concatenate(tiles, axis=1), jnp.ones((16, rows), BF)], axis=0)


def load_queries(q, h, qt_ref):
    qb = q.shape[0]
    scaled = q.astype(F32) * (DH**-0.5 * LOG2E)
    high = scaled.astype(BF)
    low = (scaled - high.astype(F32)).astype(BF)
    qt_ref[0:DH, h * qb : (h + 1) * qb] = high.T
    qt_ref[DH : 2 * DH, h * qb : (h + 1) * qb] = low.T


def exact_block(kv, behind, second, groups, qt_ref, acc, m_ref):
    rows = kv.shape[0] // 2
    heads = KV_HEADS // 2
    qb = qt_ref.shape[1] // heads
    sub = qb // groups
    kk, vt = keys_of(kv), values_of(kv)
    j = lax.broadcasted_iota(jnp.int32, (rows, qb), 1)
    pos = behind * rows + j // sub * (rows // groups) + second * sub + j % sub
    allowed = lax.broadcasted_iota(jnp.int32, (rows, qb), 0) <= pos
    for h in range(heads):
        c = slice(h * qb, (h + 1) * qb)
        s = jnp.where(allowed, jnp.dot(kk, qt_ref[:, c], preferred_element_type=F32), NEG)
        m = m_ref[0:1, c]
        top = jnp.maximum(m, jnp.max(s, axis=0, keepdims=True))
        acc[:, c] = acc[:, c] * jnp.exp2(m - top) + jnp.dot(
            vt, jnp.exp2(s - top).astype(BF), preferred_element_type=F32
        )
        m_ref[:, c] = jnp.broadcast_to(top, (8, qb))


def own_kernel(groups, q_ref, kv_ref, qt_ref, acc_ref, m_ref):
    _, _, sub, width = q_ref.shape
    for h in range(width // DH):
        load_queries(q_ref[:, 0, :, h * DH : (h + 1) * DH].reshape(groups * sub, DH), h, qt_ref)
    acc_ref[...] = jnp.zeros_like(acc_ref)
    m_ref[...] = jnp.full_like(m_ref, NEG)
    exact_block(kv_ref, 0, 0, groups, qt_ref, acc_ref, m_ref)


def own(q4, kv):
    groups, _, sub, width = q4.shape
    cols = groups * sub * width // DH
    return pl.pallas_call(
        functools.partial(own_kernel, groups),
        grid=(1,),
        in_specs=[
            pl.BlockSpec((groups, 1, sub, width), lambda i: (0, 0, 0, 0)),
            pl.BlockSpec(kv.shape, lambda i: (0, 0)),
        ],
        out_specs=[
            pl.BlockSpec((2 * DH, cols), lambda i: (0, 0)),
            pl.BlockSpec((DH + 16, cols), lambda i: (0, 0)),
            pl.BlockSpec((8, cols), lambda i: (0, 0)),
        ],
        out_shape=[
            jax.ShapeDtypeStruct((2 * DH, cols), BF),
            jax.ShapeDtypeStruct((DH + 16, cols), F32),
            jax.ShapeDtypeStruct((8, cols), F32),
        ],
        name="own",
        cost_estimate=pl.CostEstimate(
            flops=2 * cols * kv.shape[0] * 2 * DH, bytes_accessed=8 << 20, transcendentals=0
        ),
        compiler_params=PARAMS,
    )(q4, kv)


def attend_kernel(foreign, groups, n_y, n_seq, info, own_ref, *refs):
    ops = n_seq // 2
    inputs = 1 if foreign else 3
    mine, other = refs[inputs : inputs + ops], refs[inputs + ops : inputs + 2 * ops]
    o_ref, first_ref, second_ref, q_buf, kv_buf, qt_ref, acc_ref, m_ref, mx_ref, peer_buf, count, sems = refs[
        inputs + 2 * ops :
    ]
    place, core, partner = info[0], info[2], info[5]
    rows = own_ref.shape[0] // 2
    cols = qt_ref.shape[1]
    heads = KV_HEADS // 2
    qb = cols // heads
    sub = qb // groups
    half = cols // 4
    limit = partner if foreign else place
    n = len(SLOTS)
    if foreign:
        state = [pltpu.make_async_copy(refs[0], q_buf, sems.at[n + 1])]
    else:
        state = [
            pltpu.make_async_copy(refs[0], qt_ref, sems.at[n + 1]),
            pltpu.make_async_copy(refs[1], acc_ref.at[0], sems.at[n + 2]),
            pltpu.make_async_copy(refs[2], m_ref, sems.at[n + 3]),
        ]

    def behind(i):
        return limit - lax.bitwise_xor(place, info[TABLE + i])

    def start(src, slot):
        pltpu.make_async_copy(src, kv_buf.at[slot], sems.at[slot]).start()

    def wait(slot):
        pltpu.make_async_copy(own_ref, kv_buf.at[slot], sems.at[slot]).wait()

    for load in state:
        load.start()
    if foreign:

        @pl.when(place < limit)
        def _():
            start(own_ref, 0)

    for i in range(n):

        @pl.when(jnp.logical_and(behind(i) >= 0, core == i % 2))
        def _():
            start(mine[i // 2], i + 1)

        @pl.when(jnp.logical_and(behind(i) >= 0, core != i % 2))
        def _():
            start(other[i // 2], i + 1)

    for load in state:
        load.wait()
    count[0] = 0
    if foreign:
        for h in range(heads):
            load_queries(q_buf[:, :, h * DH : (h + 1) * DH].reshape(qb, DH), h, qt_ref)
        acc_ref[0] = jnp.zeros(acc_ref.shape[1:], F32)
        m_ref[...] = jnp.full_like(m_ref, NEG)

        wait(1)
        exact_block(kv_buf.at[1], 0, 1, groups, qt_ref, acc_ref.at[0], m_ref)

    def scores(kk, c0):
        return jnp.dot(kk, qt_ref[:, c0 : c0 + half], preferred_element_type=F32)

    def add_block(slot, _):
        i = jnp.maximum(slot - 1, 0)

        @pl.when(jnp.where(slot == 0, limit - place, behind(i)) > 0)
        def _():
            wait(slot)
            old = count[0] % 2
            new = 1 - old
            count[0] = count[0] + 1
            kk, vt = keys_of(kv_buf.at[slot]), values_of(kv_buf.at[slot])
            for c0 in range(0, cols, half):
                s = scores(kk, c0)
                mx_ref[:, c0 : c0 + half] = jnp.max(s.reshape(rows // 8, 8, half), axis=0)
                p = jnp.exp2(s - m_ref[0:1, c0 : c0 + half]).astype(BF)
                acc_ref[new, :, c0 : c0 + half] = acc_ref[old, :, c0 : c0 + half] + jnp.dot(
                    vt, p, preferred_element_type=F32
                )
            over = jnp.max(mx_ref[...] - m_ref[...])

            @pl.when(over > LIMIT)
            def _():
                for c0 in range(0, cols, half):
                    m = m_ref[0:1, c0 : c0 + half]
                    top = jnp.maximum(m, jnp.max(mx_ref[:, c0 : c0 + half], axis=0, keepdims=True))
                    p = jnp.exp2(scores(kk, c0) - top).astype(BF)
                    acc_ref[new, :, c0 : c0 + half] = acc_ref[old, :, c0 : c0 + half] * jnp.exp2(
                        m - top
                    ) + jnp.dot(vt, p, preferred_element_type=F32)
                    m_ref[:, c0 : c0 + half] = jnp.broadcast_to(top, (8, half))

        return 0

    lax.fori_loop(0, n + 1, add_block, 0)
    last = count[0] % 2
    for h in range(heads):
        o = acc_ref[last, :, h * qb : (h + 1) * qb]
        o = (o[0:DH] * (1.0 / o[DH : DH + 1])).astype(BF).T
        for g in range(groups):
            ry = (g // 4 + n_y - info[3]) % n_y
            rz = (g // 2 % 2) ^ info[4]
            by_y = ((ry * 2 + rz) * 2 + g % 2) * sub
            by_z = (((ry // 2 * 2 + rz) * 2 + ry % 2) * 2 + g % 2) * sub
            piece = o[g * sub : (g + 1) * sub, :]
            here = pl.multiple_of(jnp.where(core == 0, by_y, by_z), sub)
            there = pl.multiple_of(jnp.where(core == 0, by_z, by_y), sub)
            o_ref[pl.ds(here, sub), h * DH : (h + 1) * DH] = piece
            peer_buf[pl.ds(there, sub), h * DH : (h + 1) * DH] = piece
    first_ref[...] = peer_buf[: qb // 2, :]
    second_ref[...] = peer_buf[qb // 2 :, :]


def attend(info, kv, state, q_shape, mine, other, n_y, n_seq):
    foreign = len(state) == 1
    groups, sub, width = q_shape
    qb = groups * sub
    cols = qb * width // DH
    any_space = pl.BlockSpec(memory_space=pltpu.HBM)
    out = pl.BlockSpec((qb, width), lambda i, info: (0, 0))
    part = pl.BlockSpec((qb // 2, width), lambda i, info: (0, 0))
    return pl.pallas_call(
        functools.partial(attend_kernel, foreign, groups, n_y, n_seq),
        grid_spec=pltpu.PrefetchScalarGridSpec(
            num_scalar_prefetch=1,
            grid=(1,),
            in_specs=[any_space] * (1 + len(state) + 2 * len(mine)),
            out_specs=[out, part, part],
            scratch_shapes=[
                pltpu.VMEM(q_shape, BF),
                pltpu.VMEM((len(SLOTS) + 1, *kv.shape), BF),
                pltpu.VMEM((2 * DH, cols), BF),
                pltpu.VMEM((2, DH + 16, cols), F32),
                pltpu.VMEM((8, cols), F32),
                pltpu.VMEM((8, cols), F32),
                pltpu.VMEM((qb, width), BF),
                pltpu.SMEM((1,), jnp.int32),
                pltpu.SemaphoreType.DMA((len(SLOTS) + 4,)),
            ],
        ),
        out_shape=[jax.ShapeDtypeStruct((rows, width), BF) for rows in (qb, qb // 2, qb // 2)],
        name="attend_foreign" if foreign else "attend_own",
        cost_estimate=pl.CostEstimate(
            flops=2 * cols * kv.shape[0] * 4 * DH, bytes_accessed=4 << 20, transcendentals=0
        ),
        compiler_params=PARAMS,
    )(info, kv, *state, *mine, *other)


def project(info, mine, other, w, w_other, parts, tile, sums=()):
    rows, width = mine.shape
    n = w.shape[1] // 2
    steps = n // tile

    def body(info, a, b0, b1, wa, wb, *refs):
        outs = refs[len(sums) :]
        b = jnp.concatenate([b0[...], b1[...]], axis=0)
        s = jnp.dot(a[...], wa[...], preferred_element_type=F32) + jnp.dot(
            b, wb[...], preferred_element_type=F32
        )
        part = s.shape[0] // parts
        for i, o in enumerate(outs[:parts]):
            o[...] = s[i * part : (i + 1) * part].astype(BF)
        if sums:
            p0, p2, g0, g1, g2 = [ref[...].astype(F32) for ref in refs[: len(sums)]]
            first = p0 + g0 + jnp.where(info[2] == 0, g1 + g2, 0.0)
            second = p2 + g1
            half = part // 2
            for o, x in zip(outs[parts:], (first[:half], first[half:], second[:half], second[half:]), strict=True):
                o[...] = x.astype(BF)

    whole = pl.BlockSpec((rows, width), lambda i, info: (0, 0))
    part = pl.BlockSpec((rows // 2, width), lambda i, info: (0, 0))
    weights = pl.BlockSpec((width, tile), lambda i, info: (0, info[2] * steps + i))

    def strip(r):
        return pl.BlockSpec((r, tile), lambda i, info: (0, i))

    sizes = [rows // parts] * parts + [rows // parts // 2] * (4 if sums else 0)
    return pl.pallas_call(
        body,
        grid_spec=pltpu.PrefetchScalarGridSpec(
            num_scalar_prefetch=1,
            grid=(steps,),
            in_specs=[whole, part, part, weights, weights] + [strip(x.shape[0]) for x in sums],
            out_specs=[strip(r) for r in sizes],
        ),
        out_shape=[jax.ShapeDtypeStruct((r, n), BF) for r in sizes],
        name="project_and_sum" if sums else "project",
        cost_estimate=pl.CostEstimate(flops=0, bytes_accessed=0, transcendentals=0),
        compiler_params=PARAMS,
    )(info, mine, *other, w, w_other, *sums)


def add(*terms):
    total = terms[0].astype(F32)
    for t in terms[1:]:
        total = total + t.astype(F32)
    return total.astype(BF)


def local(queries, keys, values, w_out):
    n_seq, n_head = lax.axis_size("seq"), lax.axis_size("head")
    rows, width = queries.shape
    cols = w_out.shape[1]
    place = lax.axis_index("seq")
    head = lax.axis_index("head")
    core, y, z = head % 2, head // 4, head // 2 % 2
    n_y = n_head // 4
    partner = n_seq - 1 - place
    info = jnp.stack([place, head * KV_HEADS // n_head, core, y, z, partner, *SLOTS]).astype(jnp.int32)

    def over_all(x, f):
        pairs = []
        for s in range(n_seq):
            for h in range(n_head):
                to = f(s, h // 4, h // 2 % 2, h % 2)
                if to is not None:
                    s2, y2, z2, c2 = to
                    pairs.append((s * n_head + h, s2 * n_head + (y2 % n_y) * 4 + z2 * 2 + c2))
        return lax.ppermute(x, ("seq", "head"), pairs)

    def swap_core(x):
        return over_all(x, lambda s, y, z, c: (s, y, z, 1 - c))

    def fetch(x, pair):
        def to(s, y, z, c):
            if pair[c] is None:
                return None
            t = s ^ pair[c]
            return (t, y, z, c) if s <= max(t, n_seq - 1 - t) else None

        return over_all(x, to)

    sub = rows // n_head // 2
    q4 = queries.reshape(n_head, 2, sub, width)
    w_other = swap_core(w_out)
    kv = prep(info, keys, values)
    mine = [fetch(kv, pair) for pair in FETCH]
    state = own(q4, kv)
    other = [swap_core(after(x, state[2])) for x in mine]
    q_far = over_all(after(q4[:, 1], state[2], *mine), lambda s, y, z, c: (n_seq - 1 - s, y, z, c))

    def stage_one(parts):
        return [
            over_all(parts[1], lambda s, y, z, c: (s, y, 1 - z, c) if c else (s, y + 1, z, c)),
            over_all(parts[3], lambda s, y, z, c: (s, y, 1 - z, c) if c else (s, y - 1, z, c)),
            over_all(parts[2], lambda s, y, z, c: None if c else (s, y + 2, z, c)),
        ]

    def sum_one(parts, got):
        first = parts[0].astype(F32) + got[0].astype(F32)
        extra = got[1].astype(F32) + got[2].astype(F32)
        a = (first + jnp.where(core == 0, extra, 0.0)).astype(BF)
        b = add(parts[2], got[1])
        n = a.shape[0] // 2
        return a[:n], a[n:], b[:n], b[n:]

    def stage_two(total):
        return [
            over_all(total[1], lambda s, y, z, c: (s, y + 1, z, c) if c else (s, y, 1 - z, c)),
            over_all(total[3], lambda s, y, z, c: (s, y - 1, z, c) if c else None),
            over_all(total[2], lambda s, y, z, c: (s, y + 2, z, c) if c else None),
        ]

    def by_core(x, same):
        return jnp.where((core == 0) == same, x[0], x[1])

    half = (n_head, sub, width)
    near, *near_peer = attend(info, kv, state, half, mine, other, n_y, n_seq)
    near_far = [swap_core(x) for x in near_peer]
    parts_n = project(info, near, near_far, w_out, w_other, n_y, cols // 4)
    got_n = stage_one(parts_n)
    far, *far_peer = attend(after(info, parts_n[0]), kv, [q_far], half, mine, other, n_y, n_seq)
    far_far = [swap_core(x) for x in far_peer]
    *parts_f, a0, a1, b0, b1 = project(
        info, far, far_far, w_out, w_other, n_y, cols // 4, (parts_n[0], parts_n[2], *got_n)
    )
    got_f = stage_one(parts_f)
    total_f = sum_one(parts_f, got_f)
    got2_n = stage_two((a0, a1, after(b0, total_f[0]), b1))
    got2_f = stage_two(total_f)
    done_f = add(total_f[0], *got2_f).reshape(2, sub, cols // 2)
    done_n = add(after(a0, total_f[0]), *got2_n).reshape(2, sub, cols // 2)
    own_other = swap_core(by_core(done_n, False))
    home = over_all(by_core(done_f, True), lambda s, y, z, c: (n_seq - 1 - s, y, z, c))
    home_other = over_all(by_core(done_f, False), lambda s, y, z, c: (n_seq - 1 - s, y, z, 1 - c))
    here = jnp.concatenate([by_core(done_n, True), home], axis=0)
    there = jnp.concatenate([own_other, home_other], axis=0)
    left = jnp.where(core == 0, here, there)
    right = jnp.where(core == 0, there, here)
    return jnp.concatenate([left, right], axis=1)


def solution(mesh):
    placed = (P("seq", "head"), P("seq", None), P("seq", None), P("head", None))
    return jax.shard_map(
        local, mesh=mesh, in_specs=placed, out_specs=P(("seq", "head"), None), check_vma=False
    )
```

```python
import functools

import jax
import jax.numpy as jnp
from jax import lax
from jax.experimental import pallas as pl
from jax.experimental.pallas import tpu as pltpu
from jax.sharding import PartitionSpec as P

KV_HEADS = 8
DH = 128
LOG2E = 1.4426950408889634
NEG = -1e30
LIMIT = 60.0
BF = jnp.bfloat16
F32 = jnp.float32
PARAMS = pltpu.CompilerParams(vmem_limit_bytes=64 << 20)
FETCH = ((7, 3), (6, 2), (5, 1), (4, None))
SLOTS = [d for pair in FETCH for d in pair if d is not None]
TABLE = 6


def after(x, *deps):
    return lax.optimization_barrier((x, *deps))[0]


def prep_kernel(info, k_ref, v_ref, q_ref, kv_ref, away_ref):
    away_ref[...] = q_ref[:, 0]
    rows = k_ref.shape[0]
    kv_ref[0:rows, :] = k_ref[...]
    for t in range(rows // DH):
        kv_ref[rows + t * DH : rows + (t + 1) * DH, :] = v_ref[t * DH : (t + 1) * DH, :].T


def prep(info, keys, values, q4):
    groups, _, sub, width = q4.shape
    rows = keys.shape[0]
    col = pl.BlockSpec((rows, DH), lambda i, info: (0, info[1]))
    return pl.pallas_call(
        prep_kernel,
        grid_spec=pltpu.PrefetchScalarGridSpec(
            num_scalar_prefetch=1,
            grid=(1,),
            in_specs=[col, col, pl.BlockSpec((groups, 1, sub, width), lambda i, info: (0, 1, 0, 0))],
            out_specs=[
                pl.BlockSpec((2 * rows, DH), lambda i, info: (0, 0)),
                pl.BlockSpec((groups, sub, width), lambda i, info: (0, 0, 0)),
            ],
        ),
        out_shape=[
            jax.ShapeDtypeStruct((2 * rows, DH), BF),
            jax.ShapeDtypeStruct((groups, sub, width), BF),
        ],
        name="prep",
        compiler_params=PARAMS,
    )(info, keys, values, q4)


def keys_of(kv):
    k = kv[0 : kv.shape[0] // 2, :]
    return jnp.concatenate([k, k], axis=1)


def values_of(kv):
    rows = kv.shape[0] // 2
    tiles = [kv[rows + t * DH : rows + (t + 1) * DH, :] for t in range(rows // DH)]
    return jnp.concatenate([jnp.concatenate(tiles, axis=1), jnp.ones((16, rows), BF)], axis=0)


def load_queries(q, h, qt_ref):
    qb = q.shape[0]
    scaled = q.astype(F32) * (DH**-0.5 * LOG2E)
    high = scaled.astype(BF)
    low = (scaled - high.astype(F32)).astype(BF)
    qt_ref[0:DH, h * qb : (h + 1) * qb] = high.T
    qt_ref[DH : 2 * DH, h * qb : (h + 1) * qb] = low.T


def exact_block(kv, behind, second, groups, qt_ref, acc, m_ref):
    rows = kv.shape[0] // 2
    heads = KV_HEADS // 2
    qb = qt_ref.shape[1] // heads
    sub = qb // groups
    kk, vt = keys_of(kv), values_of(kv)
    j = lax.broadcasted_iota(jnp.int32, (rows, qb), 1)
    pos = behind * rows + j // sub * (rows // groups) + second * sub + j % sub
    allowed = lax.broadcasted_iota(jnp.int32, (rows, qb), 0) <= pos
    for h in range(heads):
        c = slice(h * qb, (h + 1) * qb)
        s = jnp.where(allowed, jnp.dot(kk, qt_ref[:, c], preferred_element_type=F32), NEG)
        m = m_ref[0:1, c]
        top = jnp.maximum(m, jnp.max(s, axis=0, keepdims=True))
        acc[:, c] = acc[:, c] * jnp.exp2(m - top) + jnp.dot(
            vt, jnp.exp2(s - top).astype(BF), preferred_element_type=F32
        )
        m_ref[:, c] = jnp.broadcast_to(top, (8, qb))


def own_kernel(groups, q_ref, kv_ref, qt_ref, acc_ref, m_ref):
    _, _, sub, width = q_ref.shape
    for h in range(width // DH):
        load_queries(q_ref[:, 0, :, h * DH : (h + 1) * DH].reshape(groups * sub, DH), h, qt_ref)
    acc_ref[...] = jnp.zeros_like(acc_ref)
    m_ref[...] = jnp.full_like(m_ref, NEG)
    exact_block(kv_ref, 0, 0, groups, qt_ref, acc_ref, m_ref)


def own(q4, kv):
    groups, _, sub, width = q4.shape
    cols = groups * sub * width // DH
    return pl.pallas_call(
        functools.partial(own_kernel, groups),
        grid=(1,),
        in_specs=[
            pl.BlockSpec((groups, 1, sub, width), lambda i: (0, 0, 0, 0)),
            pl.BlockSpec(kv.shape, lambda i: (0, 0)),
        ],
        out_specs=[
            pl.BlockSpec((2 * DH, cols), lambda i: (0, 0)),
            pl.BlockSpec((DH + 16, cols), lambda i: (0, 0)),
            pl.BlockSpec((8, cols), lambda i: (0, 0)),
        ],
        out_shape=[
            jax.ShapeDtypeStruct((2 * DH, cols), BF),
            jax.ShapeDtypeStruct((DH + 16, cols), F32),
            jax.ShapeDtypeStruct((8, cols), F32),
        ],
        name="own",
        cost_estimate=pl.CostEstimate(
            flops=2 * cols * kv.shape[0] * 2 * DH, bytes_accessed=8 << 20, transcendentals=0
        ),
        compiler_params=PARAMS,
    )(q4, kv)


def attend_kernel(foreign, groups, n_y, n_seq, info, own_ref, *refs):
    ops = n_seq // 2
    inputs = 1 if foreign else 3
    mine, other = refs[inputs : inputs + ops], refs[inputs + ops : inputs + 2 * ops]
    o_ref, first_ref, second_ref, q_buf, kv_buf, qt_ref, acc_ref, m_ref, mx_ref, peer_buf, count, sems = refs[
        inputs + 2 * ops :
    ]
    place, core, partner = info[0], info[2], info[5]
    rows = own_ref.shape[0] // 2
    cols = qt_ref.shape[1]
    heads = KV_HEADS // 2
    qb = cols // heads
    sub = qb // groups
    half = cols // 4
    limit = partner if foreign else place
    n = len(SLOTS)
    if foreign:
        state = [pltpu.make_async_copy(refs[0], q_buf, sems.at[n + 1])]
    else:
        state = [
            pltpu.make_async_copy(refs[0], qt_ref, sems.at[n + 1]),
            pltpu.make_async_copy(refs[1], acc_ref.at[0], sems.at[n + 2]),
            pltpu.make_async_copy(refs[2], m_ref, sems.at[n + 3]),
        ]

    def behind(i):
        return limit - lax.bitwise_xor(place, info[TABLE + i])

    def start(src, slot):
        pltpu.make_async_copy(src, kv_buf.at[slot], sems.at[slot]).start()

    def wait(slot):
        pltpu.make_async_copy(own_ref, kv_buf.at[slot], sems.at[slot]).wait()

    for load in state:
        load.start()
    if foreign:

        @pl.when(place < limit)
        def _():
            start(own_ref, 0)

    for i in range(n):

        @pl.when(jnp.logical_and(behind(i) >= 0, core == i % 2))
        def _():
            start(mine[i // 2], i + 1)

        @pl.when(jnp.logical_and(behind(i) >= 0, core != i % 2))
        def _():
            start(other[i // 2], i + 1)

    for load in state:
        load.wait()
    count[0] = 0
    if foreign:
        for h in range(heads):
            load_queries(q_buf[:, :, h * DH : (h + 1) * DH].reshape(qb, DH), h, qt_ref)
        acc_ref[0] = jnp.zeros(acc_ref.shape[1:], F32)
        m_ref[...] = jnp.full_like(m_ref, NEG)

        wait(1)
        exact_block(kv_buf.at[1], 0, 1, groups, qt_ref, acc_ref.at[0], m_ref)

    def scores(kk, c0):
        return jnp.dot(kk, qt_ref[:, c0 : c0 + half], preferred_element_type=F32)

    def add_block(slot, _):
        i = jnp.maximum(slot - 1, 0)

        @pl.when(jnp.where(slot == 0, limit - place, behind(i)) > 0)
        def _():
            wait(slot)
            old = count[0] % 2
            new = 1 - old
            count[0] = count[0] + 1
            kk, vt = keys_of(kv_buf.at[slot]), values_of(kv_buf.at[slot])
            for c0 in range(0, cols, half):
                s = scores(kk, c0)
                mx_ref[:, c0 : c0 + half] = jnp.max(s.reshape(rows // 8, 8, half), axis=0)
                p = jnp.exp2(s - m_ref[0:1, c0 : c0 + half]).astype(BF)
                acc_ref[new, :, c0 : c0 + half] = acc_ref[old, :, c0 : c0 + half] + jnp.dot(
                    vt, p, preferred_element_type=F32
                )
            over = jnp.max(mx_ref[...] - m_ref[...])

            @pl.when(over > LIMIT)
            def _():
                for c0 in range(0, cols, half):
                    m = m_ref[0:1, c0 : c0 + half]
                    top = jnp.maximum(m, jnp.max(mx_ref[:, c0 : c0 + half], axis=0, keepdims=True))
                    p = jnp.exp2(scores(kk, c0) - top).astype(BF)
                    acc_ref[new, :, c0 : c0 + half] = acc_ref[old, :, c0 : c0 + half] * jnp.exp2(
                        m - top
                    ) + jnp.dot(vt, p, preferred_element_type=F32)
                    m_ref[:, c0 : c0 + half] = jnp.broadcast_to(top, (8, half))

        return 0

    lax.fori_loop(0, n + 1, add_block, 0)
    last = count[0] % 2
    for h in range(heads):
        o = acc_ref[last, :, h * qb : (h + 1) * qb]
        o = (o[0:DH] * (1.0 / o[DH : DH + 1])).astype(BF).T
        for g in range(groups):
            ry = (g // 4) ^ info[3]
            rz = (g // 2 % 2) ^ info[4]
            by_y = ((ry * 2 + rz) * 2 + g % 2) * sub
            by_z = (((ry // 2 * 2 + rz) * 2 + ry % 2) * 2 + g % 2) * sub
            piece = o[g * sub : (g + 1) * sub, :]
            here = pl.multiple_of(jnp.where(core == 0, by_y, by_z), sub)
            there = pl.multiple_of(jnp.where(core == 0, by_z, by_y), sub)
            o_ref[pl.ds(here, sub), h * DH : (h + 1) * DH] = piece
            peer_buf[pl.ds(there, sub), h * DH : (h + 1) * DH] = piece
    first_ref[...] = peer_buf[: qb // 2, :]
    second_ref[...] = peer_buf[qb // 2 :, :]


def attend(info, kv, state, q_shape, mine, other, n_y, n_seq):
    foreign = len(state) == 1
    groups, sub, width = q_shape
    qb = groups * sub
    cols = qb * width // DH
    any_space = pl.BlockSpec(memory_space=pltpu.HBM)
    out = pl.BlockSpec((qb, width), lambda i, info: (0, 0))
    part = pl.BlockSpec((qb // 2, width), lambda i, info: (0, 0))
    return pl.pallas_call(
        functools.partial(attend_kernel, foreign, groups, n_y, n_seq),
        grid_spec=pltpu.PrefetchScalarGridSpec(
            num_scalar_prefetch=1,
            grid=(1,),
            in_specs=[any_space] * (1 + len(state) + 2 * len(mine)),
            out_specs=[out, part, part],
            scratch_shapes=[
                pltpu.VMEM(q_shape, BF),
                pltpu.VMEM((len(SLOTS) + 1, *kv.shape), BF),
                pltpu.VMEM((2 * DH, cols), BF),
                pltpu.VMEM((2, DH + 16, cols), F32),
                pltpu.VMEM((8, cols), F32),
                pltpu.VMEM((8, cols), F32),
                pltpu.VMEM((qb, width), BF),
                pltpu.SMEM((1,), jnp.int32),
                pltpu.SemaphoreType.DMA((len(SLOTS) + 4,)),
            ],
        ),
        out_shape=[jax.ShapeDtypeStruct((rows, width), BF) for rows in (qb, qb // 2, qb // 2)],
        name="attend_foreign" if foreign else "attend_own",
        cost_estimate=pl.CostEstimate(
            flops=2 * cols * kv.shape[0] * 4 * DH, bytes_accessed=4 << 20, transcendentals=0
        ),
        compiler_params=PARAMS,
    )(info, kv, *state, *mine, *other)


def project(info, mine, other, w, w_other, parts, tile, sums=()):
    rows, width = mine.shape
    n = w.shape[1] // 2
    steps = n // tile

    def body(info, a, b0, b1, wa, wb, *refs):
        outs = refs[len(sums) :]
        b = jnp.concatenate([b0[...], b1[...]], axis=0)
        s = jnp.dot(a[...], wa[...], preferred_element_type=F32) + jnp.dot(
            b, wb[...], preferred_element_type=F32
        )
        part = s.shape[0] // parts
        for i, o in enumerate(outs[:parts]):
            o[...] = s[i * part : (i + 1) * part].astype(BF)
        if sums:
            p0, p2, g0, g1, g2 = [ref[...].astype(F32) for ref in refs[: len(sums)]]
            first = p0 + g0 + jnp.where(info[2] == 0, g1 + g2, 0.0)
            second = p2 + g1
            half = part // 2
            for o, x in zip(outs[parts:], (first[:half], first[half:], second[:half], second[half:]), strict=True):
                o[...] = x.astype(BF)

    whole = pl.BlockSpec((rows, width), lambda i, info: (0, 0))
    part = pl.BlockSpec((rows // 2, width), lambda i, info: (0, 0))
    weights = pl.BlockSpec((width, tile), lambda i, info: (0, info[2] * steps + i))

    def strip(r):
        return pl.BlockSpec((r, tile), lambda i, info: (0, i))

    sizes = [rows // parts] * parts + [rows // parts // 2] * (4 if sums else 0)
    return pl.pallas_call(
        body,
        grid_spec=pltpu.PrefetchScalarGridSpec(
            num_scalar_prefetch=1,
            grid=(steps,),
            in_specs=[whole, part, part, weights, weights] + [strip(x.shape[0]) for x in sums],
            out_specs=[strip(r) for r in sizes],
        ),
        out_shape=[jax.ShapeDtypeStruct((r, n), BF) for r in sizes],
        name="project_and_sum" if sums else "project",
        cost_estimate=pl.CostEstimate(flops=0, bytes_accessed=0, transcendentals=0),
        compiler_params=PARAMS,
    )(info, mine, *other, w, w_other, *sums)


def add(*terms):
    total = terms[0].astype(F32)
    for t in terms[1:]:
        total = total + t.astype(F32)
    return total.astype(BF)


def local(queries, keys, values, w_out):
    n_seq, n_head = lax.axis_size("seq"), lax.axis_size("head")
    rows, width = queries.shape
    cols = w_out.shape[1]
    place = lax.axis_index("seq")
    head = lax.axis_index("head")
    core, y, z = head % 2, head // 4, head // 2 % 2
    n_y = n_head // 4
    partner = n_seq - 1 - place
    info = jnp.stack([place, head * KV_HEADS // n_head, core, y, z, partner, *SLOTS]).astype(jnp.int32)

    def over_all(x, f):
        pairs = []
        for s in range(n_seq):
            for h in range(n_head):
                to = f(s, h // 4, h // 2 % 2, h % 2)
                if to is not None:
                    s2, y2, z2, c2 = to
                    pairs.append((s * n_head + h, s2 * n_head + (y2 % n_y) * 4 + z2 * 2 + c2))
        return lax.ppermute(x, ("seq", "head"), pairs)

    def swap_core(x):
        return over_all(x, lambda s, y, z, c: (s, y, z, 1 - c))

    def fetch(x, pair):
        def to(s, y, z, c):
            if pair[c] is None:
                return None
            t = s ^ pair[c]
            return (t, y, z, c) if s <= max(t, n_seq - 1 - t) else None

        return over_all(x, to)

    sub = rows // n_head // 2
    q4 = queries.reshape(n_head, 2, sub, width)
    w_other = swap_core(w_out)
    kv, q_away = prep(info, keys, values, q4)
    mine = [fetch(kv, pair) for pair in FETCH]
    state = own(q4, kv)
    other = [swap_core(after(x, state[2])) for x in mine]
    q_far = over_all(after(q_away, state[2], *mine), lambda s, y, z, c: (n_seq - 1 - s, y, z, c))

    def stage_one(parts):
        return [
            over_all(parts[1], lambda s, y, z, c: (s, y, 1 - z, c) if c else (s, y ^ 1, z, c)),
            over_all(parts[3], lambda s, y, z, c: (s, y, 1 - z, c) if c else (s, y ^ 3, z, c)),
            over_all(parts[2], lambda s, y, z, c: None if c else (s, y ^ 2, z, c)),
        ]

    def sum_one(parts, got):
        first = parts[0].astype(F32) + got[0].astype(F32)
        extra = got[1].astype(F32) + got[2].astype(F32)
        a = (first + jnp.where(core == 0, extra, 0.0)).astype(BF)
        b = add(parts[2], got[1])
        n = a.shape[0] // 2
        return a[:n], a[n:], b[:n], b[n:]

    def stage_two(total):
        return [
            over_all(total[1], lambda s, y, z, c: (s, y ^ 1, z, c) if c else (s, y, 1 - z, c)),
            over_all(total[3], lambda s, y, z, c: (s, y ^ 3, z, c) if c else None),
            over_all(total[2], lambda s, y, z, c: (s, y ^ 2, z, c) if c else None),
        ]

    def by_core(x, same):
        return jnp.where((core == 0) == same, x[0], x[1])

    half = (n_head, sub, width)
    near, *near_peer = attend(info, kv, state, half, mine, other, n_y, n_seq)
    near_far = [swap_core(x) for x in near_peer]
    parts_n = project(info, near, near_far, w_out, w_other, n_y, cols // 4)
    got_n = stage_one(parts_n)
    far, *far_peer = attend(after(info, parts_n[0]), kv, [q_far], half, mine, other, n_y, n_seq)
    far_far = [swap_core(x) for x in far_peer]
    *parts_f, a0, a1, b0, b1 = project(
        info, far, far_far, w_out, w_other, n_y, cols // 4, (parts_n[0], parts_n[2], *got_n)
    )
    got_f = stage_one(parts_f)
    total_f = sum_one(parts_f, got_f)
    got2_n = stage_two((a0, a1, after(b0, total_f[0]), b1))
    got2_f = stage_two(total_f)
    done_f = add(total_f[0], *got2_f).reshape(2, sub, cols // 2)
    done_n = add(after(a0, total_f[0]), *got2_n).reshape(2, sub, cols // 2)
    own_other = swap_core(by_core(done_n, False))
    home = over_all(by_core(done_f, True), lambda s, y, z, c: (n_seq - 1 - s, y, z, c))
    home_other = over_all(by_core(done_f, False), lambda s, y, z, c: (n_seq - 1 - s, y, z, 1 - c))
    here = jnp.concatenate([by_core(done_n, True), home], axis=0)
    there = jnp.concatenate([own_other, home_other], axis=0)
    left = jnp.where(core == 0, here, there)
    right = jnp.where(core == 0, there, here)
    return jnp.concatenate([left, right], axis=1)


def solution(mesh):
    placed = (P("seq", "head"), P("seq", None), P("seq", None), P("head", None))
    return jax.shard_map(
        local, mesh=mesh, in_specs=placed, out_specs=P(("seq", "head"), None), check_vma=False
    )
```

```python
import functools

import jax
import jax.numpy as jnp
from jax import lax
from jax.experimental import pallas as pl
from jax.experimental.pallas import tpu as pltpu
from jax.sharding import PartitionSpec as P

KV_HEADS = 8
DH = 128
LOG2E = 1.4426950408889634
NEG = -1e30
LIMIT = 60.0
BF = jnp.bfloat16
F32 = jnp.float32
PARAMS = pltpu.CompilerParams(vmem_limit_bytes=28 << 20)
FETCH = ((7, 3), (6, 2), (5, 1), (4, None))
SLOTS = [d for pair in FETCH for d in pair if d is not None]
TABLE = 6


def after(x, *deps):
    return lax.optimization_barrier((x, *deps))[0]


def prep_kernel(info, k_ref, v_ref, kv_ref):
    rows = k_ref.shape[0]
    kv_ref[0:rows, :] = k_ref[...]
    for t in range(rows // DH):
        kv_ref[rows + t * DH : rows + (t + 1) * DH, :] = v_ref[t * DH : (t + 1) * DH, :].T


def prep(info, keys, values):
    rows = keys.shape[0]
    col = pl.BlockSpec((rows, DH), lambda i, info: (0, info[1]))
    return pl.pallas_call(
        prep_kernel,
        grid_spec=pltpu.PrefetchScalarGridSpec(
            num_scalar_prefetch=1,
            grid=(1,),
            in_specs=[col, col],
            out_specs=pl.BlockSpec((2 * rows, DH), lambda i, info: (0, 0)),
        ),
        out_shape=jax.ShapeDtypeStruct((2 * rows, DH), BF),
        name="prep",
        compiler_params=pltpu.CompilerParams(vmem_limit_bytes=64 << 20),
    )(info, keys, values)


def keys_of(kv):
    k = kv[0 : kv.shape[0] // 2, :]
    return jnp.concatenate([k, k], axis=1)


def values_of(kv):
    rows = kv.shape[0] // 2
    tiles = [kv[rows + t * DH : rows + (t + 1) * DH, :] for t in range(rows // DH)]
    return jnp.concatenate([jnp.concatenate(tiles, axis=1), jnp.ones((16, rows), BF)], axis=0)


def load_queries(q, h, qt_ref):
    qb = q.shape[0]
    scaled = q.astype(F32) * (DH**-0.5 * LOG2E)
    high = scaled.astype(BF)
    low = (scaled - high.astype(F32)).astype(BF)
    qt_ref[0:DH, h * qb : (h + 1) * qb] = high.T
    qt_ref[DH : 2 * DH, h * qb : (h + 1) * qb] = low.T


def exact_block(kv, behind, second, groups, qt_ref, acc, m_ref):
    rows = kv.shape[0] // 2
    heads = KV_HEADS // 2
    qb = qt_ref.shape[1] // heads
    sub = qb // groups
    kk, vt = keys_of(kv), values_of(kv)
    j = lax.broadcasted_iota(jnp.int32, (rows, qb), 1)
    pos = behind * rows + j // sub * (rows // groups) + second * sub + j % sub
    allowed = lax.broadcasted_iota(jnp.int32, (rows, qb), 0) <= pos
    for h in range(heads):
        c = slice(h * qb, (h + 1) * qb)
        s = jnp.where(allowed, jnp.dot(kk, qt_ref[:, c], preferred_element_type=F32), NEG)
        m = m_ref[0:1, c]
        top = jnp.maximum(m, jnp.max(s, axis=0, keepdims=True))
        acc[:, c] = acc[:, c] * jnp.exp2(m - top) + jnp.dot(
            vt, jnp.exp2(s - top).astype(BF), preferred_element_type=F32
        )
        m_ref[:, c] = jnp.broadcast_to(top, (8, qb))


def own_kernel(groups, q_ref, away_ref, kv_ref, qt_ref, acc_ref, m_ref, send_ref):
    send_ref[...] = away_ref[:, 0]
    _, _, sub, width = q_ref.shape
    for h in range(width // DH):
        load_queries(q_ref[:, 0, :, h * DH : (h + 1) * DH].reshape(groups * sub, DH), h, qt_ref)
    acc_ref[...] = jnp.zeros_like(acc_ref)
    m_ref[...] = jnp.full_like(m_ref, NEG)
    exact_block(kv_ref, 0, 0, groups, qt_ref, acc_ref, m_ref)


def own(q4, kv):
    groups, _, sub, width = q4.shape
    cols = groups * sub * width // DH
    return pl.pallas_call(
        functools.partial(own_kernel, groups),
        grid=(1,),
        in_specs=[
            pl.BlockSpec((groups, 1, sub, width), lambda i: (0, 0, 0, 0)),
            pl.BlockSpec((groups, 1, sub, width), lambda i: (0, 1, 0, 0)),
            pl.BlockSpec(kv.shape, lambda i: (0, 0)),
        ],
        out_specs=[
            pl.BlockSpec((2 * DH, cols), lambda i: (0, 0)),
            pl.BlockSpec((DH + 16, cols), lambda i: (0, 0)),
            pl.BlockSpec((8, cols), lambda i: (0, 0)),
            pl.BlockSpec((groups, sub, width), lambda i: (0, 0, 0)),
        ],
        out_shape=[
            jax.ShapeDtypeStruct((2 * DH, cols), BF),
            jax.ShapeDtypeStruct((DH + 16, cols), F32),
            jax.ShapeDtypeStruct((8, cols), F32),
            jax.ShapeDtypeStruct((groups, sub, width), BF),
        ],
        name="own",
        cost_estimate=pl.CostEstimate(
            flops=2 * cols * kv.shape[0] * 2 * DH, bytes_accessed=8 << 20, transcendentals=0
        ),
        compiler_params=PARAMS,
    )(q4, q4, kv)


def attend_kernel(foreign, groups, n_y, n_seq, info, own_ref, *refs):
    ops = n_seq // 2
    inputs = 1 if foreign else 3
    mine, other = refs[inputs : inputs + ops], refs[inputs + ops : inputs + 2 * ops]
    o_ref, first_ref, second_ref, q_buf, kv_buf, qt_ref, acc_ref, m_ref, mx_ref, peer_buf, count, sems = refs[
        inputs + 2 * ops :
    ]
    place, core, partner = info[0], info[2], info[5]
    rows = own_ref.shape[0] // 2
    cols = qt_ref.shape[1]
    heads = KV_HEADS // 2
    qb = cols // heads
    sub = qb // groups
    half = cols // 4
    limit = partner if foreign else place
    y_first = core == (0 if foreign else 1)
    n = len(SLOTS)
    if foreign:
        state = [pltpu.make_async_copy(refs[0], q_buf, sems.at[n + 1])]
    else:
        state = [
            pltpu.make_async_copy(refs[0], qt_ref, sems.at[n + 1]),
            pltpu.make_async_copy(refs[1], acc_ref.at[0], sems.at[n + 2]),
            pltpu.make_async_copy(refs[2], m_ref, sems.at[n + 3]),
        ]

    def behind(i):
        return limit - lax.bitwise_xor(place, info[TABLE + i])

    def start(src, slot):
        pltpu.make_async_copy(src, kv_buf.at[slot], sems.at[slot]).start()

    def wait(slot):
        pltpu.make_async_copy(own_ref, kv_buf.at[slot], sems.at[slot]).wait()

    for load in state:
        load.start()
    if foreign:

        @pl.when(place < limit)
        def _():
            start(own_ref, 0)

    for i in range(n):

        @pl.when(jnp.logical_and(behind(i) >= 0, core == i % 2))
        def _():
            start(mine[i // 2], i + 1)

        @pl.when(jnp.logical_and(behind(i) >= 0, core != i % 2))
        def _():
            start(other[i // 2], i + 1)

    for load in state:
        load.wait()
    count[0] = 0
    if foreign:
        for h in range(heads):
            load_queries(q_buf[:, :, h * DH : (h + 1) * DH].reshape(qb, DH), h, qt_ref)
        acc_ref[0] = jnp.zeros(acc_ref.shape[1:], F32)
        m_ref[...] = jnp.full_like(m_ref, NEG)

        wait(1)
        exact_block(kv_buf.at[1], 0, 1, groups, qt_ref, acc_ref.at[0], m_ref)

    def scores(kk, c0):
        return jnp.dot(kk, qt_ref[:, c0 : c0 + half], preferred_element_type=F32)

    def add_block(slot, _):
        i = jnp.maximum(slot - 1, 0)

        @pl.when(jnp.where(slot == 0, limit - place, behind(i)) > 0)
        def _():
            wait(slot)
            old = count[0] % 2
            new = 1 - old
            count[0] = count[0] + 1
            kk, vt = keys_of(kv_buf.at[slot]), values_of(kv_buf.at[slot])
            for c0 in range(0, cols, half):
                s = scores(kk, c0)
                mx_ref[:, c0 : c0 + half] = jnp.max(s.reshape(rows // 8, 8, half), axis=0)
                p = jnp.exp2(s - m_ref[0:1, c0 : c0 + half]).astype(BF)
                acc_ref[new, :, c0 : c0 + half] = acc_ref[old, :, c0 : c0 + half] + jnp.dot(
                    vt, p, preferred_element_type=F32
                )
            over = jnp.max(mx_ref[...] - m_ref[...])

            @pl.when(over > LIMIT)
            def _():
                for c0 in range(0, cols, half):
                    m = m_ref[0:1, c0 : c0 + half]
                    top = jnp.maximum(m, jnp.max(mx_ref[:, c0 : c0 + half], axis=0, keepdims=True))
                    p = jnp.exp2(scores(kk, c0) - top).astype(BF)
                    acc_ref[new, :, c0 : c0 + half] = acc_ref[old, :, c0 : c0 + half] * jnp.exp2(
                        m - top
                    ) + jnp.dot(vt, p, preferred_element_type=F32)
                    m_ref[:, c0 : c0 + half] = jnp.broadcast_to(top, (8, half))

        return 0

    lax.fori_loop(0, n + 1, add_block, 0)
    last = count[0] % 2
    for h in range(heads):
        o = acc_ref[last, :, h * qb : (h + 1) * qb]
        o = (o[0:DH] * (1.0 / o[DH : DH + 1])).astype(BF).T
        for g in range(groups):
            ry = (g // 4) ^ info[3]
            rz = (g // 2 % 2) ^ info[4]
            by_y = ((ry * 2 + rz) * 2 + g % 2) * sub
            by_z = (((ry // 2 * 2 + rz) * 2 + ry % 2) * 2 + g % 2) * sub
            piece = o[g * sub : (g + 1) * sub, :]
            here = pl.multiple_of(jnp.where(y_first, by_y, by_z), sub)
            there = pl.multiple_of(jnp.where(y_first, by_z, by_y), sub)
            o_ref[pl.ds(here, sub), h * DH : (h + 1) * DH] = piece
            peer_buf[pl.ds(there, sub), h * DH : (h + 1) * DH] = piece
    first_ref[...] = peer_buf[: qb // 2, :]
    second_ref[...] = peer_buf[qb // 2 :, :]


def attend(info, kv, state, q_shape, mine, other, n_y, n_seq):
    foreign = len(state) == 1
    groups, sub, width = q_shape
    qb = groups * sub
    cols = qb * width // DH
    any_space = pl.BlockSpec(memory_space=pl.ANY)
    out = pl.BlockSpec((qb, width), lambda i, info: (0, 0))
    part = pl.BlockSpec((qb // 2, width), lambda i, info: (0, 0))
    return pl.pallas_call(
        functools.partial(attend_kernel, foreign, groups, n_y, n_seq),
        grid_spec=pltpu.PrefetchScalarGridSpec(
            num_scalar_prefetch=1,
            grid=(1,),
            in_specs=[any_space] * (1 + len(state) + 2 * len(mine)),
            out_specs=[out, part, part],
            scratch_shapes=[
                pltpu.VMEM(q_shape, BF),
                pltpu.VMEM((len(SLOTS) + 1, *kv.shape), BF),
                pltpu.VMEM((2 * DH, cols), BF),
                pltpu.VMEM((2, DH + 16, cols), F32),
                pltpu.VMEM((8, cols), F32),
                pltpu.VMEM((8, cols), F32),
                pltpu.VMEM((qb, width), BF),
                pltpu.SMEM((1,), jnp.int32),
                pltpu.SemaphoreType.DMA((len(SLOTS) + 4,)),
            ],
        ),
        out_shape=[jax.ShapeDtypeStruct((rows, width), BF) for rows in (qb, qb // 2, qb // 2)],
        name="attend_foreign" if foreign else "attend_own",
        cost_estimate=pl.CostEstimate(
            flops=2 * cols * kv.shape[0] * 4 * DH, bytes_accessed=4 << 20, transcendentals=0
        ),
        compiler_params=PARAMS,
    )(info, kv, *state, *mine, *other)


def project(info, mine, other, w, w_other, parts, tile, sums=()):
    rows, width = mine.shape
    n = w.shape[1] // 2
    steps = n // tile

    def body(info, a, b0, b1, wa, wb, *refs):
        outs = refs[len(sums) :]
        b = jnp.concatenate([b0[...], b1[...]], axis=0)
        s = jnp.dot(a[...], wa[...], preferred_element_type=F32) + jnp.dot(
            b, wb[...], preferred_element_type=F32
        )
        part = s.shape[0] // parts
        for i, o in enumerate(outs[:parts]):
            o[...] = s[i * part : (i + 1) * part].astype(BF)
        if sums:
            p0, p2, g0, g1, g2 = [ref[...].astype(F32) for ref in refs[: len(sums)]]
            first = p0 + g0 + jnp.where(info[2] == 1, g1 + g2, 0.0)
            second = p2 + g1
            half = part // 2
            for o, x in zip(outs[parts:], (first[:half], first[half:], second[:half], second[half:]), strict=True):
                o[...] = x.astype(BF)

    whole = pl.BlockSpec((rows, width), lambda i, info: (0, 0))
    part = pl.BlockSpec((rows // 2, width), lambda i, info: (0, 0))
    weights = pl.BlockSpec((width, tile), lambda i, info: (0, info[2] * steps + i))

    def strip(r):
        return pl.BlockSpec((r, tile), lambda i, info: (0, i))

    sizes = [rows // parts] * parts + [rows // parts // 2] * (4 if sums else 0)
    return pl.pallas_call(
        body,
        grid_spec=pltpu.PrefetchScalarGridSpec(
            num_scalar_prefetch=1,
            grid=(steps,),
            in_specs=[whole, part, part, weights, weights] + [strip(x.shape[0]) for x in sums],
            out_specs=[strip(r) for r in sizes],
        ),
        out_shape=[jax.ShapeDtypeStruct((r, n), BF) for r in sizes],
        name="project_and_sum" if sums else "project",
        cost_estimate=pl.CostEstimate(flops=0, bytes_accessed=0, transcendentals=0),
        compiler_params=PARAMS,
    )(info, mine, *other, w, w_other, *sums)


def add(*terms):
    total = terms[0].astype(F32)
    for t in terms[1:]:
        total = total + t.astype(F32)
    return total.astype(BF)


def local(queries, keys, values, w_out):
    n_seq, n_head = lax.axis_size("seq"), lax.axis_size("head")
    rows, width = queries.shape
    cols = w_out.shape[1]
    place = lax.axis_index("seq")
    head = lax.axis_index("head")
    core, y, z = head % 2, head // 4, head // 2 % 2
    n_y = n_head // 4
    partner = n_seq - 1 - place
    info = jnp.stack([place, head * KV_HEADS // n_head, core, y, z, partner, *SLOTS]).astype(jnp.int32)

    def over_all(x, f):
        pairs = []
        for s in range(n_seq):
            for h in range(n_head):
                to = f(s, h // 4, h // 2 % 2, h % 2)
                if to is not None:
                    s2, y2, z2, c2 = to
                    pairs.append((s * n_head + h, s2 * n_head + (y2 % n_y) * 4 + z2 * 2 + c2))
        return lax.ppermute(x, ("seq", "head"), pairs)

    def swap_core(x):
        return over_all(x, lambda s, y, z, c: (s, y, z, 1 - c))

    def fetch(x, pair):
        def to(s, y, z, c):
            if pair[c] is None:
                return None
            t = s ^ pair[c]
            return (t, y, z, c) if s <= max(t, n_seq - 1 - t) else None

        return over_all(x, to)

    sub = rows // n_head // 2
    q4 = queries.reshape(n_head, 2, sub, width)
    w_other = swap_core(w_out)
    kv = prep(info, keys, values)
    mine = [fetch(kv, pair) for pair in FETCH]
    *state, q_away = own(q4, kv)
    other = [swap_core(after(x, state[2])) for x in mine]
    q_far = over_all(after(q_away, state[2], *mine), lambda s, y, z, c: (n_seq - 1 - s, y, z, c))

    def stage_one(parts, first):
        return [
            over_all(parts[1], lambda s, y, z, c: (s, y ^ 1, z, c) if c == first else (s, y, 1 - z, c)),
            over_all(parts[3], lambda s, y, z, c: (s, y ^ 3, z, c) if c == first else (s, y, 1 - z, c)),
            over_all(parts[2], lambda s, y, z, c: (s, y ^ 2, z, c) if c == first else None),
        ]

    def sum_one(parts, got):
        first = parts[0].astype(F32) + got[0].astype(F32)
        extra = got[1].astype(F32) + got[2].astype(F32)
        a = (first + jnp.where(core == 0, extra, 0.0)).astype(BF)
        b = add(parts[2], got[1])
        n = a.shape[0] // 2
        return a[:n], a[n:], b[:n], b[n:]

    def stage_two(total, first):
        return [
            over_all(total[1], lambda s, y, z, c: (s, y, 1 - z, c) if c == first else (s, y ^ 1, z, c)),
            over_all(total[3], lambda s, y, z, c: None if c == first else (s, y ^ 3, z, c)),
            over_all(total[2], lambda s, y, z, c: None if c == first else (s, y ^ 2, z, c)),
        ]

    def by_core(x, same):
        return jnp.where((core == 0) == same, x[0], x[1])

    half = (n_head, sub, width)
    near, *near_peer = attend(info, kv, state, half, mine, other, n_y, n_seq)
    near_far = [swap_core(x) for x in near_peer]
    parts_n = project(info, near, near_far, w_out, w_other, n_y, cols // 4)
    got_n = stage_one(parts_n, 1)
    far, *far_peer = attend(after(info, parts_n[0]), kv, [q_far], half, mine, other, n_y, n_seq)
    far_far = [swap_core(x) for x in far_peer]
    *parts_f, a0, a1, b0, b1 = project(
        info, far, far_far, w_out, w_other, n_y, cols // 4, (parts_n[0], parts_n[2], *got_n)
    )
    got_f = stage_one(parts_f, 0)
    total_f = sum_one(parts_f, got_f)
    got2_n = stage_two((a0, a1, after(b0, total_f[0]), b1), 1)
    got2_f = stage_two(total_f, 0)
    done_f = add(total_f[0], *got2_f).reshape(2, sub, cols // 2)
    done_n = add(after(a0, total_f[0]), *got2_n).reshape(2, sub, cols // 2)
    own_other = swap_core(by_core(done_n, False))
    home = over_all(by_core(done_f, True), lambda s, y, z, c: (n_seq - 1 - s, y, z, c))
    home_other = over_all(by_core(done_f, False), lambda s, y, z, c: (n_seq - 1 - s, y, z, 1 - c))
    here = jnp.concatenate([by_core(done_n, True), home], axis=0)
    there = jnp.concatenate([own_other, home_other], axis=0)
    left = jnp.where(core == 0, here, there)
    right = jnp.where(core == 0, there, here)
    return jnp.concatenate([left, right], axis=1)


def solution(mesh):
    placed = (P("seq", "head"), P("seq", None), P("seq", None), P("head", None))
    return jax.shard_map(
        local, mesh=mesh, in_specs=placed, out_specs=P(("seq", "head"), None), check_vma=False
    )
```

```python
import functools

import jax
import jax.numpy as jnp
from jax import lax
from jax.experimental import pallas as pl
from jax.experimental.pallas import tpu as pltpu
from jax.sharding import PartitionSpec as P

KV_HEADS = 8
DH = 128
LOG2E = 1.4426950408889634
NEG = -1e30
LIMIT = 60.0
BF = jnp.bfloat16
F32 = jnp.float32
PARAMS = pltpu.CompilerParams(vmem_limit_bytes=22 << 20)
FETCH = ((7, 3), (6, 2), (5, 1), (4, None))
SLOTS = [d for pair in FETCH for d in pair if d is not None]
TABLE = 6


def after(x, *deps):
    return lax.optimization_barrier((x, *deps))[0]


def prep_kernel(info, k_ref, v_ref, kv_ref):
    rows = k_ref.shape[0]
    kv_ref[0:rows, :] = k_ref[...]
    for t in range(rows // DH):
        kv_ref[rows + t * DH : rows + (t + 1) * DH, :] = v_ref[t * DH : (t + 1) * DH, :].T


def prep(info, keys, values):
    rows = keys.shape[0]
    col = pl.BlockSpec((rows, DH), lambda i, info: (0, info[1]))
    return pl.pallas_call(
        prep_kernel,
        grid_spec=pltpu.PrefetchScalarGridSpec(
            num_scalar_prefetch=1,
            grid=(1,),
            in_specs=[col, col],
            out_specs=pl.BlockSpec((2 * rows, DH), lambda i, info: (0, 0)),
        ),
        out_shape=jax.ShapeDtypeStruct((2 * rows, DH), BF),
        name="prep",
        compiler_params=pltpu.CompilerParams(vmem_limit_bytes=64 << 20),
    )(info, keys, values)


def keys_of(kv):
    k = kv[0 : kv.shape[0] // 2, :]
    return jnp.concatenate([k, k], axis=1)


def values_of(kv):
    rows = kv.shape[0] // 2
    tiles = [kv[rows + t * DH : rows + (t + 1) * DH, :] for t in range(rows // DH)]
    return jnp.concatenate([jnp.concatenate(tiles, axis=1), jnp.ones((16, rows), BF)], axis=0)


def load_queries(q, h, qt_ref):
    heads = KV_HEADS // 2
    scaled = q.astype(F32) * (DH**-0.5 * LOG2E)
    high = scaled.astype(BF)
    low = (scaled - high.astype(F32)).astype(BF)
    high, low = high.T, low.T
    for seg in range(q.shape[0] // DH):
        c = slice((seg * heads + h) * DH, (seg * heads + h + 1) * DH)
        rows = slice(seg * DH, (seg + 1) * DH)
        qt_ref[0:DH, c] = high[:, rows]
        qt_ref[DH : 2 * DH, c] = low[:, rows]


def diagonal_block(kv, second, groups, qt_ref, acc, m_ref):
    rows = kv.shape[0] // 2
    cols = qt_ref.shape[1]
    width = KV_HEADS // 2 * DH
    segs = cols // width
    quarter = rows // segs
    sub = segs * DH // groups
    kk, vt = keys_of(kv), values_of(kv)
    j = lax.broadcasted_iota(jnp.int32, (quarter, width), 1) % DH
    pos = j // sub * (rows // groups) + second * sub + j % sub
    allowed = lax.broadcasted_iota(jnp.int32, (quarter, width), 0) <= pos
    for seg in range(segs):
        c = slice(seg * width, (seg + 1) * width)
        n = (seg + 1) * quarter
        s = jnp.dot(kk[:n], qt_ref[:, c], preferred_element_type=F32)
        last = jnp.where(allowed, s[n - quarter :], NEG)
        s = last if seg == 0 else jnp.concatenate([s[: n - quarter], last], axis=0)
        m = jnp.max(s, axis=0, keepdims=True)
        acc[:, c] = jnp.dot(vt[:, :n], jnp.exp2(s - m).astype(BF), preferred_element_type=F32)
        m_ref[:, c] = jnp.broadcast_to(m, (8, width))


def own_kernel(groups, q_ref, away_ref, kv_ref, qt_ref, acc_ref, m_ref, send_ref):
    send_ref[...] = away_ref[:, 0]
    _, _, sub, width = q_ref.shape
    for h in range(width // DH):
        load_queries(q_ref[:, 0, :, h * DH : (h + 1) * DH].reshape(groups * sub, DH), h, qt_ref)
    diagonal_block(kv_ref, 0, groups, qt_ref, acc_ref, m_ref)


def own(q4, kv):
    groups, _, sub, width = q4.shape
    cols = groups * sub * width // DH
    return pl.pallas_call(
        functools.partial(own_kernel, groups),
        grid=(1,),
        in_specs=[
            pl.BlockSpec((groups, 1, sub, width), lambda i: (0, 0, 0, 0)),
            pl.BlockSpec((groups, 1, sub, width), lambda i: (0, 1, 0, 0)),
            pl.BlockSpec(kv.shape, lambda i: (0, 0)),
        ],
        out_specs=[
            pl.BlockSpec((2 * DH, cols), lambda i: (0, 0)),
            pl.BlockSpec((DH + 16, cols), lambda i: (0, 0)),
            pl.BlockSpec((8, cols), lambda i: (0, 0)),
            pl.BlockSpec((groups, sub, width), lambda i: (0, 0, 0)),
        ],
        out_shape=[
            jax.ShapeDtypeStruct((2 * DH, cols), BF),
            jax.ShapeDtypeStruct((DH + 16, cols), F32),
            jax.ShapeDtypeStruct((8, cols), F32),
            jax.ShapeDtypeStruct((groups, sub, width), BF),
        ],
        name="own",
        cost_estimate=pl.CostEstimate(
            flops=2 * cols * kv.shape[0] * 2 * DH, bytes_accessed=8 << 20, transcendentals=0
        ),
        compiler_params=PARAMS,
    )(q4, q4, kv)


def attend_kernel(foreign, groups, n_y, n_seq, info, own_ref, *refs):
    ops = n_seq // 2
    inputs = 1 if foreign else 3
    mine, other = refs[inputs : inputs + ops], refs[inputs + ops : inputs + 2 * ops]
    o_ref, first_ref, second_ref, q_buf, kv_buf, qt_ref, acc_ref, m_ref, mx_ref, peer_buf, count, sems = refs[
        inputs + 2 * ops :
    ]
    place, core, partner = info[0], info[2], info[5]
    rows = own_ref.shape[0] // 2
    cols = qt_ref.shape[1]
    heads = KV_HEADS // 2
    qb = cols // heads
    sub = qb // groups
    half = cols // 4
    limit = partner if foreign else place
    y_first = core == (0 if foreign else 1)
    n = len(SLOTS)
    if foreign:
        state = [pltpu.make_async_copy(refs[0], q_buf, sems.at[n + 1])]
    else:
        state = [
            pltpu.make_async_copy(refs[0], qt_ref, sems.at[n + 1]),
            pltpu.make_async_copy(refs[1], acc_ref.at[0], sems.at[n + 2]),
            pltpu.make_async_copy(refs[2], m_ref, sems.at[n + 3]),
        ]

    def behind(i):
        return limit - lax.bitwise_xor(place, info[TABLE + i])

    def start(src, slot):
        pltpu.make_async_copy(src, kv_buf.at[slot], sems.at[slot]).start()

    def wait(slot):
        pltpu.make_async_copy(own_ref, kv_buf.at[slot], sems.at[slot]).wait()

    for load in state:
        load.start()
    if foreign:

        @pl.when(place < limit)
        def _():
            start(own_ref, 0)

    for i in range(n):

        @pl.when(jnp.logical_and(behind(i) >= 0, core == i % 2))
        def _():
            start(mine[i // 2], i + 1)

        @pl.when(jnp.logical_and(behind(i) >= 0, core != i % 2))
        def _():
            start(other[i // 2], i + 1)

    for load in state:
        load.wait()
    count[0] = 0
    if foreign:
        for h in range(heads):
            load_queries(q_buf[:, :, h * DH : (h + 1) * DH].reshape(qb, DH), h, qt_ref)
        wait(1)
        diagonal_block(kv_buf.at[1], 1, groups, qt_ref, acc_ref.at[0], m_ref)

    def scores(kk, c0):
        return jnp.dot(kk, qt_ref[:, c0 : c0 + half], preferred_element_type=F32)

    def add_block(slot, _):
        i = jnp.maximum(slot - 1, 0)

        @pl.when(jnp.where(slot == 0, limit - place, behind(i)) > 0)
        def _():
            wait(slot)
            old = count[0] % 2
            new = 1 - old
            count[0] = count[0] + 1
            kk, vt = keys_of(kv_buf.at[slot]), values_of(kv_buf.at[slot])
            for c0 in range(0, cols, half):
                s = scores(kk, c0)
                mx_ref[:, c0 : c0 + half] = jnp.max(s.reshape(rows // 8, 8, half), axis=0)
                p = jnp.exp2(s - m_ref[0:1, c0 : c0 + half]).astype(BF)
                acc_ref[new, :, c0 : c0 + half] = acc_ref[old, :, c0 : c0 + half] + jnp.dot(
                    vt, p, preferred_element_type=F32
                )
            over = jnp.max(mx_ref[...] - m_ref[...])

            @pl.when(over > LIMIT)
            def _():
                for c0 in range(0, cols, half):
                    m = m_ref[0:1, c0 : c0 + half]
                    top = jnp.maximum(m, jnp.max(mx_ref[:, c0 : c0 + half], axis=0, keepdims=True))
                    p = jnp.exp2(scores(kk, c0) - top).astype(BF)
                    acc_ref[new, :, c0 : c0 + half] = acc_ref[old, :, c0 : c0 + half] * jnp.exp2(
                        m - top
                    ) + jnp.dot(vt, p, preferred_element_type=F32)
                    m_ref[:, c0 : c0 + half] = jnp.broadcast_to(top, (8, half))

        return 0

    lax.fori_loop(0, n + 1, add_block, 0)
    last = count[0] % 2
    per_seg = groups * DH // qb
    for seg in range(qb // DH):
        for h in range(heads):
            o = acc_ref[last, :, (seg * heads + h) * DH : (seg * heads + h + 1) * DH]
            o = (o[0:DH] * (1.0 / o[DH : DH + 1])).astype(BF).T
            for k in range(per_seg):
                g = seg * per_seg + k
                ry = (g // 4) ^ info[3]
                rz = (g // 2 % 2) ^ info[4]
                by_y = ((ry * 2 + rz) * 2 + g % 2) * sub
                by_z = (((ry // 2 * 2 + rz) * 2 + ry % 2) * 2 + g % 2) * sub
                piece = o[k * sub : (k + 1) * sub, :]
                here = pl.multiple_of(jnp.where(y_first, by_y, by_z), sub)
                there = pl.multiple_of(jnp.where(y_first, by_z, by_y), sub)
                o_ref[pl.ds(here, sub), h * DH : (h + 1) * DH] = piece
                peer_buf[pl.ds(there, sub), h * DH : (h + 1) * DH] = piece
    first_ref[...] = peer_buf[: qb // 2, :]
    second_ref[...] = peer_buf[qb // 2 :, :]


def attend(info, kv, state, q_shape, mine, other, n_y, n_seq):
    foreign = len(state) == 1
    groups, sub, width = q_shape
    qb = groups * sub
    cols = qb * width // DH
    any_space = pl.BlockSpec(memory_space=pl.ANY)
    out = pl.BlockSpec((qb, width), lambda i, info: (0, 0))
    part = pl.BlockSpec((qb // 2, width), lambda i, info: (0, 0))
    return pl.pallas_call(
        functools.partial(attend_kernel, foreign, groups, n_y, n_seq),
        grid_spec=pltpu.PrefetchScalarGridSpec(
            num_scalar_prefetch=1,
            grid=(1,),
            in_specs=[any_space] * (1 + len(state) + 2 * len(mine)),
            out_specs=[out, part, part],
            scratch_shapes=[
                pltpu.VMEM(q_shape, BF),
                pltpu.VMEM((len(SLOTS) + 1, *kv.shape), BF),
                pltpu.VMEM((2 * DH, cols), BF),
                pltpu.VMEM((2, DH + 16, cols), F32),
                pltpu.VMEM((8, cols), F32),
                pltpu.VMEM((8, cols), F32),
                pltpu.VMEM((qb, width), BF),
                pltpu.SMEM((1,), jnp.int32),
                pltpu.SemaphoreType.DMA((len(SLOTS) + 4,)),
            ],
        ),
        out_shape=[jax.ShapeDtypeStruct((rows, width), BF) for rows in (qb, qb // 2, qb // 2)],
        name="attend_foreign" if foreign else "attend_own",
        cost_estimate=pl.CostEstimate(
            flops=2 * cols * kv.shape[0] * 4 * DH, bytes_accessed=4 << 20, transcendentals=0
        ),
        compiler_params=PARAMS,
    )(info, kv, *state, *mine, *other)


def project(info, mine, other, w, w_other, parts, tile, sums=()):
    rows, width = mine.shape
    n = w.shape[1] // 2
    steps = n // tile

    def body(info, a, b0, b1, wa, wb, *refs):
        outs = refs[len(sums) :]
        b = jnp.concatenate([b0[...], b1[...]], axis=0)
        s = jnp.dot(a[...], wa[...], preferred_element_type=F32) + jnp.dot(
            b, wb[...], preferred_element_type=F32
        )
        part = s.shape[0] // parts
        for i, o in enumerate(outs[:parts]):
            o[...] = s[i * part : (i + 1) * part].astype(BF)
        if sums:
            p0, p2, g0, g1, g2 = [ref[...].astype(F32) for ref in refs[: len(sums)]]
            first = p0 + g0 + jnp.where(info[2] == 1, g1 + g2, 0.0)
            second = p2 + g1
            half = part // 2
            for o, x in zip(outs[parts:], (first[:half], first[half:], second[:half], second[half:]), strict=True):
                o[...] = x.astype(BF)

    whole = pl.BlockSpec((rows, width), lambda i, info: (0, 0))
    part = pl.BlockSpec((rows // 2, width), lambda i, info: (0, 0))
    weights = pl.BlockSpec((width, tile), lambda i, info: (0, info[2] * steps + i))

    def strip(r):
        return pl.BlockSpec((r, tile), lambda i, info: (0, i))

    sizes = [rows // parts] * parts + [rows // parts // 2] * (4 if sums else 0)
    return pl.pallas_call(
        body,
        grid_spec=pltpu.PrefetchScalarGridSpec(
            num_scalar_prefetch=1,
            grid=(steps,),
            in_specs=[whole, part, part, weights, weights] + [strip(x.shape[0]) for x in sums],
            out_specs=[strip(r) for r in sizes],
        ),
        out_shape=[jax.ShapeDtypeStruct((r, n), BF) for r in sizes],
        name="project_and_sum" if sums else "project",
        cost_estimate=pl.CostEstimate(flops=0, bytes_accessed=0, transcendentals=0),
        compiler_params=PARAMS,
    )(info, mine, *other, w, w_other, *sums)


def add(*terms):
    total = terms[0].astype(F32)
    for t in terms[1:]:
        total = total + t.astype(F32)
    return total.astype(BF)


def local(queries, keys, values, w_out):
    n_seq, n_head = lax.axis_size("seq"), lax.axis_size("head")
    rows, width = queries.shape
    cols = w_out.shape[1]
    place = lax.axis_index("seq")
    head = lax.axis_index("head")
    core, y, z = head % 2, head // 4, head // 2 % 2
    n_y = n_head // 4
    partner = n_seq - 1 - place
    info = jnp.stack([place, head * KV_HEADS // n_head, core, y, z, partner, *SLOTS]).astype(jnp.int32)

    def over_all(x, f):
        pairs = []
        for s in range(n_seq):
            for h in range(n_head):
                to = f(s, h // 4, h // 2 % 2, h % 2)
                if to is not None:
                    s2, y2, z2, c2 = to
                    pairs.append((s * n_head + h, s2 * n_head + (y2 % n_y) * 4 + z2 * 2 + c2))
        return lax.ppermute(x, ("seq", "head"), pairs)

    def swap_core(x):
        return over_all(x, lambda s, y, z, c: (s, y, z, 1 - c))

    def fetch(x, pair):
        def to(s, y, z, c):
            if pair[c] is None:
                return None
            t = s ^ pair[c]
            return (t, y, z, c) if s <= max(t, n_seq - 1 - t) else None

        return over_all(x, to)

    sub = rows // n_head // 2
    q4 = queries.reshape(n_head, 2, sub, width)
    w_other = swap_core(w_out)
    kv = prep(info, keys, values)
    mine = [fetch(kv, pair) for pair in FETCH]
    *state, q_away = own(q4, kv)
    other = [swap_core(after(x, state[2])) for x in mine]
    q_far = over_all(after(q_away, state[2], *mine), lambda s, y, z, c: (n_seq - 1 - s, y, z, c))

    def stage_one(parts, first):
        return [
            over_all(parts[1], lambda s, y, z, c: (s, y ^ 1, z, c) if c == first else (s, y, 1 - z, c)),
            over_all(parts[3], lambda s, y, z, c: (s, y ^ 3, z, c) if c == first else (s, y, 1 - z, c)),
            over_all(parts[2], lambda s, y, z, c: (s, y ^ 2, z, c) if c == first else None),
        ]

    def sum_one(parts, got):
        first = parts[0].astype(F32) + got[0].astype(F32)
        extra = got[1].astype(F32) + got[2].astype(F32)
        a = (first + jnp.where(core == 0, extra, 0.0)).astype(BF)
        b = add(parts[2], got[1])
        n = a.shape[0] // 2
        return a[:n], a[n:], b[:n], b[n:]

    def stage_two(total, first):
        return [
            over_all(total[1], lambda s, y, z, c: (s, y, 1 - z, c) if c == first else (s, y ^ 1, z, c)),
            over_all(total[3], lambda s, y, z, c: None if c == first else (s, y ^ 3, z, c)),
            over_all(total[2], lambda s, y, z, c: None if c == first else (s, y ^ 2, z, c)),
        ]

    def by_core(x, same):
        return jnp.where((core == 0) == same, x[0], x[1])

    half = (n_head, sub, width)
    near, *near_peer = attend(info, kv, state, half, mine, other, n_y, n_seq)
    near_far = [swap_core(x) for x in near_peer]
    parts_n = project(info, near, near_far, w_out, w_other, n_y, cols // 4)
    got_n = stage_one(parts_n, 1)
    far, *far_peer = attend(after(info, parts_n[0]), kv, [q_far], half, mine, other, n_y, n_seq)
    far_far = [swap_core(x) for x in far_peer]
    *parts_f, a0, a1, b0, b1 = project(
        info, far, far_far, w_out, w_other, n_y, cols // 4, (parts_n[0], parts_n[2], *got_n)
    )
    got_f = stage_one(parts_f, 0)
    total_f = sum_one(parts_f, got_f)
    got2_n = stage_two((a0, a1, after(b0, total_f[0]), b1), 1)
    got2_f = stage_two(total_f, 0)
    done_f = add(total_f[0], *got2_f).reshape(2, sub, cols // 2)
    done_n = add(after(a0, by_core(done_f, True)), *got2_n).reshape(2, sub, cols // 2)
    own_other = swap_core(after(by_core(done_n, False), done_f))
    home = over_all(by_core(done_f, True), lambda s, y, z, c: (n_seq - 1 - s, y, z, c))
    home_other = over_all(by_core(done_f, False), lambda s, y, z, c: (n_seq - 1 - s, y, z, 1 - c))
    here = jnp.concatenate([by_core(done_n, True), home], axis=0)
    there = jnp.concatenate([own_other, home_other], axis=0)
    left = jnp.where(core == 0, here, there)
    right = jnp.where(core == 0, there, here)
    return jnp.concatenate([left, right], axis=1)


def solution(mesh):
    placed = (P("seq", "head"), P("seq", None), P("seq", None), P("head", None))
    return jax.shard_map(
        local, mesh=mesh, in_specs=placed, out_specs=P(("seq", "head"), None), check_vma=False
    )
```

```python
import functools

import jax
import jax.numpy as jnp
from jax import lax
from jax.experimental import pallas as pl
from jax.experimental.pallas import tpu as pltpu
from jax.sharding import PartitionSpec as P

KV_HEADS = 8
DH = 128
LOG2E = 1.4426950408889634
NEG = -1e30
LIMIT = 60.0
BF = jnp.bfloat16
F32 = jnp.float32
PARAMS = pltpu.CompilerParams(vmem_limit_bytes=22 << 20)
FETCH = ((7, 3), (6, 2), (5, 1), (4, None))
SLOTS = [d for pair in FETCH for d in pair if d is not None]
TABLE = 6


def after(x, *deps):
    return lax.optimization_barrier((x, *deps))[0]


def prep_kernel(info, k_ref, v_ref, kv_ref):
    rows = k_ref.shape[0]
    kv_ref[0:rows, :] = k_ref[...]
    for t in range(rows // DH):
        kv_ref[rows + t * DH : rows + (t + 1) * DH, :] = v_ref[t * DH : (t + 1) * DH, :].T


def prep(info, keys, values):
    rows = keys.shape[0]
    col = pl.BlockSpec((rows, DH), lambda i, info: (0, info[1]))
    return pl.pallas_call(
        prep_kernel,
        grid_spec=pltpu.PrefetchScalarGridSpec(
            num_scalar_prefetch=1,
            grid=(1,),
            in_specs=[col, col],
            out_specs=pl.BlockSpec((2 * rows, DH), lambda i, info: (0, 0)),
        ),
        out_shape=jax.ShapeDtypeStruct((2 * rows, DH), BF),
        name="prep",
        compiler_params=pltpu.CompilerParams(vmem_limit_bytes=64 << 20),
    )(info, keys, values)


def keys_of(kv):
    k = kv[0 : kv.shape[0] // 2, :]
    return jnp.concatenate([k, k], axis=1)


def values_of(kv):
    rows = kv.shape[0] // 2
    tiles = [kv[rows + t * DH : rows + (t + 1) * DH, :] for t in range(rows // DH)]
    return jnp.concatenate([jnp.concatenate(tiles, axis=1), jnp.ones((16, rows), BF)], axis=0)


def load_queries(q, h, qt_ref):
    heads = KV_HEADS // 2
    scaled = q.astype(F32) * (DH**-0.5 * LOG2E)
    high = scaled.astype(BF)
    low = (scaled - high.astype(F32)).astype(BF)
    high, low = high.T, low.T
    for seg in range(q.shape[0] // DH):
        c = slice((seg * heads + h) * DH, (seg * heads + h + 1) * DH)
        rows = slice(seg * DH, (seg + 1) * DH)
        qt_ref[0:DH, c] = high[:, rows]
        qt_ref[DH : 2 * DH, c] = low[:, rows]


def diagonal_block(kv, second, groups, qt_ref, acc, m_ref):
    rows = kv.shape[0] // 2
    cols = qt_ref.shape[1]
    width = KV_HEADS // 2 * DH
    segs = cols // width
    quarter = rows // segs
    sub = segs * DH // groups
    kk, vt = keys_of(kv), values_of(kv)
    j = lax.broadcasted_iota(jnp.int32, (quarter, width), 1) % DH
    pos = j // sub * (rows // groups) + second * sub + j % sub
    allowed = lax.broadcasted_iota(jnp.int32, (quarter, width), 0) <= pos
    for seg in range(segs):
        c = slice(seg * width, (seg + 1) * width)
        n = (seg + 1) * quarter
        s = jnp.dot(kk[:n], qt_ref[:, c], preferred_element_type=F32)
        last = jnp.where(allowed, s[n - quarter :], NEG)
        s = last if seg == 0 else jnp.concatenate([s[: n - quarter], last], axis=0)
        m = jnp.max(s, axis=0, keepdims=True)
        acc[:, c] = jnp.dot(vt[:, :n], jnp.exp2(s - m).astype(BF), preferred_element_type=F32)
        m_ref[:, c] = jnp.broadcast_to(m, (8, width))


def own_kernel(groups, q_ref, away_ref, kv_ref, qt_ref, acc_ref, m_ref, send_ref):
    send_ref[...] = away_ref[:, 0]
    _, _, sub, width = q_ref.shape
    for h in range(width // DH):
        load_queries(q_ref[:, 0, :, h * DH : (h + 1) * DH].reshape(groups * sub, DH), h, qt_ref)
    diagonal_block(kv_ref, 0, groups, qt_ref, acc_ref, m_ref)


def own(q4, kv):
    groups, _, sub, width = q4.shape
    cols = groups * sub * width // DH
    return pl.pallas_call(
        functools.partial(own_kernel, groups),
        grid=(1,),
        in_specs=[
            pl.BlockSpec((groups, 1, sub, width), lambda i: (0, 0, 0, 0)),
            pl.BlockSpec((groups, 1, sub, width), lambda i: (0, 1, 0, 0)),
            pl.BlockSpec(kv.shape, lambda i: (0, 0)),
        ],
        out_specs=[
            pl.BlockSpec((2 * DH, cols), lambda i: (0, 0)),
            pl.BlockSpec((DH + 16, cols), lambda i: (0, 0)),
            pl.BlockSpec((8, cols), lambda i: (0, 0)),
            pl.BlockSpec((groups, sub, width), lambda i: (0, 0, 0)),
        ],
        out_shape=[
            jax.ShapeDtypeStruct((2 * DH, cols), BF),
            jax.ShapeDtypeStruct((DH + 16, cols), F32),
            jax.ShapeDtypeStruct((8, cols), F32),
            jax.ShapeDtypeStruct((groups, sub, width), BF),
        ],
        name="own",
        cost_estimate=pl.CostEstimate(
            flops=2 * cols * kv.shape[0] * 2 * DH, bytes_accessed=8 << 20, transcendentals=0
        ),
        compiler_params=PARAMS,
    )(q4, q4, kv)


def attend_kernel(foreign, groups, n_y, n_seq, info, own_ref, *refs):
    ops = n_seq // 2
    inputs = 1 if foreign else 3
    mine, other = refs[inputs : inputs + ops], refs[inputs + ops : inputs + 2 * ops]
    o_ref, first_ref, second_ref, q_buf, kv_buf, qt_ref, acc_ref, m_ref, mx_ref, peer_buf, count, sems = refs[
        inputs + 2 * ops :
    ]
    place, core, partner = info[0], info[2], info[5]
    rows = own_ref.shape[0] // 2
    cols = qt_ref.shape[1]
    heads = KV_HEADS // 2
    qb = cols // heads
    sub = qb // groups
    half = cols // 4
    limit = partner if foreign else place
    y_first = core == (0 if foreign else 1)
    n = len(SLOTS)
    if foreign:
        state = [pltpu.make_async_copy(refs[0], q_buf, sems.at[n + 1])]
    else:
        state = [
            pltpu.make_async_copy(refs[0], qt_ref, sems.at[n + 1]),
            pltpu.make_async_copy(refs[1], acc_ref.at[0], sems.at[n + 2]),
            pltpu.make_async_copy(refs[2], m_ref, sems.at[n + 3]),
        ]

    def behind(i):
        return limit - lax.bitwise_xor(place, info[TABLE + i])

    def start(src, slot):
        pltpu.make_async_copy(src, kv_buf.at[slot], sems.at[slot]).start()

    def wait(slot):
        pltpu.make_async_copy(own_ref, kv_buf.at[slot], sems.at[slot]).wait()

    for load in state:
        load.start()
    if foreign:

        @pl.when(place < limit)
        def _():
            start(own_ref, 0)

    for i in range(n):

        @pl.when(jnp.logical_and(behind(i) >= 0, core == i % 2))
        def _():
            start(mine[i // 2], i + 1)

        @pl.when(jnp.logical_and(behind(i) >= 0, core != i % 2))
        def _():
            start(other[i // 2], i + 1)

    for load in state:
        load.wait()
    count[0] = 0
    if foreign:
        for h in range(heads):
            load_queries(q_buf[:, :, h * DH : (h + 1) * DH].reshape(qb, DH), h, qt_ref)
        wait(1)
        diagonal_block(kv_buf.at[1], 1, groups, qt_ref, acc_ref.at[0], m_ref)

    def scores(kk, c0):
        return jnp.dot(kk, qt_ref[:, c0 : c0 + half], preferred_element_type=F32)

    def add_block(slot, _):
        i = jnp.maximum(slot - 1, 0)

        @pl.when(jnp.where(slot == 0, limit - place, behind(i)) > 0)
        def _():
            wait(slot)
            old = count[0] % 2
            new = 1 - old
            count[0] = count[0] + 1
            kk, vt = keys_of(kv_buf.at[slot]), values_of(kv_buf.at[slot])
            for c0 in range(0, cols, half):
                s = scores(kk, c0)
                mx_ref[:, c0 : c0 + half] = jnp.max(s.reshape(rows // 8, 8, half), axis=0)
                p = jnp.exp2(s - m_ref[0:1, c0 : c0 + half]).astype(BF)
                acc_ref[new, :, c0 : c0 + half] = acc_ref[old, :, c0 : c0 + half] + jnp.dot(
                    vt, p, preferred_element_type=F32
                )
            over = jnp.max(mx_ref[...] - m_ref[...])

            @pl.when(over > LIMIT)
            def _():
                for c0 in range(0, cols, half):
                    m = m_ref[0:1, c0 : c0 + half]
                    top = jnp.maximum(m, jnp.max(mx_ref[:, c0 : c0 + half], axis=0, keepdims=True))
                    p = jnp.exp2(scores(kk, c0) - top).astype(BF)
                    acc_ref[new, :, c0 : c0 + half] = acc_ref[old, :, c0 : c0 + half] * jnp.exp2(
                        m - top
                    ) + jnp.dot(vt, p, preferred_element_type=F32)
                    m_ref[:, c0 : c0 + half] = jnp.broadcast_to(top, (8, half))

        return 0

    lax.fori_loop(0, n + 1, add_block, 0)
    last = count[0] % 2
    per_seg = groups * DH // qb
    for seg in range(qb // DH):
        for h in range(heads):
            o = acc_ref[last, :, (seg * heads + h) * DH : (seg * heads + h + 1) * DH]
            o = (o[0:DH] * (1.0 / o[DH : DH + 1])).astype(BF).T
            for k in range(per_seg):
                g = seg * per_seg + k
                ry = (g // 4) ^ info[3]
                rz = (g // 2 % 2) ^ info[4]
                by_y = ((ry * 2 + rz) * 2 + g % 2) * sub
                by_z = (((ry // 2 * 2 + rz) * 2 + ry % 2) * 2 + g % 2) * sub
                piece = o[k * sub : (k + 1) * sub, :]
                here = pl.multiple_of(jnp.where(y_first, by_y, by_z), sub)
                there = pl.multiple_of(jnp.where(y_first, by_z, by_y), sub)
                o_ref[pl.ds(here, sub), h * DH : (h + 1) * DH] = piece
                peer_buf[pl.ds(there, sub), h * DH : (h + 1) * DH] = piece
    first_ref[...] = peer_buf[: qb // 2, :]
    second_ref[...] = peer_buf[qb // 2 :, :]


def attend(info, kv, state, q_shape, mine, other, n_y, n_seq):
    foreign = len(state) == 1
    groups, sub, width = q_shape
    qb = groups * sub
    cols = qb * width // DH
    any_space = pl.BlockSpec(memory_space=pl.ANY)
    out = pl.BlockSpec((qb, width), lambda i, info: (0, 0))
    part = pl.BlockSpec((qb // 2, width), lambda i, info: (0, 0))
    return pl.pallas_call(
        functools.partial(attend_kernel, foreign, groups, n_y, n_seq),
        grid_spec=pltpu.PrefetchScalarGridSpec(
            num_scalar_prefetch=1,
            grid=(1,),
            in_specs=[any_space] * (1 + len(state) + 2 * len(mine)),
            out_specs=[out, part, part],
            scratch_shapes=[
                pltpu.VMEM(q_shape, BF),
                pltpu.VMEM((len(SLOTS) + 1, *kv.shape), BF),
                pltpu.VMEM((2 * DH, cols), BF),
                pltpu.VMEM((2, DH + 16, cols), F32),
                pltpu.VMEM((8, cols), F32),
                pltpu.VMEM((8, cols), F32),
                pltpu.VMEM((qb, width), BF),
                pltpu.SMEM((1,), jnp.int32),
                pltpu.SemaphoreType.DMA((len(SLOTS) + 4,)),
            ],
        ),
        out_shape=[jax.ShapeDtypeStruct((rows, width), BF) for rows in (qb, qb // 2, qb // 2)],
        name="attend_foreign" if foreign else "attend_own",
        cost_estimate=pl.CostEstimate(
            flops=2 * cols * kv.shape[0] * 4 * DH, bytes_accessed=4 << 20, transcendentals=0
        ),
        compiler_params=PARAMS,
    )(info, kv, *state, *mine, *other)


def project(info, mine, other, w, w_other, parts, tile):
    rows, width = mine.shape
    n = w.shape[1] // 2
    steps = n // tile

    def body(info, a, b0, b1, wa, wb, *outs):
        b = jnp.concatenate([b0[...], b1[...]], axis=0)
        s = jnp.dot(a[...], wa[...], preferred_element_type=F32) + jnp.dot(
            b, wb[...], preferred_element_type=F32
        )
        part = s.shape[0] // parts
        for i, o in enumerate(outs):
            o[...] = s[i * part : (i + 1) * part].astype(BF)

    whole = pl.BlockSpec((rows, width), lambda i, info: (0, 0))
    half = pl.BlockSpec((rows // 2, width), lambda i, info: (0, 0))
    weights = pl.BlockSpec((width, tile), lambda i, info: (0, info[2] * steps + i))
    return pl.pallas_call(
        body,
        grid_spec=pltpu.PrefetchScalarGridSpec(
            num_scalar_prefetch=1,
            grid=(steps,),
            in_specs=[whole, half, half, weights, weights],
            out_specs=[pl.BlockSpec((rows // parts, tile), lambda i, info: (0, i))] * parts,
        ),
        out_shape=[jax.ShapeDtypeStruct((rows // parts, n), BF)] * parts,
        name="project",
        cost_estimate=pl.CostEstimate(flops=0, bytes_accessed=0, transcendentals=0),
        compiler_params=PARAMS,
    )(info, mine, *other, w, w_other)


def add(*terms):
    total = terms[0].astype(F32)
    for t in terms[1:]:
        total = total + t.astype(F32)
    return total.astype(BF)


def local(queries, keys, values, w_out):
    n_seq, n_head = lax.axis_size("seq"), lax.axis_size("head")
    rows, width = queries.shape
    cols = w_out.shape[1]
    place = lax.axis_index("seq")
    head = lax.axis_index("head")
    core, y, z = head % 2, head // 4, head // 2 % 2
    n_y = n_head // 4
    partner = n_seq - 1 - place
    info = jnp.stack([place, head * KV_HEADS // n_head, core, y, z, partner, *SLOTS]).astype(jnp.int32)

    def over_all(x, f):
        pairs = []
        for s in range(n_seq):
            for h in range(n_head):
                to = f(s, h // 4, h // 2 % 2, h % 2)
                if to is not None:
                    s2, y2, z2, c2 = to
                    pairs.append((s * n_head + h, s2 * n_head + (y2 % n_y) * 4 + z2 * 2 + c2))
        return lax.ppermute(x, ("seq", "head"), pairs)

    def swap_core(x):
        return over_all(x, lambda s, y, z, c: (s, y, z, 1 - c))

    def fetch(x, pair):
        def to(s, y, z, c):
            if pair[c] is None:
                return None
            t = s ^ pair[c]
            return (t, y, z, c) if s <= max(t, n_seq - 1 - t) else None

        return over_all(x, to)

    sub = rows // n_head // 2
    q4 = queries.reshape(n_head, 2, sub, width)
    w_other = swap_core(w_out)
    kv = prep(info, keys, values)
    mine = [fetch(kv, pair) for pair in FETCH]
    *state, q_away = own(q4, kv)
    other = [swap_core(after(x, state[2])) for x in mine]
    q_far = over_all(after(q_away, state[2], *mine), lambda s, y, z, c: (n_seq - 1 - s, y, z, c))

    def stage_one(parts, first):
        return [
            over_all(parts[1], lambda s, y, z, c: (s, y ^ 1, z, c) if c == first else (s, y, 1 - z, c)),
            over_all(parts[3], lambda s, y, z, c: (s, y ^ 3, z, c) if c == first else (s, y, 1 - z, c)),
            over_all(parts[2], lambda s, y, z, c: (s, y ^ 2, z, c) if c == first else None),
        ]

    def sum_one(parts, got, first):
        along_y = parts[0].astype(F32) + got[0].astype(F32)
        extra = got[1].astype(F32) + got[2].astype(F32)
        a = (along_y + jnp.where(core == first, extra, 0.0)).astype(BF)
        b = add(parts[2], got[1])
        n = a.shape[0] // 2
        return a[:n], a[n:], b[:n], b[n:]

    def stage_two(total, first):
        return [
            over_all(total[1], lambda s, y, z, c: (s, y, 1 - z, c) if c == first else (s, y ^ 1, z, c)),
            over_all(total[3], lambda s, y, z, c: None if c == first else (s, y ^ 3, z, c)),
            over_all(total[2], lambda s, y, z, c: None if c == first else (s, y ^ 2, z, c)),
        ]

    def by_core(x, same):
        return jnp.where((core == 0) == same, x[0], x[1])

    half = (n_head, sub, width)
    near, *near_peer = attend(info, kv, state, half, mine, other, n_y, n_seq)
    near_far = [swap_core(x) for x in near_peer]
    parts_n = project(info, near, near_far, w_out, w_other, n_y, cols // 4)
    got_n = stage_one(parts_n, 1)
    far, *far_peer = attend(after(info, parts_n[0]), kv, [q_far], half, mine, other, n_y, n_seq)
    far_far = [swap_core(x) for x in far_peer]
    parts_f = project(info, far, far_far, w_out, w_other, n_y, cols // 4)
    got_f = stage_one(parts_f, 0)
    total_n = sum_one([after(p, parts_f[0]) for p in parts_n], got_n, 1)
    total_f = sum_one(parts_f, got_f, 0)
    got2_n = stage_two((total_n[0], total_n[1], after(total_n[2], total_f[0]), total_n[3]), 1)
    got2_f = stage_two(total_f, 0)
    done_f = add(total_f[0], *got2_f).reshape(2, sub, cols // 2)
    done_n = add(after(total_n[0], total_f[0]), *got2_n).reshape(2, sub, cols // 2)
    own_other = swap_core(after(by_core(done_n, False), done_f))
    home = over_all(by_core(done_f, True), lambda s, y, z, c: (n_seq - 1 - s, y, z, c))
    home_other = over_all(by_core(done_f, False), lambda s, y, z, c: (n_seq - 1 - s, y, z, 1 - c))
    here = jnp.concatenate([by_core(done_n, True), home], axis=0)
    there = jnp.concatenate([own_other, home_other], axis=0)
    left = jnp.where(core == 0, here, there)
    right = jnp.where(core == 0, there, here)
    return jnp.concatenate([left, right], axis=1)


def solution(mesh):
    placed = (P("seq", "head"), P("seq", None), P("seq", None), P("head", None))
    return jax.shard_map(
        local, mesh=mesh, in_specs=placed, out_specs=P(("seq", "head"), None), check_vma=False
    )
```

```python
import functools

import jax
import jax.numpy as jnp
from jax import lax
from jax.experimental import pallas as pl
from jax.experimental.pallas import tpu as pltpu
from jax.sharding import PartitionSpec as P

KV_HEADS = 8
DH = 128
LOG2E = 1.4426950408889634
NEG = -1e30
LIMIT = 60.0
BF = jnp.bfloat16
F32 = jnp.float32
PARAMS = pltpu.CompilerParams(vmem_limit_bytes=17 << 20)
FETCH = ((7, 3), (6, 2), (5, 1), (4, None))
SLOTS = [d for pair in FETCH for d in pair if d is not None]
TABLE = 6


def after(x, *deps):
    return lax.optimization_barrier((x, *deps))[0]


def prep_kernel(info, k_ref, v_ref, kv_ref):
    rows = k_ref.shape[0]
    kv_ref[0:rows, :] = k_ref[...]
    for t in range(rows // DH):
        kv_ref[rows + t * DH : rows + (t + 1) * DH, :] = v_ref[t * DH : (t + 1) * DH, :].T


def prep(info, keys, values):
    rows = keys.shape[0]
    col = pl.BlockSpec((rows, DH), lambda i, info: (0, info[1]))
    return pl.pallas_call(
        prep_kernel,
        grid_spec=pltpu.PrefetchScalarGridSpec(
            num_scalar_prefetch=1,
            grid=(1,),
            in_specs=[col, col],
            out_specs=pl.BlockSpec((2 * rows, DH), lambda i, info: (0, 0)),
        ),
        out_shape=jax.ShapeDtypeStruct((2 * rows, DH), BF),
        name="prep",
        compiler_params=pltpu.CompilerParams(vmem_limit_bytes=64 << 20),
    )(info, keys, values)


def keys_of(kv):
    k = kv[0 : kv.shape[0] // 2, :]
    return jnp.concatenate([k, k], axis=1)


def values_of(kv):
    rows = kv.shape[0] // 2
    tiles = [kv[rows + t * DH : rows + (t + 1) * DH, :] for t in range(rows // DH)]
    return jnp.concatenate([jnp.concatenate(tiles, axis=1), jnp.ones((16, rows), BF)], axis=0)


def load_queries(q, h, qt_ref):
    heads = KV_HEADS // 2
    scaled = q.astype(F32) * (DH**-0.5 * LOG2E)
    high = scaled.astype(BF)
    low = (scaled - high.astype(F32)).astype(BF)
    high, low = high.T, low.T
    for seg in range(q.shape[0] // DH):
        c = slice((seg * heads + h) * DH, (seg * heads + h + 1) * DH)
        rows = slice(seg * DH, (seg + 1) * DH)
        qt_ref[0:DH, c] = high[:, rows]
        qt_ref[DH : 2 * DH, c] = low[:, rows]


def diagonal_block(kv, second, groups, qt_ref, acc, m_ref):
    rows = kv.shape[0] // 2
    cols = qt_ref.shape[1]
    width = KV_HEADS // 2 * DH
    segs = cols // width
    quarter = rows // segs
    sub = segs * DH // groups
    kk, vt = keys_of(kv), values_of(kv)
    j = lax.broadcasted_iota(jnp.int32, (quarter, width), 1) % DH
    pos = j // sub * (rows // groups) + second * sub + j % sub
    allowed = lax.broadcasted_iota(jnp.int32, (quarter, width), 0) <= pos
    for seg in range(segs):
        c = slice(seg * width, (seg + 1) * width)
        n = (seg + 1) * quarter
        s = jnp.dot(kk[:n], qt_ref[:, c], preferred_element_type=F32)
        last = jnp.where(allowed, s[n - quarter :], NEG)
        s = last if seg == 0 else jnp.concatenate([s[: n - quarter], last], axis=0)
        m = jnp.max(s, axis=0, keepdims=True)
        acc[:, c] = jnp.dot(vt[:, :n], jnp.exp2(s - m).astype(BF), preferred_element_type=F32)
        m_ref[:, c] = jnp.broadcast_to(m, (8, width))


def own_kernel(groups, q_ref, away_ref, kv_ref, qt_ref, acc_ref, m_ref, send_ref):
    send_ref[...] = away_ref[:, 0]
    _, _, sub, width = q_ref.shape
    for h in range(width // DH):
        load_queries(q_ref[:, 0, :, h * DH : (h + 1) * DH].reshape(groups * sub, DH), h, qt_ref)
    diagonal_block(kv_ref, 0, groups, qt_ref, acc_ref, m_ref)


def own(q4, kv):
    groups, _, sub, width = q4.shape
    cols = groups * sub * width // DH
    return pl.pallas_call(
        functools.partial(own_kernel, groups),
        grid=(1,),
        in_specs=[
            pl.BlockSpec((groups, 1, sub, width), lambda i: (0, 0, 0, 0)),
            pl.BlockSpec((groups, 1, sub, width), lambda i: (0, 1, 0, 0)),
            pl.BlockSpec(kv.shape, lambda i: (0, 0)),
        ],
        out_specs=[
            pl.BlockSpec((2 * DH, cols), lambda i: (0, 0)),
            pl.BlockSpec((DH + 16, cols), lambda i: (0, 0)),
            pl.BlockSpec((8, cols), lambda i: (0, 0)),
            pl.BlockSpec((groups, sub, width), lambda i: (0, 0, 0)),
        ],
        out_shape=[
            jax.ShapeDtypeStruct((2 * DH, cols), BF),
            jax.ShapeDtypeStruct((DH + 16, cols), F32),
            jax.ShapeDtypeStruct((8, cols), F32),
            jax.ShapeDtypeStruct((groups, sub, width), BF),
        ],
        name="own",
        cost_estimate=pl.CostEstimate(
            flops=2 * cols * kv.shape[0] * 2 * DH, bytes_accessed=8 << 20, transcendentals=0
        ),
        compiler_params=PARAMS,
    )(q4, q4, kv)


def attend_kernel(foreign, groups, n_y, n_seq, info, own_ref, *refs):
    ops = n_seq // 2
    inputs = 1 if foreign else 3
    mine, other = refs[inputs : inputs + ops], refs[inputs + ops : inputs + 2 * ops]
    o_ref, first_ref, second_ref, q_buf, kv_buf, qt_ref, acc_ref, m_ref, mx_ref, peer_buf, count, sems = refs[
        inputs + 2 * ops :
    ]
    place, core, partner = info[0], info[2], info[5]
    rows = own_ref.shape[0] // 2
    cols = qt_ref.shape[1]
    heads = KV_HEADS // 2
    qb = cols // heads
    sub = qb // groups
    half = cols // 4
    limit = partner if foreign else place
    y_first = core == (0 if foreign else 1)
    n = len(SLOTS)
    if foreign:
        state = [pltpu.make_async_copy(refs[0], q_buf, sems.at[n + 1])]
    else:
        state = [
            pltpu.make_async_copy(refs[0], qt_ref, sems.at[n + 1]),
            pltpu.make_async_copy(refs[1], acc_ref.at[0], sems.at[n + 2]),
            pltpu.make_async_copy(refs[2], m_ref, sems.at[n + 3]),
        ]

    def behind(i):
        return limit - lax.bitwise_xor(place, info[TABLE + i])

    def start(src, slot):
        pltpu.make_async_copy(src, kv_buf.at[slot], sems.at[slot]).start()

    def wait(slot):
        pltpu.make_async_copy(own_ref, kv_buf.at[slot], sems.at[slot]).wait()

    for load in state:
        load.start()
    if foreign:

        @pl.when(place < limit)
        def _():
            start(own_ref, 0)

    for i in range(n):

        @pl.when(jnp.logical_and(behind(i) >= 0, core == i % 2))
        def _():
            start(mine[i // 2], i + 1)

        @pl.when(jnp.logical_and(behind(i) >= 0, core != i % 2))
        def _():
            start(other[i // 2], i + 1)

    for load in state:
        load.wait()
    count[0] = 0
    if foreign:
        for h in range(heads):
            load_queries(q_buf[:, :, h * DH : (h + 1) * DH].reshape(qb, DH), h, qt_ref)
        wait(1)
        diagonal_block(kv_buf.at[1], 1, groups, qt_ref, acc_ref.at[0], m_ref)

    def scores(kk, c0):
        return jnp.dot(kk, qt_ref[:, c0 : c0 + half], preferred_element_type=F32)

    def add_block(slot, _):
        i = jnp.maximum(slot - 1, 0)

        @pl.when(jnp.where(slot == 0, limit - place, behind(i)) > 0)
        def _():
            wait(slot)
            old = count[0] % 2
            new = 1 - old
            count[0] = count[0] + 1
            kk, vt = keys_of(kv_buf.at[slot]), values_of(kv_buf.at[slot])
            for c0 in range(0, cols, half):
                s = scores(kk, c0)
                mx_ref[:, c0 : c0 + half] = jnp.max(s.reshape(rows // 8, 8, half), axis=0)
                p = jnp.exp2(s - m_ref[0:1, c0 : c0 + half]).astype(BF)
                acc_ref[new, :, c0 : c0 + half] = acc_ref[old, :, c0 : c0 + half] + jnp.dot(
                    vt, p, preferred_element_type=F32
                )
            over = jnp.max(mx_ref[...] - m_ref[...])

            @pl.when(over > LIMIT)
            def _():
                for c0 in range(0, cols, half):
                    m = m_ref[0:1, c0 : c0 + half]
                    top = jnp.maximum(m, jnp.max(mx_ref[:, c0 : c0 + half], axis=0, keepdims=True))
                    p = jnp.exp2(scores(kk, c0) - top).astype(BF)
                    acc_ref[new, :, c0 : c0 + half] = acc_ref[old, :, c0 : c0 + half] * jnp.exp2(
                        m - top
                    ) + jnp.dot(vt, p, preferred_element_type=F32)
                    m_ref[:, c0 : c0 + half] = jnp.broadcast_to(top, (8, half))

        return 0

    lax.fori_loop(0, n + 1, add_block, 0)
    last = count[0] % 2
    per_seg = groups * DH // qb
    for seg in range(qb // DH):
        for h in range(heads):
            o = acc_ref[last, :, (seg * heads + h) * DH : (seg * heads + h + 1) * DH]
            o = (o[0:DH] * (1.0 / o[DH : DH + 1])).astype(BF).T
            for k in range(per_seg):
                g = seg * per_seg + k
                ry = (g // 4) ^ info[3]
                rz = (g // 2 % 2) ^ info[4]
                by_y = ((ry * 2 + rz) * 2 + g % 2) * sub
                by_z = (((ry // 2 * 2 + rz) * 2 + ry % 2) * 2 + g % 2) * sub
                piece = o[k * sub : (k + 1) * sub, :]
                here = pl.multiple_of(jnp.where(y_first, by_y, by_z), sub)
                there = pl.multiple_of(jnp.where(y_first, by_z, by_y), sub)
                o_ref[pl.ds(here, sub), h * DH : (h + 1) * DH] = piece
                peer_buf[pl.ds(there, sub), h * DH : (h + 1) * DH] = piece
    first_ref[...] = peer_buf[: qb // 2, :]
    second_ref[...] = peer_buf[qb // 2 :, :]


def attend(info, kv, state, q_shape, mine, other, n_y, n_seq):
    foreign = len(state) == 1
    groups, sub, width = q_shape
    qb = groups * sub
    cols = qb * width // DH
    any_space = pl.BlockSpec(memory_space=pl.ANY)
    out = pl.BlockSpec((qb, width), lambda i, info: (0, 0))
    part = pl.BlockSpec((qb // 2, width), lambda i, info: (0, 0))
    return pl.pallas_call(
        functools.partial(attend_kernel, foreign, groups, n_y, n_seq),
        grid_spec=pltpu.PrefetchScalarGridSpec(
            num_scalar_prefetch=1,
            grid=(1,),
            in_specs=[any_space] * (1 + len(state) + 2 * len(mine)),
            out_specs=[out, part, part],
            scratch_shapes=[
                pltpu.VMEM(q_shape, BF),
                pltpu.VMEM((len(SLOTS) + 1, *kv.shape), BF),
                pltpu.VMEM((2 * DH, cols), BF),
                pltpu.VMEM((2, DH + 16, cols), F32),
                pltpu.VMEM((8, cols), F32),
                pltpu.VMEM((8, cols), F32),
                pltpu.VMEM((qb, width), BF),
                pltpu.SMEM((1,), jnp.int32),
                pltpu.SemaphoreType.DMA((len(SLOTS) + 4,)),
            ],
        ),
        out_shape=[jax.ShapeDtypeStruct((rows, width), BF) for rows in (qb, qb // 2, qb // 2)],
        name="attend_foreign" if foreign else "attend_own",
        cost_estimate=pl.CostEstimate(
            flops=2 * cols * kv.shape[0] * 4 * DH, bytes_accessed=4 << 20, transcendentals=0
        ),
        compiler_params=PARAMS,
    )(info, kv, *state, *mine, *other)


def project(info, mine, other, w, w_other, parts, tile):
    rows, width = mine.shape
    n = w.shape[1] // 2
    steps = n // tile

    def body(info, a, b0, b1, wa, wb, *outs):
        b = jnp.concatenate([b0[...], b1[...]], axis=0)
        s = jnp.dot(a[...], wa[...], preferred_element_type=F32) + jnp.dot(
            b, wb[...], preferred_element_type=F32
        )
        part = s.shape[0] // parts
        for i, o in enumerate(outs):
            o[...] = s[i * part : (i + 1) * part].astype(BF)

    whole = pl.BlockSpec((rows, width), lambda i, info: (0, 0))
    half = pl.BlockSpec((rows // 2, width), lambda i, info: (0, 0))
    weights = pl.BlockSpec((width, tile), lambda i, info: (0, info[2] * steps + i))
    return pl.pallas_call(
        body,
        grid_spec=pltpu.PrefetchScalarGridSpec(
            num_scalar_prefetch=1,
            grid=(steps,),
            in_specs=[whole, half, half, weights, weights],
            out_specs=[pl.BlockSpec((rows // parts, tile), lambda i, info: (0, i))] * parts,
        ),
        out_shape=[jax.ShapeDtypeStruct((rows // parts, n), BF)] * parts,
        name="project",
        cost_estimate=pl.CostEstimate(flops=0, bytes_accessed=0, transcendentals=0),
        compiler_params=PARAMS,
    )(info, mine, *other, w, w_other)


def add(*terms):
    total = terms[0].astype(F32)
    for t in terms[1:]:
        total = total + t.astype(F32)
    return total.astype(BF)


def local(queries, keys, values, w_out):
    n_seq, n_head = lax.axis_size("seq"), lax.axis_size("head")
    rows, width = queries.shape
    cols = w_out.shape[1]
    place = lax.axis_index("seq")
    head = lax.axis_index("head")
    core, y, z = head % 2, head // 4, head // 2 % 2
    n_y = n_head // 4
    partner = n_seq - 1 - place
    info = jnp.stack([place, head * KV_HEADS // n_head, core, y, z, partner, *SLOTS]).astype(jnp.int32)

    def over_all(x, f):
        pairs = []
        for s in range(n_seq):
            for h in range(n_head):
                to = f(s, h // 4, h // 2 % 2, h % 2)
                if to is not None:
                    s2, y2, z2, c2 = to
                    pairs.append((s * n_head + h, s2 * n_head + (y2 % n_y) * 4 + z2 * 2 + c2))
        return lax.ppermute(x, ("seq", "head"), pairs)

    def swap_core(x):
        return over_all(x, lambda s, y, z, c: (s, y, z, 1 - c))

    def fetch(x, pair):
        def to(s, y, z, c):
            if pair[c] is None:
                return None
            t = s ^ pair[c]
            return (t, y, z, c) if s <= max(t, n_seq - 1 - t) else None

        return over_all(x, to)

    sub = rows // n_head // 2
    q4 = queries.reshape(n_head, 2, sub, width)
    w_other = swap_core(w_out)
    kv = prep(info, keys, values)
    mine = [fetch(kv, pair) for pair in FETCH]
    *state, q_away = own(q4, kv)
    other = [swap_core(after(x, state[2])) for x in mine]
    q_far = over_all(after(q_away, state[2], *mine), lambda s, y, z, c: (n_seq - 1 - s, y, z, c))

    def stage_one(parts, first):
        return [
            over_all(parts[1], lambda s, y, z, c: (s, y ^ 1, z, c) if c == first else (s, y, 1 - z, c)),
            over_all(parts[3], lambda s, y, z, c: (s, y ^ 3, z, c) if c == first else (s, y, 1 - z, c)),
            over_all(parts[2], lambda s, y, z, c: (s, y ^ 2, z, c) if c == first else None),
        ]

    def sum_one(parts, got, first):
        along_y = parts[0].astype(F32) + got[0].astype(F32)
        extra = got[1].astype(F32) + got[2].astype(F32)
        a = (along_y + jnp.where(core == first, extra, 0.0)).astype(BF)
        b = add(parts[2], got[1])
        n = a.shape[0] // 2
        return a[:n], a[n:], b[:n], b[n:]

    def stage_two(total, first):
        return [
            over_all(total[1], lambda s, y, z, c: (s, y, 1 - z, c) if c == first else (s, y ^ 1, z, c)),
            over_all(total[3], lambda s, y, z, c: None if c == first else (s, y ^ 3, z, c)),
            over_all(total[2], lambda s, y, z, c: None if c == first else (s, y ^ 2, z, c)),
        ]

    def by_core(x, same):
        return jnp.where((core == 0) == same, x[0], x[1])

    half = (n_head, sub, width)
    near, *near_peer = attend(info, kv, state, half, mine, other, n_y, n_seq)
    near_far = [swap_core(x) for x in near_peer]
    parts_n = project(info, near, near_far, w_out, w_other, n_y, cols // 4)
    got_n = stage_one(parts_n, 1)
    far, *far_peer = attend(after(info, parts_n[0]), kv, [q_far], half, mine, other, n_y, n_seq)
    far_far = [swap_core(x) for x in far_peer]
    parts_f = project(info, far, far_far, w_out, w_other, n_y, cols // 4)
    got_f = stage_one(parts_f, 0)
    total_n = sum_one([after(p, parts_f[0]) for p in parts_n], got_n, 1)
    total_f = sum_one(parts_f, got_f, 0)
    got2_n = stage_two((total_n[0], total_n[1], after(total_n[2], total_f[0]), total_n[3]), 1)
    got2_f = stage_two(total_f, 0)
    done_f = add(total_f[0], *got2_f).reshape(2, sub, cols // 2)
    done_n = add(after(total_n[0], total_f[0]), *got2_n).reshape(2, sub, cols // 2)
    own_other = swap_core(after(by_core(done_n, False), done_f))
    home = over_all(by_core(done_f, True), lambda s, y, z, c: (n_seq - 1 - s, y, z, c))
    home_other = over_all(by_core(done_f, False), lambda s, y, z, c: (n_seq - 1 - s, y, z, 1 - c))
    here = jnp.concatenate([by_core(done_n, True), home], axis=0)
    there = jnp.concatenate([own_other, home_other], axis=0)
    left = jnp.where(core == 0, here, there)
    right = jnp.where(core == 0, there, here)
    return jnp.concatenate([left, right], axis=1)


def solution(mesh):
    placed = (P("seq", "head"), P("seq", None), P("seq", None), P("head", None))
    return jax.shard_map(
        local, mesh=mesh, in_specs=placed, out_specs=P(("seq", "head"), None), check_vma=False
    )
```

```python
import functools

import jax
import jax.numpy as jnp
from jax import lax
from jax.experimental import pallas as pl
from jax.experimental.pallas import tpu as pltpu
from jax.sharding import PartitionSpec as P

KV_HEADS = 8
DH = 128
LOG2E = 1.4426950408889634
NEG = -1e30
LIMIT = 60.0
BF = jnp.bfloat16
F32 = jnp.float32
PARAMS = pltpu.CompilerParams(vmem_limit_bytes=17 << 20)
FETCH = ((7, 3), (6, 2), (5, 1), (4, None))
SLOTS = [d for pair in FETCH for d in pair if d is not None]
TABLE = 6


def after(x, *deps):
    return lax.optimization_barrier((x, *deps))[0]


def prep_kernel(info, k_ref, v_ref, kv_ref):
    rows = k_ref.shape[0]
    kv_ref[0:rows, :] = k_ref[...]
    for t in range(rows // DH):
        kv_ref[rows + t * DH : rows + (t + 1) * DH, :] = v_ref[t * DH : (t + 1) * DH, :].T


def prep(info, keys, values):
    rows = keys.shape[0]
    col = pl.BlockSpec((rows, DH), lambda i, info: (0, info[1]))
    return pl.pallas_call(
        prep_kernel,
        grid_spec=pltpu.PrefetchScalarGridSpec(
            num_scalar_prefetch=1,
            grid=(1,),
            in_specs=[col, col],
            out_specs=pl.BlockSpec((2 * rows, DH), lambda i, info: (0, 0)),
        ),
        out_shape=jax.ShapeDtypeStruct((2 * rows, DH), BF),
        name="prep",
        compiler_params=pltpu.CompilerParams(vmem_limit_bytes=64 << 20),
    )(info, keys, values)


def keys_of(kv):
    k = kv[0 : kv.shape[0] // 2, :]
    return jnp.concatenate([k, k], axis=1)


def values_of(kv):
    rows = kv.shape[0] // 2
    tiles = [kv[rows + t * DH : rows + (t + 1) * DH, :] for t in range(rows // DH)]
    return jnp.concatenate([jnp.concatenate(tiles, axis=1), jnp.ones((16, rows), BF)], axis=0)


def load_queries(q, h, qt_ref):
    heads = KV_HEADS // 2
    scaled = q.astype(F32) * (DH**-0.5 * LOG2E)
    high = scaled.astype(BF)
    low = (scaled - high.astype(F32)).astype(BF)
    high, low = high.T, low.T
    for seg in range(q.shape[0] // DH):
        c = slice((seg * heads + h) * DH, (seg * heads + h + 1) * DH)
        rows = slice(seg * DH, (seg + 1) * DH)
        qt_ref[0:DH, c] = high[:, rows]
        qt_ref[DH : 2 * DH, c] = low[:, rows]


def diagonal_block(kv, second, groups, qt_ref, acc, m_ref):
    rows = kv.shape[0] // 2
    cols = qt_ref.shape[1]
    width = KV_HEADS // 2 * DH
    segs = cols // width
    quarter = rows // segs
    sub = segs * DH // groups
    kk, vt = keys_of(kv), values_of(kv)
    j = lax.broadcasted_iota(jnp.int32, (quarter, width), 1) % DH
    pos = j // sub * (rows // groups) + second * sub + j % sub
    allowed = lax.broadcasted_iota(jnp.int32, (quarter, width), 0) <= pos
    for seg in range(segs):
        c = slice(seg * width, (seg + 1) * width)
        n = (seg + 1) * quarter
        s = jnp.dot(kk[:n], qt_ref[:, c], preferred_element_type=F32)
        last = jnp.where(allowed, s[n - quarter :], NEG)
        s = last if seg == 0 else jnp.concatenate([s[: n - quarter], last], axis=0)
        m = jnp.max(s, axis=0, keepdims=True)
        acc[:, c] = jnp.dot(vt[:, :n], jnp.exp2(s - m).astype(BF), preferred_element_type=F32)
        m_ref[:, c] = jnp.broadcast_to(m, (8, width))


def own_kernel(groups, q_ref, away_ref, kv_ref, qt_ref, acc_ref, m_ref, send_ref):
    send_ref[...] = away_ref[:, 0]
    _, _, sub, width = q_ref.shape
    for h in range(width // DH):
        load_queries(q_ref[:, 0, :, h * DH : (h + 1) * DH].reshape(groups * sub, DH), h, qt_ref)
    diagonal_block(kv_ref, 0, groups, qt_ref, acc_ref, m_ref)


def own(q4, kv):
    groups, _, sub, width = q4.shape
    cols = groups * sub * width // DH
    return pl.pallas_call(
        functools.partial(own_kernel, groups),
        grid=(1,),
        in_specs=[
            pl.BlockSpec((groups, 1, sub, width), lambda i: (0, 0, 0, 0)),
            pl.BlockSpec((groups, 1, sub, width), lambda i: (0, 1, 0, 0)),
            pl.BlockSpec(kv.shape, lambda i: (0, 0)),
        ],
        out_specs=[
            pl.BlockSpec((2 * DH, cols), lambda i: (0, 0)),
            pl.BlockSpec((DH + 16, cols), lambda i: (0, 0)),
            pl.BlockSpec((8, cols), lambda i: (0, 0)),
            pl.BlockSpec((groups, sub, width), lambda i: (0, 0, 0)),
        ],
        out_shape=[
            jax.ShapeDtypeStruct((2 * DH, cols), BF),
            jax.ShapeDtypeStruct((DH + 16, cols), F32),
            jax.ShapeDtypeStruct((8, cols), F32),
            jax.ShapeDtypeStruct((groups, sub, width), BF),
        ],
        name="own",
        cost_estimate=pl.CostEstimate(
            flops=2 * cols * kv.shape[0] * 2 * DH, bytes_accessed=8 << 20, transcendentals=0
        ),
        compiler_params=PARAMS,
    )(q4, q4, kv)


def attend_kernel(foreign, groups, n_y, n_seq, info, own_ref, *refs):
    ops = n_seq // 2
    inputs = 1 if foreign else 3
    mine, other = refs[inputs : inputs + ops], refs[inputs + ops : inputs + 2 * ops]
    o_ref, first_ref, second_ref, q_buf, kv_buf, qt_ref, acc_ref, m_ref, mx_ref, peer_buf, count, sems = refs[
        inputs + 2 * ops :
    ]
    place, core, partner = info[0], info[2], info[5]
    rows = own_ref.shape[0] // 2
    cols = qt_ref.shape[1]
    heads = KV_HEADS // 2
    qb = cols // heads
    sub = qb // groups
    half = cols // 4
    limit = partner if foreign else place
    y_first = core == 0
    n = len(SLOTS)
    if foreign:
        state = [pltpu.make_async_copy(refs[0], q_buf, sems.at[n + 1])]
    else:
        state = [
            pltpu.make_async_copy(refs[0], qt_ref, sems.at[n + 1]),
            pltpu.make_async_copy(refs[1], acc_ref.at[0], sems.at[n + 2]),
            pltpu.make_async_copy(refs[2], m_ref, sems.at[n + 3]),
        ]

    def behind(i):
        return limit - lax.bitwise_xor(place, info[TABLE + i])

    def start(src, slot):
        pltpu.make_async_copy(src, kv_buf.at[slot], sems.at[slot]).start()

    def wait(slot):
        pltpu.make_async_copy(own_ref, kv_buf.at[slot], sems.at[slot]).wait()

    for load in state:
        load.start()
    if foreign:

        @pl.when(place < limit)
        def _():
            start(own_ref, 0)

    for i in range(n):

        @pl.when(jnp.logical_and(behind(i) >= 0, core == i % 2))
        def _():
            start(mine[i // 2], i + 1)

        @pl.when(jnp.logical_and(behind(i) >= 0, core != i % 2))
        def _():
            start(other[i // 2], i + 1)

    for load in state:
        load.wait()
    count[0] = 0
    if foreign:
        for h in range(heads):
            load_queries(q_buf[:, :, h * DH : (h + 1) * DH].reshape(qb, DH), h, qt_ref)
        wait(1)
        diagonal_block(kv_buf.at[1], 1, groups, qt_ref, acc_ref.at[0], m_ref)

    def scores(kk, c0):
        return jnp.dot(kk, qt_ref[:, c0 : c0 + half], preferred_element_type=F32)

    def add_block(slot, _):
        i = jnp.maximum(slot - 1, 0)

        @pl.when(jnp.where(slot == 0, limit - place, behind(i)) > 0)
        def _():
            wait(slot)
            old = count[0] % 2
            new = 1 - old
            count[0] = count[0] + 1
            kk, vt = keys_of(kv_buf.at[slot]), values_of(kv_buf.at[slot])
            for c0 in range(0, cols, half):
                s = scores(kk, c0)
                mx_ref[:, c0 : c0 + half] = jnp.max(s.reshape(rows // 8, 8, half), axis=0)
                p = jnp.exp2(s - m_ref[0:1, c0 : c0 + half]).astype(BF)
                acc_ref[new, :, c0 : c0 + half] = acc_ref[old, :, c0 : c0 + half] + jnp.dot(
                    vt, p, preferred_element_type=F32
                )
            over = jnp.max(mx_ref[...] - m_ref[...])

            @pl.when(over > LIMIT)
            def _():
                for c0 in range(0, cols, half):
                    m = m_ref[0:1, c0 : c0 + half]
                    top = jnp.maximum(m, jnp.max(mx_ref[:, c0 : c0 + half], axis=0, keepdims=True))
                    p = jnp.exp2(scores(kk, c0) - top).astype(BF)
                    acc_ref[new, :, c0 : c0 + half] = acc_ref[old, :, c0 : c0 + half] * jnp.exp2(
                        m - top
                    ) + jnp.dot(vt, p, preferred_element_type=F32)
                    m_ref[:, c0 : c0 + half] = jnp.broadcast_to(top, (8, half))

        return 0

    lax.fori_loop(0, n + 1, add_block, 0)
    last = count[0] % 2
    per_seg = groups * DH // qb
    for seg in range(qb // DH):
        for h in range(heads):
            o = acc_ref[last, :, (seg * heads + h) * DH : (seg * heads + h + 1) * DH]
            o = (o[0:DH] * (1.0 / o[DH : DH + 1])).astype(BF).T
            for k in range(per_seg):
                g = seg * per_seg + k
                ry = (g // 4) ^ info[3]
                rz = (g // 2 % 2) ^ info[4]
                by_y = ((ry * 2 + rz) * 2 + g % 2) * sub
                by_z = (((ry // 2 * 2 + rz) * 2 + ry % 2) * 2 + g % 2) * sub
                piece = o[k * sub : (k + 1) * sub, :]
                here = pl.multiple_of(jnp.where(y_first, by_y, by_z), sub)
                there = pl.multiple_of(jnp.where(y_first, by_z, by_y), sub)
                o_ref[pl.ds(here, sub), h * DH : (h + 1) * DH] = piece
                peer_buf[pl.ds(there, sub), h * DH : (h + 1) * DH] = piece
    first_ref[...] = peer_buf[: qb // 2, :]
    second_ref[...] = peer_buf[qb // 2 :, :]


def attend(info, kv, state, q_shape, mine, other, n_y, n_seq):
    foreign = len(state) == 1
    groups, sub, width = q_shape
    qb = groups * sub
    cols = qb * width // DH
    any_space = pl.BlockSpec(memory_space=pl.ANY)
    out = pl.BlockSpec((qb, width), lambda i, info: (0, 0))
    part = pl.BlockSpec((qb // 2, width), lambda i, info: (0, 0))
    return pl.pallas_call(
        functools.partial(attend_kernel, foreign, groups, n_y, n_seq),
        grid_spec=pltpu.PrefetchScalarGridSpec(
            num_scalar_prefetch=1,
            grid=(1,),
            in_specs=[any_space] * (1 + len(state) + 2 * len(mine)),
            out_specs=[out, part, part],
            scratch_shapes=[
                pltpu.VMEM(q_shape, BF),
                pltpu.VMEM((len(SLOTS) + 1, *kv.shape), BF),
                pltpu.VMEM((2 * DH, cols), BF),
                pltpu.VMEM((2, DH + 16, cols), F32),
                pltpu.VMEM((8, cols), F32),
                pltpu.VMEM((8, cols), F32),
                pltpu.VMEM((qb, width), BF),
                pltpu.SMEM((1,), jnp.int32),
                pltpu.SemaphoreType.DMA((len(SLOTS) + 4,)),
            ],
        ),
        out_shape=[jax.ShapeDtypeStruct((rows, width), BF) for rows in (qb, qb // 2, qb // 2)],
        name="attend_foreign" if foreign else "attend_own",
        cost_estimate=pl.CostEstimate(
            flops=2 * cols * kv.shape[0] * 4 * DH, bytes_accessed=4 << 20, transcendentals=0
        ),
        compiler_params=PARAMS,
    )(info, kv, *state, *mine, *other)


def project(info, mine, other, w, w_other, parts, tile):
    rows, width = mine.shape
    n = w.shape[1] // 2
    steps = n // tile

    def body(info, a, b0, b1, w_hbm, wb, *refs):
        *outs, w_buf, sems = refs
        step = pl.program_id(0)

        def copy(i):
            first = pl.multiple_of((info[2] * steps + i) * tile, tile)
            return pltpu.make_async_copy(w_hbm.at[:, pl.ds(first, tile)], w_buf.at[i], sems.at[i])

        @pl.when(step == 0)
        def _():
            for i in range(steps):
                copy(i).start()

        b = jnp.concatenate([b0[...], b1[...]], axis=0)
        s = jnp.dot(b, wb[...], preferred_element_type=F32)
        copy(step).wait()
        s = s + jnp.dot(a[...], w_buf[step], preferred_element_type=F32)
        part = s.shape[0] // parts
        for i, o in enumerate(outs):
            o[...] = s[i * part : (i + 1) * part].astype(BF)

    whole = pl.BlockSpec((rows, width), lambda i, info: (0, 0))
    half = pl.BlockSpec((rows // 2, width), lambda i, info: (0, 0))
    weights = pl.BlockSpec((width, tile), lambda i, info: (0, info[2] * steps + i))
    return pl.pallas_call(
        body,
        grid_spec=pltpu.PrefetchScalarGridSpec(
            num_scalar_prefetch=1,
            grid=(steps,),
            in_specs=[whole, half, half, pl.BlockSpec(memory_space=pltpu.HBM), weights],
            out_specs=[pl.BlockSpec((rows // parts, tile), lambda i, info: (0, i))] * parts,
            scratch_shapes=[pltpu.VMEM((steps, width, tile), BF), pltpu.SemaphoreType.DMA((steps,))],
        ),
        out_shape=[jax.ShapeDtypeStruct((rows // parts, n), BF)] * parts,
        name="project",
        cost_estimate=pl.CostEstimate(flops=0, bytes_accessed=0, transcendentals=0),
        compiler_params=PARAMS,
    )(info, mine, *other, w, w_other)


def add(*terms):
    total = terms[0].astype(F32)
    for t in terms[1:]:
        total = total + t.astype(F32)
    return total.astype(BF)


def local(queries, keys, values, w_out):
    n_seq, n_head = lax.axis_size("seq"), lax.axis_size("head")
    rows, width = queries.shape
    cols = w_out.shape[1]
    place = lax.axis_index("seq")
    head = lax.axis_index("head")
    core, y, z = head % 2, head // 4, head // 2 % 2
    n_y = n_head // 4
    partner = n_seq - 1 - place
    info = jnp.stack([place, head * KV_HEADS // n_head, core, y, z, partner, *SLOTS]).astype(jnp.int32)

    def over_all(x, f):
        pairs = []
        for s in range(n_seq):
            for h in range(n_head):
                to = f(s, h // 4, h // 2 % 2, h % 2)
                if to is not None:
                    s2, y2, z2, c2 = to
                    pairs.append((s * n_head + h, s2 * n_head + (y2 % n_y) * 4 + z2 * 2 + c2))
        return lax.ppermute(x, ("seq", "head"), pairs)

    def swap_core(x):
        return over_all(x, lambda s, y, z, c: (s, y, z, 1 - c))

    def fetch(x, pair):
        def to(s, y, z, c):
            if pair[c] is None:
                return None
            t = s ^ pair[c]
            return (t, y, z, c) if s <= max(t, n_seq - 1 - t) else None

        return over_all(x, to)

    sub = rows // n_head // 2
    q4 = queries.reshape(n_head, 2, sub, width)
    w_other = swap_core(w_out)
    kv = prep(info, keys, values)
    mine = [fetch(kv, pair) for pair in FETCH]
    *state, q_away = own(q4, kv)
    other = [swap_core(after(x, state[2])) for x in mine]
    q_far = over_all(after(q_away, state[2], *mine), lambda s, y, z, c: (n_seq - 1 - s, y, z, c))

    def to_y_or_z(x, d):
        return over_all(x, lambda s, y, z, c: (s, y, 1 - z, c) if c else (s, y ^ d, z, c))

    def to_z_or_y(x):
        return over_all(x, lambda s, y, z, c: (s, y ^ 1, z, c) if c else (s, y, 1 - z, c))

    def to_y(x, *d):
        d = (*d, None)
        return over_all(x, lambda s, y, z, c: None if d[c] is None else (s, y ^ d[c], z, c))

    def stage_sum(parts, got):
        along_y = parts[0].astype(F32) + got[0].astype(F32)
        extra = got[1].astype(F32) + got[2].astype(F32)
        a = (along_y + jnp.where(core == 0, extra, 0.0)).astype(BF)
        b = add(parts[2], got[1])
        n = a.shape[0] // 2
        return a[:n], a[n:], b[:n], b[n:]

    def by_core(x, same):
        return jnp.where((core == 0) == same, x[0], x[1])

    half = (n_head, sub, width)
    near, *near_peer = attend(info, kv, state, half, mine, other, n_y, n_seq)
    near_far = [swap_core(x) for x in near_peer]
    parts_n = project(info, near, near_far, w_out, w_other, n_y, cols // 4)
    got_n = [to_y_or_z(parts_n[1], 1), to_y_or_z(parts_n[3], 3), to_y(parts_n[2], 2)]
    far, *far_peer = attend(after(info, parts_n[0]), kv, [q_far], half, mine, other, n_y, n_seq)
    far_far = [swap_core(x) for x in far_peer]
    parts_f = project(info, far, far_far, w_out, w_other, n_y, cols // 4)
    got_f = [to_y_or_z(parts_f[1], 1), to_y_or_z(parts_f[3], 3)]
    total_n = stage_sum([after(p, parts_f[0]) for p in parts_n], got_n)
    n = total_n[0].shape[0]
    mixed_a = to_y(jnp.where(core == 0, parts_f[2][:n], total_n[2]), 2, 2)
    mixed_b = to_y(jnp.where(core == 0, parts_f[2][n:], total_n[3]), 2, 3)
    got_one = to_z_or_y(total_n[1])
    total_f = stage_sum(parts_f, [*got_f, jnp.concatenate([mixed_a, mixed_b], axis=0)])
    got2_f = [to_z_or_y(total_f[1]), to_y(total_f[3], None, 3), to_y(total_f[2], None, 2)]
    rest = jnp.where(core == 0, 0.0, mixed_a.astype(F32) + mixed_b.astype(F32))
    done_n = (total_n[0].astype(F32) + got_one.astype(F32) + rest).astype(BF).reshape(2, sub, cols // 2)
    done_f = add(total_f[0], *got2_f).reshape(2, sub, cols // 2)
    own_other = swap_core(by_core(done_n, False))
    home = over_all(by_core(done_f, True), lambda s, y, z, c: (n_seq - 1 - s, y, z, c))
    home_other = over_all(by_core(done_f, False), lambda s, y, z, c: (n_seq - 1 - s, y, z, 1 - c))
    here = jnp.concatenate([by_core(done_n, True), home], axis=0)
    there = jnp.concatenate([own_other, home_other], axis=0)
    left = jnp.where(core == 0, here, there)
    right = jnp.where(core == 0, there, here)
    return jnp.concatenate([left, right], axis=1)


def solution(mesh):
    placed = (P("seq", "head"), P("seq", None), P("seq", None), P("head", None))
    return jax.shard_map(
        local, mesh=mesh, in_specs=placed, out_specs=P(("seq", "head"), None), check_vma=False
    )
```

```python
import functools

import jax
import jax.numpy as jnp
from jax import lax
from jax.experimental import pallas as pl
from jax.experimental.pallas import tpu as pltpu
from jax.sharding import PartitionSpec as P

KV_HEADS = 8
DH = 128
LOG2E = 1.4426950408889634
NEG = -1e30
LIMIT = 60.0
BF = jnp.bfloat16
F32 = jnp.float32
PARAMS = pltpu.CompilerParams(vmem_limit_bytes=17 << 20)
FETCH = ((7, 3), (6, 2), (5, 1), (4, None))
SLOTS = [d for pair in FETCH for d in pair if d is not None]
TABLE = 6


def after(x, *deps):
    return lax.optimization_barrier((x, *deps))[0]


def prep_kernel(info, k_ref, v_ref, kv_ref):
    kv_ref[0] = k_ref[...]
    for t in range(v_ref.shape[0] // DH):
        kv_ref[1, t * DH : (t + 1) * DH, :] = v_ref[t * DH : (t + 1) * DH, :].T


def prep(info, keys, values, steps=4):
    rows = keys.shape[0]
    part = rows // steps
    col = pl.BlockSpec((part, DH), lambda i, info: (i, info[1]))
    return pl.pallas_call(
        prep_kernel,
        grid_spec=pltpu.PrefetchScalarGridSpec(
            num_scalar_prefetch=1,
            grid=(steps,),
            in_specs=[col, col],
            out_specs=pl.BlockSpec((2, part, DH), lambda i, info: (0, i, 0)),
        ),
        out_shape=jax.ShapeDtypeStruct((2, rows, DH), BF),
        name="prep",
        compiler_params=pltpu.CompilerParams(vmem_limit_bytes=64 << 20),
    )(info, keys, values).reshape(2 * rows, DH)


def keys_of(kv):
    k = kv[0 : kv.shape[0] // 2, :]
    return jnp.concatenate([k, k], axis=1)


def values_of(kv):
    rows = kv.shape[0] // 2
    tiles = [kv[rows + t * DH : rows + (t + 1) * DH, :] for t in range(rows // DH)]
    return jnp.concatenate([jnp.concatenate(tiles, axis=1), jnp.ones((16, rows), BF)], axis=0)


def load_queries(q, h, qt_ref):
    heads = KV_HEADS // 2
    scaled = q.astype(F32) * (DH**-0.5 * LOG2E)
    high = scaled.astype(BF)
    low = (scaled - high.astype(F32)).astype(BF)
    high, low = high.T, low.T
    for seg in range(q.shape[0] // DH):
        c = slice((seg * heads + h) * DH, (seg * heads + h + 1) * DH)
        rows = slice(seg * DH, (seg + 1) * DH)
        qt_ref[0:DH, c] = high[:, rows]
        qt_ref[DH : 2 * DH, c] = low[:, rows]


def diagonal_block(kv, second, groups, qt_ref, acc, m_ref):
    rows = kv.shape[0] // 2
    cols = qt_ref.shape[1]
    width = KV_HEADS // 2 * DH
    segs = cols // width
    quarter = rows // segs
    sub = segs * DH // groups
    kk, vt = keys_of(kv), values_of(kv)
    j = lax.broadcasted_iota(jnp.int32, (quarter, width), 1) % DH
    pos = j // sub * (rows // groups) + second * sub + j % sub
    allowed = lax.broadcasted_iota(jnp.int32, (quarter, width), 0) <= pos
    for seg in range(segs):
        c = slice(seg * width, (seg + 1) * width)
        n = (seg + 1) * quarter
        s = jnp.dot(kk[:n], qt_ref[:, c], preferred_element_type=F32)
        last = jnp.where(allowed, s[n - quarter :], NEG)
        s = last if seg == 0 else jnp.concatenate([s[: n - quarter], last], axis=0)
        m = jnp.max(s, axis=0, keepdims=True)
        acc[:, c] = jnp.dot(vt[:, :n], jnp.exp2(s - m).astype(BF), preferred_element_type=F32)
        m_ref[:, c] = jnp.broadcast_to(m, (8, width))


def own_kernel(groups, q_ref, away_ref, kv_ref, qt_ref, acc_ref, m_ref, send_ref):
    send_ref[...] = away_ref[:, 0]
    _, _, sub, width = q_ref.shape
    for h in range(width // DH):
        load_queries(q_ref[:, 0, :, h * DH : (h + 1) * DH].reshape(groups * sub, DH), h, qt_ref)
    diagonal_block(kv_ref, 0, groups, qt_ref, acc_ref, m_ref)


def own(q4, kv):
    groups, _, sub, width = q4.shape
    cols = groups * sub * width // DH
    return pl.pallas_call(
        functools.partial(own_kernel, groups),
        grid=(1,),
        in_specs=[
            pl.BlockSpec((groups, 1, sub, width), lambda i: (0, 0, 0, 0)),
            pl.BlockSpec((groups, 1, sub, width), lambda i: (0, 1, 0, 0)),
            pl.BlockSpec(kv.shape, lambda i: (0, 0)),
        ],
        out_specs=[
            pl.BlockSpec((2 * DH, cols), lambda i: (0, 0)),
            pl.BlockSpec((DH + 16, cols), lambda i: (0, 0)),
            pl.BlockSpec((8, cols), lambda i: (0, 0)),
            pl.BlockSpec((groups, sub, width), lambda i: (0, 0, 0)),
        ],
        out_shape=[
            jax.ShapeDtypeStruct((2 * DH, cols), BF),
            jax.ShapeDtypeStruct((DH + 16, cols), F32),
            jax.ShapeDtypeStruct((8, cols), F32),
            jax.ShapeDtypeStruct((groups, sub, width), BF),
        ],
        name="own",
        cost_estimate=pl.CostEstimate(
            flops=2 * cols * kv.shape[0] * 2 * DH, bytes_accessed=8 << 20, transcendentals=0
        ),
        compiler_params=PARAMS,
    )(q4, q4, kv)


def attend_kernel(foreign, groups, n_y, n_seq, info, own_ref, *refs):
    ops = n_seq // 2
    inputs = 2 if foreign else 3
    mine, other = refs[inputs : inputs + ops], refs[inputs + ops : inputs + 2 * ops]
    o_ref, first_ref, second_ref, q_buf, kv_buf, qt_ref, acc_ref, m_ref, mx_ref, peer_buf, count, sems = refs[
        inputs + 2 * ops :
    ]
    place, core, partner = info[0], info[2], info[5]
    rows = own_ref.shape[0] // 2
    cols = qt_ref.shape[1]
    heads = KV_HEADS // 2
    qb = cols // heads
    sub = qb // groups
    half = cols // 4
    limit = partner if foreign else place
    y_first = core == (0 if foreign else 1)
    n = len(SLOTS)
    if foreign:
        state = [pltpu.make_async_copy(refs[0], q_buf, sems.at[n + 1])]
    else:
        state = [
            pltpu.make_async_copy(refs[0], qt_ref, sems.at[n + 1]),
            pltpu.make_async_copy(refs[1], acc_ref.at[0], sems.at[n + 2]),
            pltpu.make_async_copy(refs[2], m_ref, sems.at[n + 3]),
        ]

    def behind(i):
        return limit - lax.bitwise_xor(place, info[TABLE + i])

    def start(src, slot):
        pltpu.make_async_copy(src, kv_buf.at[slot], sems.at[slot]).start()

    def wait(slot):
        pltpu.make_async_copy(own_ref, kv_buf.at[slot], sems.at[slot]).wait()

    for load in state:
        load.start()
    if foreign:

        @pl.when(place < limit)
        def _():
            start(own_ref, 0)

    for i in range(n):

        @pl.when(jnp.logical_and(behind(i) >= 0, core == i % 2))
        def _():
            start(mine[i // 2], i + 1)

        @pl.when(jnp.logical_and(behind(i) >= 0, core != i % 2))
        def _():
            start(other[i // 2], i + 1)

    for load in state:
        load.wait()
    count[0] = 0
    if foreign:
        for h in range(heads):
            load_queries(q_buf[:, :, h * DH : (h + 1) * DH].reshape(qb, DH), h, qt_ref)
        wait(1)
        diagonal_block(kv_buf.at[1], 1, groups, qt_ref, acc_ref.at[0], m_ref)

    def scores(kk, c0):
        return jnp.dot(kk, qt_ref[:, c0 : c0 + half], preferred_element_type=F32)

    def add_block(slot, _):
        i = jnp.maximum(slot - 1, 0)

        @pl.when(jnp.where(slot == 0, limit - place, behind(i)) > 0)
        def _():
            wait(slot)
            old = count[0] % 2
            new = 1 - old
            count[0] = count[0] + 1
            kk, vt = keys_of(kv_buf.at[slot]), values_of(kv_buf.at[slot])
            for c0 in range(0, cols, half):
                s = scores(kk, c0)
                mx_ref[:, c0 : c0 + half] = jnp.max(s.reshape(rows // 8, 8, half), axis=0)
                p = jnp.exp2(s - m_ref[0:1, c0 : c0 + half]).astype(BF)
                acc_ref[new, :, c0 : c0 + half] = acc_ref[old, :, c0 : c0 + half] + jnp.dot(
                    vt, p, preferred_element_type=F32
                )
            over = jnp.max(mx_ref[...] - m_ref[...])

            @pl.when(over > LIMIT)
            def _():
                for c0 in range(0, cols, half):
                    m = m_ref[0:1, c0 : c0 + half]
                    top = jnp.maximum(m, jnp.max(mx_ref[:, c0 : c0 + half], axis=0, keepdims=True))
                    p = jnp.exp2(scores(kk, c0) - top).astype(BF)
                    acc_ref[new, :, c0 : c0 + half] = acc_ref[old, :, c0 : c0 + half] * jnp.exp2(
                        m - top
                    ) + jnp.dot(vt, p, preferred_element_type=F32)
                    m_ref[:, c0 : c0 + half] = jnp.broadcast_to(top, (8, half))

        return 0

    lax.fori_loop(0, n + 1, add_block, 0)
    last = count[0] % 2
    per_seg = groups * DH // qb
    for seg in range(qb // DH):
        for h in range(heads):
            o = acc_ref[last, :, (seg * heads + h) * DH : (seg * heads + h + 1) * DH]
            o = (o[0:DH] * (1.0 / o[DH : DH + 1])).astype(BF).T
            for k in range(per_seg):
                g = seg * per_seg + k
                ry = (g // 4) ^ info[3]
                rz = (g // 2 % 2) ^ info[4]
                by_y = ((ry * 2 + rz) * 2 + g % 2) * sub
                by_z = (((ry // 2 * 2 + rz) * 2 + ry % 2) * 2 + g % 2) * sub
                piece = o[k * sub : (k + 1) * sub, :]
                here = pl.multiple_of(jnp.where(y_first, by_y, by_z), sub)
                there = pl.multiple_of(jnp.where(y_first, by_z, by_y), sub)
                o_ref[pl.ds(here, sub), h * DH : (h + 1) * DH] = piece
                peer_buf[pl.ds(there, sub), h * DH : (h + 1) * DH] = piece
    first_ref[...] = peer_buf[: qb // 2, :]
    second_ref[...] = peer_buf[qb // 2 :, :]


def attend(info, kv, state, q_shape, mine, other, n_y, n_seq):
    foreign = len(state) == 2
    groups, sub, width = q_shape
    qb = groups * sub
    cols = qb * width // DH
    any_space = pl.BlockSpec(memory_space=pl.ANY)
    out = pl.BlockSpec((qb, width), lambda i, info: (0, 0))
    part = pl.BlockSpec((qb // 2, width), lambda i, info: (0, 0))
    return pl.pallas_call(
        functools.partial(attend_kernel, foreign, groups, n_y, n_seq),
        grid_spec=pltpu.PrefetchScalarGridSpec(
            num_scalar_prefetch=1,
            grid=(1,),
            in_specs=[any_space] * (1 + len(state) + 2 * len(mine)),
            out_specs=[out, part, part],
            scratch_shapes=[
                pltpu.VMEM(q_shape, BF),
                pltpu.VMEM((len(SLOTS) + 1, *kv.shape), BF),
                pltpu.VMEM((2 * DH, cols), BF),
                pltpu.VMEM((2, DH + 16, cols), F32),
                pltpu.VMEM((8, cols), F32),
                pltpu.VMEM((8, cols), F32),
                pltpu.VMEM((qb, width), BF),
                pltpu.SMEM((1,), jnp.int32),
                pltpu.SemaphoreType.DMA((len(SLOTS) + 4,)),
            ],
        ),
        out_shape=[jax.ShapeDtypeStruct((rows, width), BF) for rows in (qb, qb // 2, qb // 2)],
        name="attend_foreign" if foreign else "attend_own",
        cost_estimate=pl.CostEstimate(
            flops=2 * cols * kv.shape[0] * 4 * DH, bytes_accessed=4 << 20, transcendentals=0
        ),
        compiler_params=PARAMS,
    )(info, kv, *state, *mine, *other)


def project(info, mine, other, w, w_other, parts, tile):
    rows, width = mine.shape
    n = w.shape[1] // 2
    steps = n // tile

    def body(info, a, b0, b1, wa, wb, *outs):
        b = jnp.concatenate([b0[...], b1[...]], axis=0)
        s = jnp.dot(a[...], wa[...], preferred_element_type=F32) + jnp.dot(
            b, wb[...], preferred_element_type=F32
        )
        part = s.shape[0] // parts
        for i, o in enumerate(outs):
            o[...] = s[i * part : (i + 1) * part].astype(BF)

    whole = pl.BlockSpec((rows, width), lambda i, info: (0, 0))
    half = pl.BlockSpec((rows // 2, width), lambda i, info: (0, 0))
    weights = pl.BlockSpec((width, tile), lambda i, info: (0, info[2] * steps + i))
    return pl.pallas_call(
        body,
        grid_spec=pltpu.PrefetchScalarGridSpec(
            num_scalar_prefetch=1,
            grid=(steps,),
            in_specs=[whole, half, half, weights, weights],
            out_specs=[pl.BlockSpec((rows // parts, tile), lambda i, info: (0, i))] * parts,
        ),
        out_shape=[jax.ShapeDtypeStruct((rows // parts, n), BF)] * parts,
        name="project",
        cost_estimate=pl.CostEstimate(flops=0, bytes_accessed=0, transcendentals=0),
        compiler_params=PARAMS,
    )(info, mine, *other, w, w_other)


def add(*terms):
    total = terms[0].astype(F32)
    for t in terms[1:]:
        total = total + t.astype(F32)
    return total.astype(BF)


def local(queries, keys, values, w_out):
    n_seq, n_head = lax.axis_size("seq"), lax.axis_size("head")
    rows, width = queries.shape
    cols = w_out.shape[1]
    place = lax.axis_index("seq")
    head = lax.axis_index("head")
    core, y, z = head % 2, head // 4, head // 2 % 2
    n_y = n_head // 4
    partner = n_seq - 1 - place
    info = jnp.stack([place, head * KV_HEADS // n_head, core, y, z, partner, *SLOTS]).astype(jnp.int32)

    def over_all(x, f):
        pairs = []
        for s in range(n_seq):
            for h in range(n_head):
                to = f(s, h // 4, h // 2 % 2, h % 2)
                if to is not None:
                    s2, y2, z2, c2 = to
                    pairs.append((s * n_head + h, s2 * n_head + (y2 % n_y) * 4 + z2 * 2 + c2))
        return lax.ppermute(x, ("seq", "head"), pairs)

    def swap_core(x):
        return over_all(x, lambda s, y, z, c: (s, y, z, 1 - c))

    def fetch(x, pair):
        def to(s, y, z, c):
            if pair[c] is None:
                return None
            t = s ^ pair[c]
            return (t, y, z, c) if s <= max(t, n_seq - 1 - t) else None

        return over_all(x, to)

    sub = rows // n_head // 2
    q4 = queries.reshape(n_head, 2, sub, width)
    w_other = swap_core(w_out)
    kv = prep(info, keys, values)
    mine = [fetch(kv, pair) for pair in FETCH]
    *state, q_away = own(q4, kv)
    other = [swap_core(after(x, state[2])) for x in mine]
    q_far = over_all(after(q_away, state[2], *mine), lambda s, y, z, c: (n_seq - 1 - s, y, z, c))

    def stage_one(parts, first):
        return [
            over_all(parts[1], lambda s, y, z, c: (s, y ^ 1, z, c) if c == first else (s, y, 1 - z, c)),
            over_all(parts[3], lambda s, y, z, c: (s, y ^ 3, z, c) if c == first else (s, y, 1 - z, c)),
            over_all(parts[2], lambda s, y, z, c: (s, y ^ 2, z, c) if c == first else None),
        ]

    def sum_one(parts, got, first):
        along_y = parts[0].astype(F32) + got[0].astype(F32)
        extra = got[1].astype(F32) + got[2].astype(F32)
        a = (along_y + jnp.where(core == first, extra, 0.0)).astype(BF)
        b = add(parts[2], got[1])
        n = a.shape[0] // 2
        return a[:n], a[n:], b[:n], b[n:]

    def stage_two(total, first):
        return [
            over_all(total[1], lambda s, y, z, c: (s, y, 1 - z, c) if c == first else (s, y ^ 1, z, c)),
            over_all(total[3], lambda s, y, z, c: None if c == first else (s, y ^ 3, z, c)),
            over_all(total[2], lambda s, y, z, c: None if c == first else (s, y ^ 2, z, c)),
        ]

    def by_core(x, same):
        return jnp.where((core == 0) == same, x[0], x[1])

    half = (n_head, sub, width)
    near, *near_peer = attend(info, kv, state, half, mine, other, n_y, n_seq)
    near_far = [swap_core(x) for x in near_peer]
    parts_n = project(info, near, near_far, w_out, w_other, n_y, cols // 4)
    got_n = stage_one(parts_n, 1)
    far, *far_peer = attend(after(info, parts_n[0]), kv, [q_far, w_out], half, mine, other, n_y, n_seq)
    far_far = [swap_core(x) for x in far_peer]
    parts_f = project(info, far, far_far, w_out, w_other, n_y, cols // 4)
    got_f = stage_one(parts_f, 0)
    total_n = sum_one([after(p, parts_f[0]) for p in parts_n], got_n, 1)
    total_f = sum_one(parts_f, got_f, 0)
    got2_n = stage_two((total_n[0], total_n[1], after(total_n[2], total_f[0]), total_n[3]), 1)
    got2_f = stage_two(total_f, 0)
    done_f = add(total_f[0], *got2_f).reshape(2, sub, cols // 2)
    done_n = add(after(total_n[0], total_f[0]), *got2_n).reshape(2, sub, cols // 2)
    own_other = swap_core(after(by_core(done_n, False), done_f))
    home = over_all(by_core(done_f, True), lambda s, y, z, c: (n_seq - 1 - s, y, z, c))
    home_other = over_all(by_core(done_f, False), lambda s, y, z, c: (n_seq - 1 - s, y, z, 1 - c))
    here = jnp.concatenate([by_core(done_n, True), home], axis=0)
    there = jnp.concatenate([own_other, home_other], axis=0)
    left = jnp.where(core == 0, here, there)
    right = jnp.where(core == 0, there, here)
    return jnp.concatenate([left, right], axis=1)


def solution(mesh):
    placed = (P("seq", "head"), P("seq", None), P("seq", None), P("head", None))
    return jax.shard_map(
        local, mesh=mesh, in_specs=placed, out_specs=P(("seq", "head"), None), check_vma=False
    )
```

```python
import functools

import jax
import jax.numpy as jnp
from jax import lax
from jax.experimental import pallas as pl
from jax.experimental.pallas import tpu as pltpu
from jax.sharding import PartitionSpec as P

KV_HEADS = 8
DH = 128
LOG2E = 1.4426950408889634
NEG = -1e30
LIMIT = 60.0
BF = jnp.bfloat16
F32 = jnp.float32
PARAMS = pltpu.CompilerParams(vmem_limit_bytes=17 << 20)
FETCH = ((7, 3), (6, 2), (5, 1), (4, None))
SLOTS = [d for pair in FETCH for d in pair if d is not None]
TABLE = 6


def after(x, *deps):
    return lax.optimization_barrier((x, *deps))[0]


def prep_kernel(info, k_ref, v_ref, kv_ref):
    rows = k_ref.shape[0]
    kv_ref[0:rows, :] = k_ref[...]
    for t in range(rows // DH):
        kv_ref[rows + t * DH : rows + (t + 1) * DH, :] = v_ref[t * DH : (t + 1) * DH, :].T


def prep(info, keys, values):
    rows = keys.shape[0]
    col = pl.BlockSpec((rows, DH), lambda i, info: (0, info[1]))
    return pl.pallas_call(
        prep_kernel,
        grid_spec=pltpu.PrefetchScalarGridSpec(
            num_scalar_prefetch=1,
            grid=(1,),
            in_specs=[col, col],
            out_specs=pl.BlockSpec((2 * rows, DH), lambda i, info: (0, 0)),
        ),
        out_shape=jax.ShapeDtypeStruct((2 * rows, DH), BF),
        name="prep",
        compiler_params=pltpu.CompilerParams(vmem_limit_bytes=64 << 20),
    )(info, keys, values)


def keys_of(kv):
    k = kv[0 : kv.shape[0] // 2, :]
    return jnp.concatenate([k, k], axis=1)


def values_of(kv):
    rows = kv.shape[0] // 2
    tiles = [kv[rows + t * DH : rows + (t + 1) * DH, :] for t in range(rows // DH)]
    return jnp.concatenate([jnp.concatenate(tiles, axis=1), jnp.ones((16, rows), BF)], axis=0)


def load_queries(q, h, qt_ref):
    heads = KV_HEADS // 2
    scaled = q.astype(F32) * (DH**-0.5 * LOG2E)
    high = scaled.astype(BF)
    low = (scaled - high.astype(F32)).astype(BF)
    high, low = high.T, low.T
    for seg in range(q.shape[0] // DH):
        c = slice((seg * heads + h) * DH, (seg * heads + h + 1) * DH)
        rows = slice(seg * DH, (seg + 1) * DH)
        qt_ref[0:DH, c] = high[:, rows]
        qt_ref[DH : 2 * DH, c] = low[:, rows]


def diagonal_block(kv, second, groups, qt_ref, acc, m_ref):
    rows = kv.shape[0] // 2
    cols = qt_ref.shape[1]
    width = KV_HEADS // 2 * DH
    segs = cols // width
    quarter = rows // segs
    sub = segs * DH // groups
    kk, vt = keys_of(kv), values_of(kv)
    j = lax.broadcasted_iota(jnp.int32, (quarter, width), 1) % DH
    pos = j // sub * (rows // groups) + second * sub + j % sub
    allowed = lax.broadcasted_iota(jnp.int32, (quarter, width), 0) <= pos
    for seg in range(segs):
        c = slice(seg * width, (seg + 1) * width)
        n = (seg + 1) * quarter
        s = jnp.dot(kk[:n], qt_ref[:, c], preferred_element_type=F32)
        last = jnp.where(allowed, s[n - quarter :], NEG)
        s = last if seg == 0 else jnp.concatenate([s[: n - quarter], last], axis=0)
        m = jnp.max(s, axis=0, keepdims=True)
        acc[:, c] = jnp.dot(vt[:, :n], jnp.exp2(s - m).astype(BF), preferred_element_type=F32)
        m_ref[:, c] = jnp.broadcast_to(m, (8, width))


def own_kernel(groups, q_ref, away_ref, kv_ref, qt_ref, acc_ref, m_ref, send_ref):
    send_ref[...] = away_ref[:, 0]
    _, _, sub, width = q_ref.shape
    for h in range(width // DH):
        load_queries(q_ref[:, 0, :, h * DH : (h + 1) * DH].reshape(groups * sub, DH), h, qt_ref)
    diagonal_block(kv_ref, 0, groups, qt_ref, acc_ref, m_ref)


def own(q4, kv):
    groups, _, sub, width = q4.shape
    cols = groups * sub * width // DH
    return pl.pallas_call(
        functools.partial(own_kernel, groups),
        grid=(1,),
        in_specs=[
            pl.BlockSpec((groups, 1, sub, width), lambda i: (0, 0, 0, 0)),
            pl.BlockSpec((groups, 1, sub, width), lambda i: (0, 1, 0, 0)),
            pl.BlockSpec(kv.shape, lambda i: (0, 0)),
        ],
        out_specs=[
            pl.BlockSpec((2 * DH, cols), lambda i: (0, 0)),
            pl.BlockSpec((DH + 16, cols), lambda i: (0, 0)),
            pl.BlockSpec((8, cols), lambda i: (0, 0)),
            pl.BlockSpec((groups, sub, width), lambda i: (0, 0, 0)),
        ],
        out_shape=[
            jax.ShapeDtypeStruct((2 * DH, cols), BF),
            jax.ShapeDtypeStruct((DH + 16, cols), F32),
            jax.ShapeDtypeStruct((8, cols), F32),
            jax.ShapeDtypeStruct((groups, sub, width), BF),
        ],
        name="own",
        cost_estimate=pl.CostEstimate(
            flops=2 * cols * kv.shape[0] * 2 * DH, bytes_accessed=8 << 20, transcendentals=0
        ),
        compiler_params=PARAMS,
    )(q4, q4, kv)


def attend_kernel(foreign, groups, n_y, n_seq, info, own_ref, *refs):
    ops = n_seq // 2
    inputs = 1 if foreign else 3
    mine, other = refs[inputs : inputs + ops], refs[inputs + ops : inputs + 2 * ops]
    o_ref, first_ref, second_ref, q_buf, kv_buf, qt_ref, acc_ref, m_ref, mx_ref, peer_buf, count, sems = refs[
        inputs + 2 * ops :
    ]
    place, core, partner = info[0], info[2], info[5]
    rows = own_ref.shape[0] // 2
    cols = qt_ref.shape[1]
    heads = KV_HEADS // 2
    qb = cols // heads
    sub = qb // groups
    half = cols // 4
    limit = partner if foreign else place
    y_first = core == (0 if foreign else 1)
    n = len(SLOTS)
    if foreign:
        state = [pltpu.make_async_copy(refs[0], q_buf, sems.at[n + 1])]
    else:
        state = [
            pltpu.make_async_copy(refs[0], qt_ref, sems.at[n + 1]),
            pltpu.make_async_copy(refs[1], acc_ref.at[0], sems.at[n + 2]),
            pltpu.make_async_copy(refs[2], m_ref, sems.at[n + 3]),
        ]

    def behind(i):
        return limit - lax.bitwise_xor(place, info[TABLE + i])

    def start(src, slot):
        pltpu.make_async_copy(src, kv_buf.at[slot], sems.at[slot]).start()

    def wait(slot):
        pltpu.make_async_copy(own_ref, kv_buf.at[slot], sems.at[slot]).wait()

    for load in state:
        load.start()
    if foreign:

        @pl.when(place < limit)
        def _():
            start(own_ref, 0)

    for i in range(n):

        @pl.when(jnp.logical_and(behind(i) >= 0, core == i % 2))
        def _():
            start(mine[i // 2], i + 1)

        @pl.when(jnp.logical_and(behind(i) >= 0, core != i % 2))
        def _():
            start(other[i // 2], i + 1)

    for load in state:
        load.wait()
    count[0] = 0
    if foreign:
        for h in range(heads):
            load_queries(q_buf[:, :, h * DH : (h + 1) * DH].reshape(qb, DH), h, qt_ref)
        wait(1)
        diagonal_block(kv_buf.at[1], 1, groups, qt_ref, acc_ref.at[0], m_ref)

    def scores(kk, c0):
        return jnp.dot(kk, qt_ref[:, c0 : c0 + half], preferred_element_type=F32)

    def add_block(slot, _):
        i = jnp.maximum(slot - 1, 0)

        @pl.when(jnp.where(slot == 0, limit - place, behind(i)) > 0)
        def _():
            wait(slot)
            old = count[0] % 2
            new = 1 - old
            count[0] = count[0] + 1
            kk, vt = keys_of(kv_buf.at[slot]), values_of(kv_buf.at[slot])
            for c0 in range(0, cols, half):
                s = scores(kk, c0)
                mx_ref[:, c0 : c0 + half] = jnp.max(s.reshape(rows // 8, 8, half), axis=0)
                p = jnp.exp2(s - m_ref[0:1, c0 : c0 + half]).astype(BF)
                acc_ref[new, :, c0 : c0 + half] = acc_ref[old, :, c0 : c0 + half] + jnp.dot(
                    vt, p, preferred_element_type=F32
                )
            over = jnp.max(mx_ref[...] - m_ref[...])

            @pl.when(over > LIMIT)
            def _():
                for c0 in range(0, cols, half):
                    m = m_ref[0:1, c0 : c0 + half]
                    top = jnp.maximum(m, jnp.max(mx_ref[:, c0 : c0 + half], axis=0, keepdims=True))
                    p = jnp.exp2(scores(kk, c0) - top).astype(BF)
                    acc_ref[new, :, c0 : c0 + half] = acc_ref[old, :, c0 : c0 + half] * jnp.exp2(
                        m - top
                    ) + jnp.dot(vt, p, preferred_element_type=F32)
                    m_ref[:, c0 : c0 + half] = jnp.broadcast_to(top, (8, half))

        return 0

    lax.fori_loop(0, n + 1, add_block, 0)
    last = count[0] % 2
    per_seg = groups * DH // qb
    for seg in range(qb // DH):
        for h in range(heads):
            o = acc_ref[last, :, (seg * heads + h) * DH : (seg * heads + h + 1) * DH]
            o = (o[0:DH] * (1.0 / o[DH : DH + 1])).astype(BF).T
            for k in range(per_seg):
                g = seg * per_seg + k
                ry = (g // 4) ^ info[3]
                rz = (g // 2 % 2) ^ info[4]
                by_y = ((ry * 2 + rz) * 2 + g % 2) * sub
                by_z = (((ry // 2 * 2 + rz) * 2 + ry % 2) * 2 + g % 2) * sub
                piece = o[k * sub : (k + 1) * sub, :]
                here = pl.multiple_of(jnp.where(y_first, by_y, by_z), sub)
                there = pl.multiple_of(jnp.where(y_first, by_z, by_y), sub)
                o_ref[pl.ds(here, sub), h * DH : (h + 1) * DH] = piece
                peer_buf[pl.ds(there, sub), h * DH : (h + 1) * DH] = piece
    first_ref[...] = peer_buf[: qb // 2, :]
    second_ref[...] = peer_buf[qb // 2 :, :]


def attend(info, kv, state, q_shape, mine, other, n_y, n_seq):
    foreign = len(state) == 1
    groups, sub, width = q_shape
    qb = groups * sub
    cols = qb * width // DH
    any_space = pl.BlockSpec(memory_space=pl.ANY)
    out = pl.BlockSpec((qb, width), lambda i, info: (0, 0))
    part = pl.BlockSpec((qb // 2, width), lambda i, info: (0, 0))
    return pl.pallas_call(
        functools.partial(attend_kernel, foreign, groups, n_y, n_seq),
        grid_spec=pltpu.PrefetchScalarGridSpec(
            num_scalar_prefetch=1,
            grid=(1,),
            in_specs=[any_space] * (1 + len(state) + 2 * len(mine)),
            out_specs=[out, part, part],
            scratch_shapes=[
                pltpu.VMEM(q_shape, BF),
                pltpu.VMEM((len(SLOTS) + 1, *kv.shape), BF),
                pltpu.VMEM((2 * DH, cols), BF),
                pltpu.VMEM((2, DH + 16, cols), F32),
                pltpu.VMEM((8, cols), F32),
                pltpu.VMEM((8, cols), F32),
                pltpu.VMEM((qb, width), BF),
                pltpu.SMEM((1,), jnp.int32),
                pltpu.SemaphoreType.DMA((len(SLOTS) + 4,)),
            ],
        ),
        out_shape=[jax.ShapeDtypeStruct((rows, width), BF) for rows in (qb, qb // 2, qb // 2)],
        name="attend_foreign" if foreign else "attend_own",
        cost_estimate=pl.CostEstimate(
            flops=2 * cols * kv.shape[0] * 4 * DH, bytes_accessed=4 << 20, transcendentals=0
        ),
        compiler_params=PARAMS,
    )(info, kv, *state, *mine, *other)


def project(info, mine, other, w, w_other, parts, tile, params=PARAMS):
    rows, width = mine.shape
    n = w.shape[1] // 2
    steps = n // tile

    def body(info, a, b0, b1, wa, wb, *outs):
        b = jnp.concatenate([b0[...], b1[...]], axis=0)
        s = jnp.dot(a[...], wa[...], preferred_element_type=F32) + jnp.dot(
            b, wb[...], preferred_element_type=F32
        )
        part = s.shape[0] // parts
        for i, o in enumerate(outs):
            o[...] = s[i * part : (i + 1) * part].astype(BF)

    whole = pl.BlockSpec((rows, width), lambda i, info: (0, 0))
    half = pl.BlockSpec((rows // 2, width), lambda i, info: (0, 0))
    weights = pl.BlockSpec((width, tile), lambda i, info: (0, info[2] * steps + i))
    return pl.pallas_call(
        body,
        grid_spec=pltpu.PrefetchScalarGridSpec(
            num_scalar_prefetch=1,
            grid=(steps,),
            in_specs=[whole, half, half, weights, weights],
            out_specs=[pl.BlockSpec((rows // parts, tile), lambda i, info: (0, i))] * parts,
        ),
        out_shape=[jax.ShapeDtypeStruct((rows // parts, n), BF)] * parts,
        name="project",
        cost_estimate=pl.CostEstimate(flops=0, bytes_accessed=0, transcendentals=0),
        compiler_params=params,
    )(info, mine, *other, w, w_other)


def add(*terms):
    total = terms[0].astype(F32)
    for t in terms[1:]:
        total = total + t.astype(F32)
    return total.astype(BF)


def local(queries, keys, values, w_out):
    n_seq, n_head = lax.axis_size("seq"), lax.axis_size("head")
    rows, width = queries.shape
    cols = w_out.shape[1]
    place = lax.axis_index("seq")
    head = lax.axis_index("head")
    core, y, z = head % 2, head // 4, head // 2 % 2
    n_y = n_head // 4
    partner = n_seq - 1 - place
    info = jnp.stack([place, head * KV_HEADS // n_head, core, y, z, partner, *SLOTS]).astype(jnp.int32)

    def over_all(x, f):
        pairs = []
        for s in range(n_seq):
            for h in range(n_head):
                to = f(s, h // 4, h // 2 % 2, h % 2)
                if to is not None:
                    s2, y2, z2, c2 = to
                    pairs.append((s * n_head + h, s2 * n_head + (y2 % n_y) * 4 + z2 * 2 + c2))
        return lax.ppermute(x, ("seq", "head"), pairs)

    def swap_core(x):
        return over_all(x, lambda s, y, z, c: (s, y, z, 1 - c))

    def fetch(x, pair):
        def to(s, y, z, c):
            if pair[c] is None:
                return None
            t = s ^ pair[c]
            return (t, y, z, c) if s <= max(t, n_seq - 1 - t) else None

        return over_all(x, to)

    sub = rows // n_head // 2
    q4 = queries.reshape(n_head, 2, sub, width)
    w_other = swap_core(w_out)
    kv = prep(info, keys, values)
    mine = [fetch(kv, pair) for pair in FETCH]
    *state, q_away = own(q4, kv)
    other = [swap_core(after(x, state[2])) for x in mine]
    q_far = over_all(after(q_away, state[2], *mine), lambda s, y, z, c: (n_seq - 1 - s, y, z, c))

    def stage_one(parts, first):
        return [
            over_all(parts[1], lambda s, y, z, c: (s, y ^ 1, z, c) if c == first else (s, y, 1 - z, c)),
            over_all(parts[3], lambda s, y, z, c: (s, y ^ 3, z, c) if c == first else (s, y, 1 - z, c)),
            over_all(parts[2], lambda s, y, z, c: (s, y ^ 2, z, c) if c == first else None),
        ]

    def sum_one(parts, got, first):
        along_y = parts[0].astype(F32) + got[0].astype(F32)
        extra = got[1].astype(F32) + got[2].astype(F32)
        a = (along_y + jnp.where(core == first, extra, 0.0)).astype(BF)
        b = add(parts[2], got[1])
        n = a.shape[0] // 2
        return a[:n], a[n:], b[:n], b[n:]

    def stage_two(total, first):
        return [
            over_all(total[1], lambda s, y, z, c: (s, y, 1 - z, c) if c == first else (s, y ^ 1, z, c)),
            over_all(total[3], lambda s, y, z, c: None if c == first else (s, y ^ 3, z, c)),
            over_all(total[2], lambda s, y, z, c: None if c == first else (s, y ^ 2, z, c)),
        ]

    def by_core(x, same):
        return jnp.where((core == 0) == same, x[0], x[1])

    half = (n_head, sub, width)
    near, *near_peer = attend(info, kv, state, half, mine, other, n_y, n_seq)
    near_far = [swap_core(x) for x in near_peer]
    parts_n = project(info, near, near_far, w_out, w_other, n_y, cols // 4)
    got_n = stage_one(parts_n, 1)
    far, *far_peer = attend(after(info, parts_n[0]), kv, [q_far], half, mine, other, n_y, n_seq)
    far_far = [swap_core(x) for x in far_peer]
    wide = pltpu.CompilerParams(vmem_limit_bytes=50 << 20)
    parts_f = project(info, far, far_far, w_out, w_other, n_y, cols // 4, wide)
    got_f = stage_one(parts_f, 0)
    total_n = sum_one([after(p, parts_f[0]) for p in parts_n], got_n, 1)
    total_f = sum_one(parts_f, got_f, 0)
    got2_n = stage_two((total_n[0], total_n[1], after(total_n[2], total_f[0]), total_n[3]), 1)
    got2_f = stage_two(total_f, 0)
    done_f = add(total_f[0], *got2_f).reshape(2, sub, cols // 2)
    done_n = add(after(total_n[0], total_f[0]), *got2_n).reshape(2, sub, cols // 2)
    own_other = swap_core(after(by_core(done_n, False), done_f))
    home = over_all(by_core(done_f, True), lambda s, y, z, c: (n_seq - 1 - s, y, z, c))
    home_other = over_all(by_core(done_f, False), lambda s, y, z, c: (n_seq - 1 - s, y, z, 1 - c))
    here = jnp.concatenate([by_core(done_n, True), home], axis=0)
    there = jnp.concatenate([own_other, home_other], axis=0)
    left = jnp.where(core == 0, here, there)
    right = jnp.where(core == 0, there, here)
    return jnp.concatenate([left, right], axis=1)


def solution(mesh):
    placed = (P("seq", "head"), P("seq", None), P("seq", None), P("head", None))
    return jax.shard_map(
        local, mesh=mesh, in_specs=placed, out_specs=P(("seq", "head"), None), check_vma=False
    )
```

```python
import functools

import jax
import jax.numpy as jnp
from jax import lax
from jax.experimental import pallas as pl
from jax.experimental.pallas import tpu as pltpu
from jax.sharding import PartitionSpec as P

KV_HEADS = 8
DH = 128
LOG2E = 1.4426950408889634
NEG = -1e30
LIMIT = 60.0
BF = jnp.bfloat16
F32 = jnp.float32
PARAMS = pltpu.CompilerParams(vmem_limit_bytes=17 << 20)
FETCH = ((7, 3), (6, 2), (5, 1), (4, None))
SLOTS = [d for pair in FETCH for d in pair if d is not None]
TABLE = 6


def after(x, *deps):
    return lax.optimization_barrier((x, *deps))[0]


def prep_kernel(info, k_ref, v_ref, kv_ref):
    rows = k_ref.shape[0]
    kv_ref[0:rows, :] = k_ref[...]
    for t in range(rows // DH):
        kv_ref[rows + t * DH : rows + (t + 1) * DH, :] = v_ref[t * DH : (t + 1) * DH, :].T


def prep(info, keys, values):
    rows = keys.shape[0]
    col = pl.BlockSpec((rows, DH), lambda i, info: (0, info[1]))
    return pl.pallas_call(
        prep_kernel,
        grid_spec=pltpu.PrefetchScalarGridSpec(
            num_scalar_prefetch=1,
            grid=(1,),
            in_specs=[col, col],
            out_specs=pl.BlockSpec((2 * rows, DH), lambda i, info: (0, 0)),
        ),
        out_shape=jax.ShapeDtypeStruct((2 * rows, DH), BF),
        name="prep",
        compiler_params=pltpu.CompilerParams(vmem_limit_bytes=64 << 20),
    )(info, keys, values)


def keys_of(kv):
    k = kv[0 : kv.shape[0] // 2, :]
    return jnp.concatenate([k, k], axis=1)


def values_of(kv):
    rows = kv.shape[0] // 2
    tiles = [kv[rows + t * DH : rows + (t + 1) * DH, :] for t in range(rows // DH)]
    return jnp.concatenate([jnp.concatenate(tiles, axis=1), jnp.ones((16, rows), BF)], axis=0)


def load_queries(q, h, qt_ref):
    heads = KV_HEADS // 2
    scaled = q.astype(F32) * (DH**-0.5 * LOG2E)
    high = scaled.astype(BF)
    low = (scaled - high.astype(F32)).astype(BF)
    high, low = high.T, low.T
    for seg in range(q.shape[0] // DH):
        c = slice((seg * heads + h) * DH, (seg * heads + h + 1) * DH)
        rows = slice(seg * DH, (seg + 1) * DH)
        qt_ref[0:DH, c] = high[:, rows]
        qt_ref[DH : 2 * DH, c] = low[:, rows]


def diagonal_block(kv, second, groups, qt_ref, acc, m_ref):
    rows = kv.shape[0] // 2
    cols = qt_ref.shape[1]
    width = KV_HEADS // 2 * DH
    segs = cols // width
    quarter = rows // segs
    sub = segs * DH // groups
    kk, vt = keys_of(kv), values_of(kv)
    j = lax.broadcasted_iota(jnp.int32, (quarter, width), 1) % DH
    pos = j // sub * (rows // groups) + second * sub + j % sub
    allowed = lax.broadcasted_iota(jnp.int32, (quarter, width), 0) <= pos
    for seg in range(segs):
        c = slice(seg * width, (seg + 1) * width)
        n = (seg + 1) * quarter
        s = jnp.dot(kk[:n], qt_ref[:, c], preferred_element_type=F32)
        last = jnp.where(allowed, s[n - quarter :], NEG)
        s = last if seg == 0 else jnp.concatenate([s[: n - quarter], last], axis=0)
        m = jnp.max(s, axis=0, keepdims=True)
        acc[:, c] = jnp.dot(vt[:, :n], jnp.exp2(s - m).astype(BF), preferred_element_type=F32)
        m_ref[:, c] = jnp.broadcast_to(m, (8, width))


def own_kernel(groups, q_ref, away_ref, kv_ref, qt_ref, acc_ref, m_ref, send_ref):
    send_ref[...] = away_ref[:, 0]
    _, _, sub, width = q_ref.shape
    for h in range(width // DH):
        load_queries(q_ref[:, 0, :, h * DH : (h + 1) * DH].reshape(groups * sub, DH), h, qt_ref)
    diagonal_block(kv_ref, 0, groups, qt_ref, acc_ref, m_ref)


def own(q4, kv):
    groups, _, sub, width = q4.shape
    cols = groups * sub * width // DH
    return pl.pallas_call(
        functools.partial(own_kernel, groups),
        grid=(1,),
        in_specs=[
            pl.BlockSpec((groups, 1, sub, width), lambda i: (0, 0, 0, 0)),
            pl.BlockSpec((groups, 1, sub, width), lambda i: (0, 1, 0, 0)),
            pl.BlockSpec(kv.shape, lambda i: (0, 0)),
        ],
        out_specs=[
            pl.BlockSpec((2 * DH, cols), lambda i: (0, 0)),
            pl.BlockSpec((DH + 16, cols), lambda i: (0, 0)),
            pl.BlockSpec((8, cols), lambda i: (0, 0)),
            pl.BlockSpec((groups, sub, width), lambda i: (0, 0, 0)),
        ],
        out_shape=[
            jax.ShapeDtypeStruct((2 * DH, cols), BF),
            jax.ShapeDtypeStruct((DH + 16, cols), F32),
            jax.ShapeDtypeStruct((8, cols), F32),
            jax.ShapeDtypeStruct((groups, sub, width), BF),
        ],
        name="own",
        cost_estimate=pl.CostEstimate(
            flops=2 * cols * kv.shape[0] * 2 * DH, bytes_accessed=8 << 20, transcendentals=0
        ),
        compiler_params=PARAMS,
    )(q4, q4, kv)


def attend_kernel(foreign, groups, n_y, n_seq, info, own_ref, *refs):
    ops = n_seq // 2
    inputs = 1 if foreign else 3
    mine, other = refs[inputs : inputs + ops], refs[inputs + ops : inputs + 2 * ops]
    o_ref, *peer_refs, q_buf, kv_buf, qt_ref, acc_ref, m_ref, mx_ref, peer_buf, count, sems = refs[inputs + 2 * ops :]
    place, core, partner = info[0], info[2], info[5]
    rows = own_ref.shape[0] // 2
    cols = qt_ref.shape[1]
    heads = KV_HEADS // 2
    qb = cols // heads
    sub = qb // groups
    half = cols // 4
    limit = partner if foreign else place
    y_first = core == (0 if foreign else 1)
    n = len(SLOTS)
    if foreign:
        state = [pltpu.make_async_copy(refs[0], q_buf, sems.at[n + 1])]
    else:
        state = [
            pltpu.make_async_copy(refs[0], qt_ref, sems.at[n + 1]),
            pltpu.make_async_copy(refs[1], acc_ref.at[0], sems.at[n + 2]),
            pltpu.make_async_copy(refs[2], m_ref, sems.at[n + 3]),
        ]

    def behind(i):
        return limit - lax.bitwise_xor(place, info[TABLE + i])

    def start(src, slot):
        pltpu.make_async_copy(src, kv_buf.at[slot], sems.at[slot]).start()

    def wait(slot):
        pltpu.make_async_copy(own_ref, kv_buf.at[slot], sems.at[slot]).wait()

    for load in state:
        load.start()
    if foreign:

        @pl.when(place < limit)
        def _():
            start(own_ref, 0)

    for i in range(n):

        @pl.when(jnp.logical_and(behind(i) >= 0, core == i % 2))
        def _():
            start(mine[i // 2], i + 1)

        @pl.when(jnp.logical_and(behind(i) >= 0, core != i % 2))
        def _():
            start(other[i // 2], i + 1)

    for load in state:
        load.wait()
    count[0] = 0
    if foreign:
        for h in range(heads):
            load_queries(q_buf[:, :, h * DH : (h + 1) * DH].reshape(qb, DH), h, qt_ref)
        wait(1)
        diagonal_block(kv_buf.at[1], 1, groups, qt_ref, acc_ref.at[0], m_ref)

    def scores(kk, c0):
        return jnp.dot(kk, qt_ref[:, c0 : c0 + half], preferred_element_type=F32)

    def add_block(slot, _):
        i = jnp.maximum(slot - 1, 0)

        @pl.when(jnp.where(slot == 0, limit - place, behind(i)) > 0)
        def _():
            wait(slot)
            old = count[0] % 2
            new = 1 - old
            count[0] = count[0] + 1
            kk, vt = keys_of(kv_buf.at[slot]), values_of(kv_buf.at[slot])
            for c0 in range(0, cols, half):
                s = scores(kk, c0)
                mx_ref[:, c0 : c0 + half] = jnp.max(s.reshape(rows // 8, 8, half), axis=0)
                p = jnp.exp2(s - m_ref[0:1, c0 : c0 + half]).astype(BF)
                acc_ref[new, :, c0 : c0 + half] = acc_ref[old, :, c0 : c0 + half] + jnp.dot(
                    vt, p, preferred_element_type=F32
                )
            over = jnp.max(mx_ref[...] - m_ref[...])

            @pl.when(over > LIMIT)
            def _():
                for c0 in range(0, cols, half):
                    m = m_ref[0:1, c0 : c0 + half]
                    top = jnp.maximum(m, jnp.max(mx_ref[:, c0 : c0 + half], axis=0, keepdims=True))
                    p = jnp.exp2(scores(kk, c0) - top).astype(BF)
                    acc_ref[new, :, c0 : c0 + half] = acc_ref[old, :, c0 : c0 + half] * jnp.exp2(
                        m - top
                    ) + jnp.dot(vt, p, preferred_element_type=F32)
                    m_ref[:, c0 : c0 + half] = jnp.broadcast_to(top, (8, half))

        return 0

    lax.fori_loop(0, n + 1, add_block, 0)
    last = count[0] % 2
    per_seg = groups * DH // qb
    for seg in range(qb // DH):
        for h in range(heads):
            o = acc_ref[last, :, (seg * heads + h) * DH : (seg * heads + h + 1) * DH]
            o = (o[0:DH] * (1.0 / o[DH : DH + 1])).astype(BF).T
            for k in range(per_seg):
                g = seg * per_seg + k
                ry = (g // 4) ^ info[3]
                rz = (g // 2 % 2) ^ info[4]
                by_y = ((ry * 2 + rz) * 2 + g % 2) * sub
                by_z = (((ry // 2 * 2 + rz) * 2 + ry % 2) * 2 + g % 2) * sub
                piece = o[k * sub : (k + 1) * sub, :]
                here = pl.multiple_of(jnp.where(y_first, by_y, by_z), sub)
                there = pl.multiple_of(jnp.where(y_first, by_z, by_y), sub)
                o_ref[pl.ds(here, sub), h * DH : (h + 1) * DH] = piece
                peer_buf[pl.ds(there, sub), h * DH : (h + 1) * DH] = piece
    for i, ref in enumerate(peer_refs):
        ref[...] = peer_buf[i * ref.shape[0] : (i + 1) * ref.shape[0], :]


def attend(info, kv, state, q_shape, mine, other, n_y, n_seq):
    foreign = len(state) == 1
    groups, sub, width = q_shape
    qb = groups * sub
    cols = qb * width // DH
    any_space = pl.BlockSpec(memory_space=pl.ANY)
    out = pl.BlockSpec((qb, width), lambda i, info: (0, 0))
    pieces = 1 if foreign else 2
    part = pl.BlockSpec((qb // pieces, width), lambda i, info: (0, 0))
    return pl.pallas_call(
        functools.partial(attend_kernel, foreign, groups, n_y, n_seq),
        grid_spec=pltpu.PrefetchScalarGridSpec(
            num_scalar_prefetch=1,
            grid=(1,),
            in_specs=[any_space] * (1 + len(state) + 2 * len(mine)),
            out_specs=[out] + [part] * pieces,
            scratch_shapes=[
                pltpu.VMEM(q_shape, BF),
                pltpu.VMEM((len(SLOTS) + 1, *kv.shape), BF),
                pltpu.VMEM((2 * DH, cols), BF),
                pltpu.VMEM((2, DH + 16, cols), F32),
                pltpu.VMEM((8, cols), F32),
                pltpu.VMEM((8, cols), F32),
                pltpu.VMEM((qb, width), BF),
                pltpu.SMEM((1,), jnp.int32),
                pltpu.SemaphoreType.DMA((len(SLOTS) + 4,)),
            ],
        ),
        out_shape=[jax.ShapeDtypeStruct((rows, width), BF) for rows in [qb] + [qb // pieces] * pieces],
        name="attend_foreign" if foreign else "attend_own",
        cost_estimate=pl.CostEstimate(
            flops=2 * cols * kv.shape[0] * 4 * DH, bytes_accessed=4 << 20, transcendentals=0
        ),
        compiler_params=PARAMS,
    )(info, kv, *state, *mine, *other)


def project(info, mine, other, w, w_other, parts, tile, params=PARAMS):
    rows, width = mine.shape
    n = w.shape[1] // 2
    steps = n // tile

    def body(info, a, *refs):
        pieces, (wa, wb), outs = refs[: len(other)], refs[len(other) : len(other) + 2], refs[len(other) + 2 :]
        b = jnp.concatenate([ref[...] for ref in pieces], axis=0)
        s = jnp.dot(a[...], wa[...], preferred_element_type=F32) + jnp.dot(
            b, wb[...], preferred_element_type=F32
        )
        part = s.shape[0] // parts
        for i, o in enumerate(outs):
            o[...] = s[i * part : (i + 1) * part].astype(BF)

    whole = pl.BlockSpec((rows, width), lambda i, info: (0, 0))
    piece = pl.BlockSpec((rows // len(other), width), lambda i, info: (0, 0))
    weights = pl.BlockSpec((width, tile), lambda i, info: (0, info[2] * steps + i))
    return pl.pallas_call(
        body,
        grid_spec=pltpu.PrefetchScalarGridSpec(
            num_scalar_prefetch=1,
            grid=(steps,),
            in_specs=[whole] + [piece] * len(other) + [weights, weights],
            out_specs=[pl.BlockSpec((rows // parts, tile), lambda i, info: (0, i))] * parts,
        ),
        out_shape=[jax.ShapeDtypeStruct((rows // parts, n), BF)] * parts,
        name="project",
        cost_estimate=pl.CostEstimate(flops=0, bytes_accessed=0, transcendentals=0),
        compiler_params=params,
    )(info, mine, *other, w, w_other)


def add(*terms):
    total = terms[0].astype(F32)
    for t in terms[1:]:
        total = total + t.astype(F32)
    return total.astype(BF)


def local(queries, keys, values, w_out):
    n_seq, n_head = lax.axis_size("seq"), lax.axis_size("head")
    rows, width = queries.shape
    cols = w_out.shape[1]
    place = lax.axis_index("seq")
    head = lax.axis_index("head")
    core, y, z = head % 2, head // 4, head // 2 % 2
    n_y = n_head // 4
    partner = n_seq - 1 - place
    info = jnp.stack([place, head * KV_HEADS // n_head, core, y, z, partner, *SLOTS]).astype(jnp.int32)

    def over_all(x, f):
        pairs = []
        for s in range(n_seq):
            for h in range(n_head):
                to = f(s, h // 4, h // 2 % 2, h % 2)
                if to is not None:
                    s2, y2, z2, c2 = to
                    pairs.append((s * n_head + h, s2 * n_head + (y2 % n_y) * 4 + z2 * 2 + c2))
        return lax.ppermute(x, ("seq", "head"), pairs)

    def swap_core(x):
        return over_all(x, lambda s, y, z, c: (s, y, z, 1 - c))

    def fetch(x, pair):
        def to(s, y, z, c):
            if pair[c] is None:
                return None
            t = s ^ pair[c]
            return (t, y, z, c) if s <= max(t, n_seq - 1 - t) else None

        return over_all(x, to)

    sub = rows // n_head // 2
    q4 = queries.reshape(n_head, 2, sub, width)
    w_other = swap_core(w_out)
    kv = prep(info, keys, values)
    mine = [fetch(kv, pair) for pair in FETCH]
    *state, q_away = own(q4, kv)
    other = [swap_core(after(x, state[2])) for x in mine]
    q_far = over_all(after(q_away, state[2], *mine), lambda s, y, z, c: (n_seq - 1 - s, y, z, c))

    def stage_one(parts, first):
        return [
            over_all(parts[1], lambda s, y, z, c: (s, y ^ 1, z, c) if c == first else (s, y, 1 - z, c)),
            over_all(parts[3], lambda s, y, z, c: (s, y ^ 3, z, c) if c == first else (s, y, 1 - z, c)),
            over_all(parts[2], lambda s, y, z, c: (s, y ^ 2, z, c) if c == first else None),
        ]

    def sum_one(parts, got, first):
        along_y = parts[0].astype(F32) + got[0].astype(F32)
        extra = got[1].astype(F32) + got[2].astype(F32)
        a = (along_y + jnp.where(core == first, extra, 0.0)).astype(BF)
        b = add(parts[2], got[1])
        n = a.shape[0] // 2
        return a[:n], a[n:], b[:n], b[n:]

    def stage_two(total, first):
        return [
            over_all(total[1], lambda s, y, z, c: (s, y, 1 - z, c) if c == first else (s, y ^ 1, z, c)),
            over_all(total[3], lambda s, y, z, c: None if c == first else (s, y ^ 3, z, c)),
            over_all(total[2], lambda s, y, z, c: None if c == first else (s, y ^ 2, z, c)),
        ]

    def by_core(x, same):
        return jnp.where((core == 0) == same, x[0], x[1])

    half = (n_head, sub, width)
    near, *near_peer = attend(info, kv, state, half, mine, other, n_y, n_seq)
    near_far = [swap_core(x) for x in near_peer]
    parts_n = project(info, near, near_far, w_out, w_other, n_y, cols // 4)
    got_n = stage_one(parts_n, 1)
    far, *far_peer = attend(after(info, parts_n[0]), kv, [q_far], half, mine, other, n_y, n_seq)
    far_far = [swap_core(x) for x in far_peer]
    wide = pltpu.CompilerParams(vmem_limit_bytes=50 << 20)
    parts_f = project(info, far, far_far, w_out, w_other, n_y, cols // 4, wide)
    got_f = stage_one(parts_f, 0)
    total_n = sum_one([after(p, parts_f[0]) for p in parts_n], got_n, 1)
    total_f = sum_one(parts_f, got_f, 0)
    got2_n = stage_two((total_n[0], total_n[1], after(total_n[2], total_f[0]), total_n[3]), 1)
    got2_f = stage_two(total_f, 0)
    done_f = add(total_f[0], *got2_f).reshape(2, sub, cols // 2)
    done_n = add(after(total_n[0], total_f[0]), *got2_n).reshape(2, sub, cols // 2)
    own_other = swap_core(after(by_core(done_n, False), done_f))
    home = over_all(by_core(done_f, True), lambda s, y, z, c: (n_seq - 1 - s, y, z, c))
    home_other = over_all(by_core(done_f, False), lambda s, y, z, c: (n_seq - 1 - s, y, z, 1 - c))
    here = jnp.concatenate([by_core(done_n, True), home], axis=0)
    there = jnp.concatenate([own_other, home_other], axis=0)
    left = jnp.where(core == 0, here, there)
    right = jnp.where(core == 0, there, here)
    return jnp.concatenate([left, right], axis=1)


def solution(mesh):
    placed = (P("seq", "head"), P("seq", None), P("seq", None), P("head", None))
    return jax.shard_map(
        local, mesh=mesh, in_specs=placed, out_specs=P(("seq", "head"), None), check_vma=False
    )
```
